32 devices in a mesh: group: 2 (over x), expert: 16 (over z, y, core).
Axes of the slice: x: 2, y: 2, z: 4, core: 2. Of those that a mesh axis runs over, the one named last changes fastest.
Arguments:
- tokens: bfloat16 [32, 256, 1280], P(('group', 'expert')), parts along dimension 0, may hold values from -6 to 6
- out_grad: bfloat16 [32, 256, 1280], P(('group', 'expert')), parts along dimension 0, may hold values from -6 to 6
- router: bfloat16 [1280, 8], replicated, may hold values from -8 to 8
- in_weight: bfloat16 [1280, 20480], P(None, 'expert'), may hold values from -0.15625 to 0.15625
- out_weight: bfloat16 [20480, 1280], P('expert'), may hold values from -0.125 to 0.125
Outputs:
- tokens_grad: bfloat16 [32, 256, 1280], P(('group', 'expert')), parts along dimension 0
- router_grad: float32 [2560, 8], P('group'), parts along dimension 0
The draws below stay inside these ranges and needn't reach their ends.
There are 2 independent parts, one for each index of `group`. The reference program is written for one: setup_inputs(seed, part) draws one part's arguments, and reference() takes and returns one part's arrays. A program takes and returns all parts, laid end to end along the dimension named above; an argument that names none is the same for every part. Nothing has to cross between parts.
All inputs are finite; a program needn't handle non-finite values.
Results may differ from the reference program's by a relative error of at most 0.011.
Values may be sent and summed in bfloat16 or wider, within the bound.
No kernel may reach another device: no remote copies, remote signals or barrier semaphores. Data moves between devices by JAX's collectives and lax.ppermute only.
A program may use at most 64 MiB of HBM per device.

```python
import math
import jax
import jax.numpy as jnp
from jax import lax

D = 1280
HID = 2560
P_SIZE = 256
EXPERTS = 8
IMAGES = 16


def draw_router(key, part):
    key = jax.random.fold_in(key, 11)
    base_key = jax.random.fold_in(key, 0)
    values = jax.random.normal(base_key, (D, EXPERTS), jnp.float32) * (3.0 / math.sqrt(D))
    return jnp.clip(values, -8.0, 8.0).astype(jnp.bfloat16)


def steps_of(stream_key, dims, cuts, least, largest):
    def one(axis_at, parts):
        draws = jax.random.uniform(jax.random.fold_in(jax.random.fold_in(stream_key, 6), axis_at), (parts,), jnp.float32, least / len(cuts), largest / len(cuts))
        return jnp.repeat(jnp.exp(draws), dims[axis_at] // parts).reshape((-1,) + (1,) * (len(dims) - axis_at - 1))

    factor_of = one(*cuts[0])
    for cut in cuts[1:]:
        factor_of = factor_of * one(*cut)
    return factor_of


def normal_values(own_key, extent, scale, bound, cuts=(), kind=jnp.bfloat16):
    values = jax.random.normal(own_key, extent, jnp.float32) * scale
    if len(cuts) > 0:
        values = steps_of(own_key, extent, cuts, -0.22, 0.18) * values
    return jnp.clip(values, min=-bound, max=bound).astype(kind)


def setup_inputs(seed: int = 0, part: int = 0) -> dict:
    key_list = jax.random.split(jax.random.key(seed), 6)
    part_splits = jax.random.split(jax.random.fold_in(key_list[5], part), 6)
    return {
        "tokens": normal_values(part_splits[0], (IMAGES, P_SIZE, D), 1.0, 6.0, ((0, 16),)),
        "out_grad": normal_values(part_splits[1], (IMAGES, P_SIZE, D), 1.0, 6.0, ((0, 16),)),
        "router": draw_router(jax.random.fold_in(key_list[5], 71), part),
        "in_weight": normal_values(key_list[3], (D, EXPERTS * HID), D ** -0.5, 0.15625, ((1, 16),)),
        "out_weight": normal_values(key_list[4], (EXPERTS * HID, D), HID ** -0.5, 0.125, ((0, 16),)),
    }


def gelu_pair(hidden):
    normal_cdf = 0.5 * (1.0 + jax.scipy.special.erf(hidden * (1.0 / math.sqrt(2.0))))
    normal_pdf = jnp.exp(-0.5 * hidden * hidden) * (1.0 / math.sqrt(2.0 * math.pi))
    return (hidden * normal_cdf, normal_cdf + hidden * normal_pdf)

def reference(tokens, out_grad, router, in_weight, out_weight):
    tokens_float = tokens.astype(jnp.float32)
    grads_float = out_grad.astype(jnp.float32)
    router_float = router.astype(jnp.float32)
    logits = jnp.einsum('bpd,ds->bps', tokens_float, router_float)
    dispatch = jax.nn.softmax(logits, axis=1)
    combine = jax.nn.softmax(logits, axis=2)
    dispatch_b = dispatch.astype(jnp.bfloat16)
    combine_b = combine.astype(jnp.bfloat16)
    slot_in = jnp.einsum('bps,bpd->sbd', dispatch_b.astype(jnp.float32), tokens_float).astype(jnp.bfloat16)
    slot_grad = jnp.einsum('bps,bpd->sbd', combine_b.astype(jnp.float32), grads_float).astype(jnp.bfloat16)
    first_blocks = in_weight.reshape(D, EXPERTS, HID).transpose(1, 0, 2)
    second_blocks = out_weight.reshape(EXPERTS, HID, D)

    def expert_step(operands):
        slot_rows, grad_rows, first_block, second_block = operands
        hidden = jnp.dot(slot_rows, first_block, preferred_element_type=jnp.float32)
        activation, gelu_slope = gelu_pair(hidden)
        result = jnp.dot(activation.astype(jnp.bfloat16), second_block, preferred_element_type=jnp.float32)
        act_grad = jnp.dot(grad_rows, second_block.T, preferred_element_type=jnp.float32)
        hidden_grad = (act_grad * gelu_slope).astype(jnp.bfloat16)
        back = jnp.dot(hidden_grad, first_block.T, preferred_element_type=jnp.float32)
        return (result.astype(jnp.bfloat16), back.astype(jnp.bfloat16))
    slot_out, slot_back = lax.map(expert_step, (slot_in, slot_grad, first_blocks, second_blocks))
    out_float = slot_out.astype(jnp.float32)
    back_float = slot_back.astype(jnp.float32)
    combine_grad = jnp.einsum('bpd,sbd->bps', grads_float, out_float)
    dispatch_grad = jnp.einsum('bpd,sbd->bps', tokens_float, back_float)
    logits_grad = combine * (combine_grad - lax.optimization_barrier(jnp.sum(combine * combine_grad, axis=2, keepdims=True)))
    logits_grad = logits_grad + dispatch * (dispatch_grad - lax.optimization_barrier(jnp.sum(dispatch * dispatch_grad, axis=1, keepdims=True)))
    logits_b = logits_grad.astype(jnp.bfloat16).astype(jnp.float32)
    tokens_grad = jnp.einsum('bps,sbd->bpd', dispatch_b.astype(jnp.float32), back_float)
    tokens_grad = tokens_grad + jnp.einsum('bps,ds->bpd', logits_b, router_float)
    router_grad = jnp.einsum('bpd,bps->ds', tokens_float, logits_b)
    return (tokens_grad.astype(jnp.bfloat16), router_grad)
```

```python
import math

import jax
import jax.numpy as jnp
from jax import lax
from jax.sharding import PartitionSpec as P


def gelu_pair(hidden):
    normal_cdf = 0.5 * (1.0 + jax.scipy.special.erf(hidden * (1.0 / math.sqrt(2.0))))
    normal_pdf = jnp.exp(-0.5 * hidden * hidden) * (1.0 / math.sqrt(2.0 * math.pi))
    return (hidden * normal_cdf, normal_cdf + hidden * normal_pdf)


def expert_rows(slot_rows, grad_rows, in_weight, out_weight):
    hidden = jnp.einsum("kd,dh->kh", slot_rows, in_weight, preferred_element_type=jnp.float32)
    activation, gelu_slope = gelu_pair(hidden)
    part_out = jnp.einsum(
        "kh,hd->kd",
        activation.astype(jnp.bfloat16),
        out_weight,
        preferred_element_type=jnp.float32,
    )
    act_grad = jnp.einsum("kd,hd->kh", grad_rows, out_weight, preferred_element_type=jnp.float32)
    hidden_grad = (act_grad * gelu_slope).astype(jnp.bfloat16)
    part_in = jnp.einsum("kh,dh->kd", hidden_grad, in_weight, preferred_element_type=jnp.float32)
    return (part_out, part_in)


def doubling_sum(value, axis, size):
    step = 1
    while step < size:
        pairs = [(i, i ^ step) for i in range(size)]
        value = value + lax.ppermute(value, axis, pairs)
        step *= 2
    return value


def make_per_device(size):
    def per_device(tokens, out_grad, router, in_weight, out_weight):
        _, patches, model_width = tokens.shape
        slot_count = router.shape[1]
        halves = size // slot_count
        tokens = tokens[0]
        out_grad = out_grad[0]
        logits = jnp.einsum("ds,pd->sp", router, tokens, preferred_element_type=jnp.float32)
        dispatch = jax.nn.softmax(logits, axis=1)
        combine = jax.nn.softmax(logits, axis=0)
        dispatch_b = dispatch.astype(jnp.bfloat16)
        combine_b = combine.astype(jnp.bfloat16)
        slot_in = jnp.einsum(
            "sp,pd->sd", dispatch_b, tokens, preferred_element_type=jnp.float32
        ).astype(jnp.bfloat16)
        slot_grad = jnp.einsum(
            "sp,pd->sd", combine_b, out_grad, preferred_element_type=jnp.float32
        ).astype(jnp.bfloat16)
        sent = jnp.repeat(jnp.concatenate([slot_in, slot_grad], axis=1), halves, axis=0)
        got = lax.all_to_all(sent, "expert", split_axis=0, concat_axis=0, tiled=True)
        part_out, part_in = expert_rows(
            got[:, :model_width], got[:, model_width:], in_weight, out_weight
        )
        parts = jnp.concatenate([part_out, part_in], axis=1).astype(jnp.bfloat16)
        back = lax.all_to_all(parts, "expert", split_axis=0, concat_axis=0, tiled=True)
        back = (
            back.reshape(slot_count, halves, 2 * model_width)
            .astype(jnp.float32)
            .sum(axis=1)
            .astype(jnp.bfloat16)
        )
        slot_out = back[:, :model_width]
        slot_back = back[:, model_width:]
        combine_grad = jnp.einsum("pd,sd->sp", out_grad, slot_out, preferred_element_type=jnp.float32)
        dispatch_grad = jnp.einsum("pd,sd->sp", tokens, slot_back, preferred_element_type=jnp.float32)
        logits_grad = combine * (combine_grad - jnp.sum(combine * combine_grad, axis=0, keepdims=True))
        logits_grad = logits_grad + dispatch * (
            dispatch_grad - jnp.sum(dispatch * dispatch_grad, axis=1, keepdims=True)
        )
        logits_b = logits_grad.astype(jnp.bfloat16)
        router_part = jnp.einsum("pd,sp->ds", tokens, logits_b, preferred_element_type=jnp.float32)
        router_grad = doubling_sum(router_part, "expert", size)
        tokens_grad = jnp.einsum(
            "sp,sd->pd", dispatch_b, slot_back, preferred_element_type=jnp.float32
        )
        tokens_grad = tokens_grad + jnp.einsum(
            "sp,ds->pd", logits_b, router, preferred_element_type=jnp.float32
        )
        return (tokens_grad.astype(jnp.bfloat16)[None], router_grad)

    return per_device


def solution(mesh):
    in_specs = (
        P(("group", "expert"), None, None),
        P(("group", "expert"), None, None),
        P(),
        P(None, "expert"),
        P("expert", None),
    )
    out_specs = (P(("group", "expert"), None, None), P("group", None))
    return jax.shard_map(
        make_per_device(mesh.shape["expert"]),
        mesh=mesh,
        in_specs=in_specs,
        out_specs=out_specs,
        check_vma=False,
    )
```

```python
import math

import jax
import jax.numpy as jnp
from jax import lax
from jax.sharding import PartitionSpec as P


def gelu_pair(hidden):
    normal_cdf = 0.5 * (1.0 + jax.scipy.special.erf(hidden * (1.0 / math.sqrt(2.0))))
    normal_pdf = jnp.exp(-0.5 * hidden * hidden) * (1.0 / math.sqrt(2.0 * math.pi))
    return (hidden * normal_cdf, normal_cdf + hidden * normal_pdf)


def expert_rows(slot_rows, grad_rows, in_weight, out_weight):
    hidden = jnp.einsum("kd,dh->kh", slot_rows, in_weight, preferred_element_type=jnp.float32)
    activation, gelu_slope = gelu_pair(hidden)
    part_out = jnp.einsum(
        "kh,hd->kd",
        activation.astype(jnp.bfloat16),
        out_weight,
        preferred_element_type=jnp.float32,
    )
    act_grad = jnp.einsum("kd,hd->kh", grad_rows, out_weight, preferred_element_type=jnp.float32)
    hidden_grad = (act_grad * gelu_slope).astype(jnp.bfloat16)
    part_in = jnp.einsum("kh,dh->kd", hidden_grad, in_weight, preferred_element_type=jnp.float32)
    return (part_out, part_in)


def by_offset(size, offset):
    return [(i, i ^ offset) for i in range(size)]


def make_per_device(size):
    def per_device(tokens, out_grad, router, in_weight, out_weight):
        _, patches, model_width = tokens.shape
        chips = router.shape[1]
        me = lax.axis_index("expert")
        chip = me // 2
        core = me % 2
        tokens = tokens[0]
        out_grad = out_grad[0]
        slots = jnp.arange(chips)
        swap = (slots[:, None] == (slots[None, :] ^ chip)).astype(jnp.bfloat16)
        router_rel = jnp.einsum("ds,sk->dk", router, swap)
        logits = jnp.einsum("ds,pd->sp", router_rel, tokens, preferred_element_type=jnp.float32)
        dispatch = jax.nn.softmax(logits, axis=1)
        combine = jax.nn.softmax(logits, axis=0)
        dispatch_b = dispatch.astype(jnp.bfloat16)
        combine_b = combine.astype(jnp.bfloat16)
        slot_in = jnp.einsum(
            "sp,pd->sd", dispatch_b, tokens, preferred_element_type=jnp.float32
        ).astype(jnp.bfloat16)
        slot_grad = jnp.einsum(
            "sp,pd->sd", combine_b, out_grad, preferred_element_type=jnp.float32
        ).astype(jnp.bfloat16)
        rows = []
        for k in range(chips):
            message = jnp.stack([slot_in[k], slot_grad[k]])
            for c in range(2):
                offset = 2 * k + c
                if offset:
                    message_k = lax.ppermute(message, "expert", by_offset(size, offset))
                else:
                    message_k = message
                rows.append(message_k)
        got = jnp.stack(rows)
        part_out, part_in = expert_rows(got[:, 0], got[:, 1], in_weight, out_weight)
        parts = jnp.stack([part_out, part_in], axis=1).reshape(chips, 2, 2, model_width)
        other = lax.ppermute(parts[:, 1], "expert", by_offset(size, 1))
        mine = (parts[:, 0] + other).astype(jnp.bfloat16)
        back = [mine[0]]
        for k in range(1, chips):
            back.append(lax.ppermute(mine[k], "expert", by_offset(size, 2 * k)))
        back = jnp.stack(back)
        slot_out = back[:, 0]
        slot_back = back[:, 1]
        combine_grad = jnp.einsum("pd,sd->sp", out_grad, slot_out, preferred_element_type=jnp.float32)
        dispatch_grad = jnp.einsum("pd,sd->sp", tokens, slot_back, preferred_element_type=jnp.float32)
        logits_grad = combine * (combine_grad - jnp.sum(combine * combine_grad, axis=0, keepdims=True))
        logits_grad = logits_grad + dispatch * (
            dispatch_grad - jnp.sum(dispatch * dispatch_grad, axis=1, keepdims=True)
        )
        logits_b = logits_grad.astype(jnp.bfloat16)
        logits_abs = jnp.einsum("ks,kp->sp", swap, logits_b)
        half = model_width // 2
        router_part = jnp.einsum("sp,pd->sd", logits_abs, tokens, preferred_element_type=jnp.float32)
        router_part = router_part.reshape(chips, 2, half)
        kept = lax.dynamic_index_in_dim(router_part, core, 1, keepdims=False)
        given = lax.dynamic_index_in_dim(router_part, 1 - core, 1, keepdims=False)
        total = kept + lax.ppermute(given, "expert", by_offset(size, 1))
        radix = 2
        while radix < size:
            width = 2 if radix == 2 else min(4, size // radix)
            total = sum_of(total, radix, width, size)
            radix *= width
        theirs = lax.ppermute(total, "expert", by_offset(size, 1))
        pair = jnp.where(core == 0, jnp.stack([total, theirs]), jnp.stack([theirs, total]))
        router_grad = pair.transpose(0, 2, 1).reshape(model_width, chips)
        tokens_grad = jnp.einsum(
            "sp,sd->pd", dispatch_b, slot_back, preferred_element_type=jnp.float32
        )
        tokens_grad = tokens_grad + jnp.einsum(
            "sp,ds->pd", logits_abs, router, preferred_element_type=jnp.float32
        )
        return (tokens_grad.astype(jnp.bfloat16)[None], router_grad)

    return per_device


def sum_of(value, radix, width, size):
    if width == 2:
        return value + lax.ppermute(value, "expert", by_offset(size, radix))
    terms = [value] + [
        lax.ppermute(value, "expert", by_offset(size, radix * k)) for k in range(1, width)
    ]
    return (terms[0] + terms[1]) + (terms[2] + terms[3])


def solution(mesh):
    in_specs = (
        P(("group", "expert"), None, None),
        P(("group", "expert"), None, None),
        P(),
        P(None, "expert"),
        P("expert", None),
    )
    out_specs = (P(("group", "expert"), None, None), P("group", None))
    return jax.shard_map(
        make_per_device(mesh.shape["expert"]),
        mesh=mesh,
        in_specs=in_specs,
        out_specs=out_specs,
        check_vma=False,
    )
```

```python
import functools
import math

import jax
import jax.numpy as jnp
from jax import lax
from jax.experimental import pallas as pl
from jax.experimental.pallas import tpu as pltpu
from jax.sharding import PartitionSpec as P

F32 = jnp.float32
BF16 = jnp.bfloat16
NN = (((1,), (0,)), ((), ()))
NT = (((1,), (1,)), ((), ()))
TN = (((0,), (0,)), ((), ()))


def dot(a, b, dims):
    return lax.dot_general(a, b, dims, preferred_element_type=F32)


def even_rows(shape):
    return lax.broadcasted_iota(jnp.int32, shape, 0) % 2 == 0


def spread_matrix(rows):
    row = lax.broadcasted_iota(jnp.int32, (rows, rows // 2), 0)
    column = lax.broadcasted_iota(jnp.int32, (rows, rows // 2), 1)
    return (row // 2 == column).astype(F32).astype(BF16)


def pick_matrix(rows):
    row = lax.broadcasted_iota(jnp.int32, (rows // 2, rows), 0)
    column = lax.broadcasted_iota(jnp.int32, (rows // 2, rows), 1)
    return (2 * row == column).astype(F32).astype(BF16)


def slots_kernel(tokens_ref, grad_ref, router_ref, sent_ref, dispatch_ref, combine_ref, router2_ref):
    slots = router_ref.shape[0]
    rows = 2 * slots
    router2 = dot(spread_matrix(rows), router_ref[...], NN).astype(BF16)
    router2_ref[...] = router2
    logits = dot(router2, tokens_ref[...], NT)
    even = even_rows(logits.shape)
    over_patches = jnp.exp(logits - jnp.max(logits, axis=1, keepdims=True))
    dispatch = over_patches / jnp.sum(over_patches, axis=1, keepdims=True)
    over_slots = jnp.exp(logits - jnp.max(logits, axis=0, keepdims=True))
    slot_sum = jnp.sum(jnp.where(even, over_slots, 0.0), axis=0, keepdims=True)
    combine = over_slots / slot_sum
    dispatch_ref[...] = dispatch
    combine_ref[...] = combine
    both = dot(jnp.where(even, dispatch, 0.0).astype(BF16), tokens_ref[...], NN)
    both = both + dot(jnp.where(even, 0.0, combine).astype(BF16), grad_ref[...], NN)
    for s in range(slots):
        sent_ref[s] = both[2 * s : 2 * s + 2].astype(BF16)


def experts_kernel(
    got_ref, other_ref, in_weight_ref, out_weight_ref, mine_ref, theirs_ref, rows_ref
):
    images = got_ref.shape[0]
    for k in range(images):
        rows_ref[2 * k : 2 * k + 2] = got_ref[k].astype(F32)
        rows_ref[2 * (images + k) : 2 * (images + k) + 2] = other_ref[k].astype(F32)
    rows = rows_ref[...].astype(BF16)
    hidden = dot(rows, in_weight_ref[...], NN)
    act_grad = dot(rows, out_weight_ref[...], NT)
    even = even_rows(hidden.shape)
    normal_cdf = 0.5 * (1.0 + lax.erf(hidden * (1.0 / math.sqrt(2.0))))
    normal_pdf = jnp.exp(-0.5 * hidden * hidden) * (1.0 / math.sqrt(2.0 * math.pi))
    slope = pltpu.roll(normal_cdf + hidden * normal_pdf, 1, 0)
    inner = jnp.where(even, hidden * normal_cdf, act_grad * slope).astype(BF16)
    part_out = dot(inner, out_weight_ref[...], NN)
    part_in = dot(inner, in_weight_ref[...], NT)
    parts = jnp.where(even_rows(part_out.shape), part_out, part_in)
    for k in range(images):
        mine_ref[k] = parts[2 * k : 2 * k + 2]
        theirs_ref[k] = parts[2 * (images + k) : 2 * (images + k) + 2]


def logits_kernel(
    tokens_ref,
    grad_ref,
    router2_ref,
    dispatch_ref,
    combine_ref,
    back_ref,
    kept_ref,
    given_ref,
    left_ref,
    right_ref,
    rows_ref,
):
    slots = back_ref.shape[0]
    for s in range(slots):
        rows_ref[2 * s : 2 * s + 2] = back_ref[s].astype(F32)
    back = rows_ref[...]
    back_b = back.astype(BF16)
    combine_grad = dot(back_b, grad_ref[...], NT)
    dispatch_grad = dot(back_b, tokens_ref[...], NT)
    even = even_rows(combine_grad.shape)
    dispatch = dispatch_ref[...]
    combine = combine_ref[...]
    slot_sum = jnp.sum(jnp.where(even, combine * combine_grad, 0.0), axis=0, keepdims=True)
    patch_sum = jnp.sum(dispatch * dispatch_grad, axis=1, keepdims=True)
    patch_term = dispatch * (dispatch_grad - patch_sum)
    patch_term = pltpu.roll(patch_term, 2 * slots - 1, 0)
    logits_grad = combine * (combine_grad - slot_sum) + patch_term
    logits_b = jnp.where(even, logits_grad, 0.0).astype(BF16)
    packed = dot(pick_matrix(2 * slots), logits_b, NN).astype(BF16)
    part = dot(packed, tokens_ref[...], NN)
    half = part.shape[1] // 2
    first = lax.axis_index("core") == 0
    kept_ref[...] = jnp.where(first, part[:, :half], part[:, half:])
    given_ref[...] = jnp.where(first, part[:, half:], part[:, :half])
    left_ref[...] = jnp.where(even, logits_grad, dispatch).astype(BF16)
    right_ref[...] = jnp.where(
        even_rows(back.shape), router2_ref[...].astype(F32), back
    ).astype(BF16)


def tokens_kernel(left_ref, right_ref, tokens_grad_ref):
    tokens_grad_ref[...] = dot(left_ref[...], right_ref[...], TN).astype(BF16)


def call(kernel, outs, scratch, cost, *operands):
    return pl.pallas_call(
        kernel,
        out_shape=[jax.ShapeDtypeStruct(shape, dtype) for shape, dtype in outs],
        in_specs=[pl.BlockSpec(memory_space=pltpu.VMEM)] * len(operands),
        out_specs=[pl.BlockSpec(memory_space=pltpu.VMEM)] * len(outs),
        scratch_shapes=[pltpu.VMEM(shape, F32) for shape in scratch],
        compiler_params=pltpu.CompilerParams(vmem_limit_bytes=16 * 1024 * 1024),
        cost_estimate=pl.CostEstimate(flops=cost[0], bytes_accessed=cost[1], transcendentals=0),
    )(*operands)


def swap_cores(value):
    return lax.ppermute(value, "core", [(0, 1), (1, 0)])


def between_chips(value):
    return lax.all_to_all(value, "chip", split_axis=0, concat_axis=0, tiled=True)


def per_device(tokens, out_grad, router, in_weight, out_weight):
    _, patches, width = tokens.shape
    hidden = in_weight.shape[1]
    slots = router.shape[1]
    tokens = tokens[0]
    out_grad = out_grad[0]
    image_bytes = 2 * patches * width
    weight_bytes = 2 * width * hidden
    sent, dispatch, combine, router2 = call(
        slots_kernel,
        [
            ((slots, 2, width), BF16),
            ((2 * slots, patches), F32),
            ((2 * slots, patches), F32),
            ((2 * slots, width), BF16),
        ],
        [],
        (12 * patches * width * slots, 2 * image_bytes),
        tokens,
        out_grad,
        router.T,
    )
    got = between_chips(sent)
    other = swap_cores(got)
    mine, theirs = call(
        experts_kernel,
        [((slots, 2, width), F32), ((slots, 2, width), F32)],
        [(4 * slots, width)],
        (32 * slots * width * hidden, 2 * weight_bytes),
        got,
        other,
        in_weight,
        out_weight,
    )
    back = between_chips((mine + swap_cores(theirs)).astype(BF16))
    kept, given, left, right = call(
        logits_kernel,
        [
            ((slots, width // 2), F32),
            ((slots, width // 2), F32),
            ((2 * slots, patches), BF16),
            ((2 * slots, width), BF16),
        ],
        [(2 * slots, width)],
        (12 * patches * width * slots, 2 * image_bytes),
        tokens,
        out_grad,
        router2,
        dispatch,
        combine,
        back,
    )
    pair = kept + swap_cores(given)
    chips = lax.axis_size("chip")
    terms = between_chips(jnp.broadcast_to(pair[None], (chips,) + pair.shape))
    total = jnp.sum(terms, axis=0)
    theirs_total = swap_cores(total)
    first = lax.axis_index("core") == 0
    router_grad = jnp.concatenate(
        [jnp.where(first, total, theirs_total), jnp.where(first, theirs_total, total)], axis=1
    )
    (tokens_grad,) = call(
        tokens_kernel,
        [((patches, width), BF16)],
        [],
        (4 * patches * width * slots, image_bytes),
        left,
        right,
    )
    return (tokens_grad[None], router_grad.T)


def solution(mesh):
    shape = (mesh.shape["group"], mesh.shape["expert"] // 2, 2)
    fine = jax.sharding.Mesh(mesh.devices.reshape(shape), ("group", "chip", "core"))
    expert = ("chip", "core")
    in_specs = (
        P(("group", "chip", "core"), None, None),
        P(("group", "chip", "core"), None, None),
        P(),
        P(None, expert),
        P(expert, None),
    )
    out_specs = (P(("group", "chip", "core"), None, None), P("group", None))
    return jax.shard_map(
        per_device, mesh=fine, in_specs=in_specs, out_specs=out_specs, check_vma=False
    )
```

```python
import functools
import math

import jax
import jax.numpy as jnp
from jax import lax
from jax.experimental import pallas as pl
from jax.experimental.pallas import tpu as pltpu
from jax.sharding import PartitionSpec as P

F32 = jnp.float32
BF16 = jnp.bfloat16
NN = (((1,), (0,)), ((), ()))
NT = (((1,), (1,)), ((), ()))
AHEAD_FLOPS = 3 * 10**10
TN = (((0,), (0,)), ((), ()))


def dot(a, b, dims):
    return lax.dot_general(a, b, dims, preferred_element_type=F32)


def even_rows(shape):
    return lax.broadcasted_iota(jnp.int32, shape, 0) % 2 == 0


def spread_matrix(rows):
    row = lax.broadcasted_iota(jnp.int32, (rows, rows // 2), 0)
    column = lax.broadcasted_iota(jnp.int32, (rows, rows // 2), 1)
    return (row // 2 == column).astype(F32).astype(BF16)


def pick_matrix(rows):
    row = lax.broadcasted_iota(jnp.int32, (rows // 2, rows), 0)
    column = lax.broadcasted_iota(jnp.int32, (rows // 2, rows), 1)
    return (2 * row == column).astype(F32).astype(BF16)


def spread_kernel(spread_ref):
    spread_ref[...] = spread_matrix(spread_ref.shape[0])


def slots_kernel(
    tokens_ref, grad_ref, router_ref, spread_ref, sent_ref, dispatch_ref, combine_ref, router2_ref
):
    slots = router_ref.shape[0]
    router2 = dot(spread_ref[...], router_ref[...], NN).astype(BF16)
    router2_ref[...] = router2
    logits = dot(router2, tokens_ref[...], NT)
    even = even_rows(logits.shape)
    over_patches = jnp.exp(logits - jnp.max(logits, axis=1, keepdims=True))
    dispatch = over_patches / jnp.sum(over_patches, axis=1, keepdims=True)
    over_slots = jnp.exp(logits - jnp.max(logits, axis=0, keepdims=True))
    slot_sum = jnp.sum(jnp.where(even, over_slots, 0.0), axis=0, keepdims=True)
    combine = over_slots / slot_sum
    dispatch_ref[...] = dispatch
    combine_ref[...] = combine
    both = dot(jnp.where(even, dispatch, 0.0).astype(BF16), tokens_ref[...], NN)
    both = both + dot(jnp.where(even, 0.0, combine).astype(BF16), grad_ref[...], NN)
    for s in range(slots):
        sent_ref[s] = both[2 * s : 2 * s + 2].astype(BF16)


def experts_kernel(
    got_ref, other_ref, in_weight_ref, out_weight_ref, mine_ref, theirs_ref, rows_ref
):
    images = got_ref.shape[0]
    for k in range(images):
        rows_ref[2 * k : 2 * k + 2] = got_ref[k].astype(F32)
        rows_ref[2 * (images + k) : 2 * (images + k) + 2] = other_ref[k].astype(F32)
    rows = rows_ref[...].astype(BF16)
    hidden = dot(rows, in_weight_ref[...], NN)
    act_grad = dot(rows, out_weight_ref[...], NT)
    even = even_rows(hidden.shape)
    normal_cdf = 0.5 * (1.0 + lax.erf(hidden * (1.0 / math.sqrt(2.0))))
    normal_pdf = jnp.exp(-0.5 * hidden * hidden) * (1.0 / math.sqrt(2.0 * math.pi))
    slope = pltpu.roll(normal_cdf + hidden * normal_pdf, 1, 0)
    inner = jnp.where(even, hidden * normal_cdf, act_grad * slope).astype(BF16)
    part_out = dot(inner, out_weight_ref[...], NN)
    part_in = dot(inner, in_weight_ref[...], NT)
    parts = jnp.where(even_rows(part_out.shape), part_out, part_in)
    for k in range(images):
        mine_ref[k] = parts[2 * k : 2 * k + 2]
        theirs_ref[k] = parts[2 * (images + k) : 2 * (images + k) + 2]


def logits_kernel(
    tokens_ref,
    grad_ref,
    router2_ref,
    dispatch_ref,
    combine_ref,
    back_ref,
    kept_ref,
    given_ref,
    left_ref,
    right_ref,
    rows_ref,
):
    slots = back_ref.shape[0]
    for s in range(slots):
        rows_ref[2 * s : 2 * s + 2] = back_ref[s].astype(F32)
    back = rows_ref[...]
    back_b = back.astype(BF16)
    combine_grad = dot(back_b, grad_ref[...], NT)
    dispatch_grad = dot(back_b, tokens_ref[...], NT)
    even = even_rows(combine_grad.shape)
    dispatch = dispatch_ref[...]
    combine = combine_ref[...]
    slot_sum = jnp.sum(jnp.where(even, combine * combine_grad, 0.0), axis=0, keepdims=True)
    patch_sum = jnp.sum(dispatch * dispatch_grad, axis=1, keepdims=True)
    patch_term = dispatch * (dispatch_grad - patch_sum)
    patch_term = pltpu.roll(patch_term, 2 * slots - 1, 0)
    logits_grad = combine * (combine_grad - slot_sum) + patch_term
    logits_b = jnp.where(even, logits_grad, 0.0).astype(BF16)
    packed = dot(pick_matrix(2 * slots), logits_b, NN).astype(BF16)
    part = dot(packed, tokens_ref[...], NN)
    half = part.shape[1] // 2
    first = lax.axis_index("core") == 0
    kept_ref[...] = jnp.where(first, part[:, :half], part[:, half:])
    given_ref[...] = jnp.where(first, part[:, half:], part[:, :half])
    left_ref[...] = jnp.where(even, logits_grad, dispatch).astype(BF16)
    right_ref[...] = jnp.where(
        even_rows(back.shape), router2_ref[...].astype(F32), back
    ).astype(BF16)


def tokens_kernel(left_ref, right_ref, tokens_grad_ref):
    tokens_grad_ref[...] = dot(left_ref[...], right_ref[...], TN).astype(BF16)


def call(kernel, outs, scratch, cost, *operands):
    return pl.pallas_call(
        kernel,
        out_shape=[jax.ShapeDtypeStruct(shape, dtype) for shape, dtype in outs],
        in_specs=[pl.BlockSpec(memory_space=pltpu.VMEM)] * len(operands),
        out_specs=[pl.BlockSpec(memory_space=pltpu.VMEM)] * len(outs),
        scratch_shapes=[pltpu.VMEM(shape, F32) for shape in scratch],
        compiler_params=pltpu.CompilerParams(vmem_limit_bytes=16 * 1024 * 1024),
        cost_estimate=pl.CostEstimate(flops=cost[0], bytes_accessed=cost[1], transcendentals=0),
    )(*operands)


def swap_cores(value):
    return lax.ppermute(value, "core", [(0, 1), (1, 0)])


def between_chips(value):
    return lax.all_to_all(value, "chip", split_axis=0, concat_axis=0, tiled=True)


def per_device(tokens, out_grad, router, in_weight, out_weight):
    _, patches, width = tokens.shape
    hidden = in_weight.shape[1]
    slots = router.shape[1]
    tokens = tokens[0]
    out_grad = out_grad[0]
    image_bytes = 2 * patches * width
    weight_bytes = 2 * width * hidden
    (spread,) = call(
        spread_kernel,
        [((2 * slots, slots), BF16)],
        [],
        (AHEAD_FLOPS, image_bytes),
    )
    sent, dispatch, combine, router2 = call(
        slots_kernel,
        [
            ((slots, 2, width), BF16),
            ((2 * slots, patches), F32),
            ((2 * slots, patches), F32),
            ((2 * slots, width), BF16),
        ],
        [],
        (12 * patches * width * slots, 2 * image_bytes),
        tokens,
        out_grad,
        router.T,
        spread,
    )
    got = between_chips(sent)
    other = swap_cores(got)
    mine, theirs = call(
        experts_kernel,
        [((slots, 2, width), F32), ((slots, 2, width), F32)],
        [(4 * slots, width)],
        (32 * slots * width * hidden, 2 * weight_bytes),
        got,
        other,
        in_weight,
        out_weight,
    )
    back = between_chips((mine + swap_cores(theirs)).astype(BF16))
    kept, given, left, right = call(
        logits_kernel,
        [
            ((slots, width // 2), F32),
            ((slots, width // 2), F32),
            ((2 * slots, patches), BF16),
            ((2 * slots, width), BF16),
        ],
        [(2 * slots, width)],
        (12 * patches * width * slots, 2 * image_bytes),
        tokens,
        out_grad,
        router2,
        dispatch,
        combine,
        back,
    )
    pair = (kept + swap_cores(given)).astype(BF16)
    terms = lax.all_gather(pair, "chip")
    total = jnp.sum(terms.astype(F32), axis=0)
    theirs_total = swap_cores(total)
    first = lax.axis_index("core") == 0
    router_grad = jnp.concatenate(
        [jnp.where(first, total, theirs_total), jnp.where(first, theirs_total, total)], axis=1
    )
    (tokens_grad,) = call(
        tokens_kernel,
        [((patches, width), BF16)],
        [],
        (4 * patches * width * slots, image_bytes),
        left,
        right,
    )
    return (tokens_grad[None], router_grad.T)


def solution(mesh):
    shape = (mesh.shape["group"], mesh.shape["expert"] // 2, 2)
    fine = jax.sharding.Mesh(mesh.devices.reshape(shape), ("group", "chip", "core"))
    expert = ("chip", "core")
    in_specs = (
        P(("group", "chip", "core"), None, None),
        P(("group", "chip", "core"), None, None),
        P(),
        P(None, expert),
        P(expert, None),
    )
    out_specs = (P(("group", "chip", "core"), None, None), P("group", None))
    return jax.shard_map(
        per_device, mesh=fine, in_specs=in_specs, out_specs=out_specs, check_vma=False
    )
```

```python
import math

import jax
import jax.numpy as jnp
from jax import lax
from jax.experimental import pallas as pl
from jax.experimental.pallas import tpu as pltpu
from jax.sharding import PartitionSpec as P

F32 = jnp.float32
BF16 = jnp.bfloat16
NN = (((1,), (0,)), ((), ()))
NT = (((1,), (1,)), ((), ()))
TN = (((0,), (0,)), ((), ()))
AHEAD_FLOPS = 3 * 10**10


def dot(a, b, dims):
    return lax.dot_general(a, b, dims, preferred_element_type=F32)


def first_kernel(token_ref):
    token_ref[...] = jnp.zeros(token_ref.shape, F32)


def slots_kernel(
    tokens_ref, grad_ref, router_ref, token_ref, sent_ref, dispatch_ref, combine_ref
):
    slots = router_ref.shape[0]
    logits = dot(router_ref[...], tokens_ref[...], NT)
    over_patches = jnp.exp(logits - jnp.max(logits, axis=1, keepdims=True))
    dispatch = over_patches / jnp.sum(over_patches, axis=1, keepdims=True)
    over_slots = jnp.exp(logits - jnp.max(logits, axis=0, keepdims=True))
    combine = over_slots / jnp.sum(over_slots, axis=0, keepdims=True)
    dispatch_ref[...] = dispatch
    combine_ref[...] = combine
    slot_in = dot(dispatch.astype(BF16), tokens_ref[...], NN)
    slot_grad = dot(combine.astype(BF16), grad_ref[...], NN)
    for s in range(slots):
        message = jnp.concatenate([slot_in[s : s + 1], slot_grad[s : s + 1]], axis=0).astype(BF16)
        for half in range(2):
            sent_ref[2 * s + half] = message


def experts_kernel(
    got_ref, in_weight_ref, out_weight_ref, mine_ref, theirs_ref, in_rows_ref, grad_rows_ref
):
    images = got_ref.shape[0]
    for k in range(images):
        message = got_ref[k].astype(F32)
        in_rows_ref[k : k + 1] = message[0:1]
        grad_rows_ref[k : k + 1] = message[1:2]
    hidden = dot(in_rows_ref[...].astype(BF16), in_weight_ref[...], NN)
    act_grad = dot(grad_rows_ref[...].astype(BF16), out_weight_ref[...], NT)
    normal_cdf = 0.5 * (1.0 + lax.erf(hidden * (1.0 / math.sqrt(2.0))))
    normal_pdf = jnp.exp(-0.5 * hidden * hidden) * (1.0 / math.sqrt(2.0 * math.pi))
    activation = (hidden * normal_cdf).astype(BF16)
    hidden_grad = (act_grad * (normal_cdf + hidden * normal_pdf)).astype(BF16)
    part_out = dot(activation, out_weight_ref[...], NN)
    part_in = dot(hidden_grad, in_weight_ref[...], NT)
    first = lax.axis_index("core") == 0
    for k in range(images // 2):
        pair = [
            jnp.concatenate([part_out[i : i + 1], part_in[i : i + 1]], axis=0)
            for i in (2 * k, 2 * k + 1)
        ]
        mine_ref[k] = jnp.where(first, pair[0], pair[1])
        theirs_ref[k] = jnp.where(first, pair[1], pair[0])


def logits_kernel(
    tokens_ref,
    grad_ref,
    router_ref,
    dispatch_ref,
    combine_ref,
    back_ref,
    kept_ref,
    given_ref,
    left_ref,
    right_ref,
    out_rows_ref,
    back_rows_ref,
):
    slots = back_ref.shape[0]
    for s in range(slots):
        message = back_ref[s].astype(F32)
        out_rows_ref[s : s + 1] = message[0:1]
        back_rows_ref[s : s + 1] = message[1:2]
    slot_back = back_rows_ref[...].astype(BF16)
    combine_grad = dot(out_rows_ref[...].astype(BF16), grad_ref[...], NT)
    dispatch_grad = dot(slot_back, tokens_ref[...], NT)
    dispatch = dispatch_ref[...]
    combine = combine_ref[...]
    slot_sum = jnp.sum(combine * combine_grad, axis=0, keepdims=True)
    patch_sum = jnp.sum(dispatch * dispatch_grad, axis=1, keepdims=True)
    logits_grad = combine * (combine_grad - slot_sum) + dispatch * (dispatch_grad - patch_sum)
    part = dot(logits_grad.astype(BF16), tokens_ref[...], NN)
    half = part.shape[1] // 2
    first = lax.axis_index("core") == 0
    kept_ref[...] = jnp.where(first, part[:, :half], part[:, half:])
    given_ref[...] = jnp.where(first, part[:, half:], part[:, :half])
    left_ref[...] = jnp.concatenate([logits_grad, dispatch], axis=0).astype(BF16)
    right_ref[...] = jnp.concatenate(
        [router_ref[...].astype(F32), back_rows_ref[...]], axis=0
    ).astype(BF16)


def tokens_kernel(left_ref, right_ref, tokens_grad_ref):
    tokens_grad_ref[...] = dot(left_ref[...], right_ref[...], TN).astype(BF16)


def call(kernel, outs, scratch, cost, *operands):
    return pl.pallas_call(
        kernel,
        out_shape=[jax.ShapeDtypeStruct(shape, dtype) for shape, dtype in outs],
        in_specs=[pl.BlockSpec(memory_space=pltpu.VMEM)] * len(operands),
        out_specs=[pl.BlockSpec(memory_space=pltpu.VMEM)] * len(outs),
        scratch_shapes=[pltpu.VMEM(shape, F32) for shape in scratch],
        compiler_params=pltpu.CompilerParams(vmem_limit_bytes=16 * 1024 * 1024),
        cost_estimate=pl.CostEstimate(flops=cost[0], bytes_accessed=cost[1], transcendentals=0),
    )(*operands)


def swap_cores(value):
    return lax.ppermute(value, "core", [(0, 1), (1, 0)])


def exchange(value, axes):
    return lax.all_to_all(value, axes, split_axis=0, concat_axis=0, tiled=True)


def per_device(tokens, out_grad, router, in_weight, out_weight):
    _, patches, width = tokens.shape
    hidden = in_weight.shape[1]
    slots = router.shape[1]
    chips = lax.axis_size("chip")
    tokens = tokens[0]
    out_grad = out_grad[0]
    router_rows = router.T
    image_bytes = 2 * patches * width
    weight_bytes = 2 * width * hidden
    (token,) = call(first_kernel, [((8, 128), F32)], [], (AHEAD_FLOPS, image_bytes))
    sent, dispatch, combine = call(
        slots_kernel,
        [((2 * slots, 2, width), BF16), ((slots, patches), F32), ((slots, patches), F32)],
        [],
        (12 * patches * width * slots, 2 * image_bytes),
        tokens,
        out_grad,
        router_rows,
        token,
    )
    got = exchange(sent, ("chip", "core"))
    mine, theirs = call(
        experts_kernel,
        [((chips, 2, width), F32), ((chips, 2, width), F32)],
        [(2 * chips, width), (2 * chips, width)],
        (16 * chips * width * hidden, 2 * weight_bytes),
        got,
        in_weight,
        out_weight,
    )
    back = exchange((mine + swap_cores(theirs)).astype(BF16), "chip")
    kept, given, left, right = call(
        logits_kernel,
        [
            ((slots, width // 2), F32),
            ((slots, width // 2), F32),
            ((2 * slots, patches), BF16),
            ((2 * slots, width), BF16),
        ],
        [(slots, width), (slots, width)],
        (12 * patches * width * slots, 2 * image_bytes),
        tokens,
        out_grad,
        router_rows,
        dispatch,
        combine,
        back,
    )
    pair = (kept + swap_cores(given)).astype(BF16)
    terms = exchange(jnp.broadcast_to(pair[None], (chips,) + pair.shape), "chip")
    total = jnp.sum(terms.astype(F32), axis=0)
    other = swap_cores(total)
    first = lax.axis_index("core") == 0
    router_grad = jnp.concatenate(
        [jnp.where(first, total, other), jnp.where(first, other, total)], axis=1
    )
    (tokens_grad,) = call(
        tokens_kernel,
        [((patches, width), BF16)],
        [],
        (4 * patches * width * slots, image_bytes),
        left,
        right,
    )
    return (tokens_grad[None], router_grad.T)


def solution(mesh):
    shape = (mesh.shape["group"], mesh.shape["expert"] // 2, 2)
    fine = jax.sharding.Mesh(mesh.devices.reshape(shape), ("group", "chip", "core"))
    expert = ("chip", "core")
    in_specs = (
        P(("group", "chip", "core"), None, None),
        P(("group", "chip", "core"), None, None),
        P(),
        P(None, expert),
        P(expert, None),
    )
    out_specs = (P(("group", "chip", "core"), None, None), P("group", None))
    return jax.shard_map(
        per_device, mesh=fine, in_specs=in_specs, out_specs=out_specs, check_vma=False
    )
```

```python
import math

import jax
import jax.numpy as jnp
from jax import lax
from jax.experimental import pallas as pl
from jax.experimental.pallas import tpu as pltpu
from jax.sharding import PartitionSpec as P

F32 = jnp.float32
BF16 = jnp.bfloat16
NN = (((1,), (0,)), ((), ()))
NT = (((1,), (1,)), ((), ()))
TN = (((0,), (0,)), ((), ()))
AHEAD_FLOPS = 3 * 10**10
PIECES = 4


def dot(a, b, dims):
    return lax.dot_general(a, b, dims, preferred_element_type=F32)


def slots_kernel(
    tokens_hbm,
    grad_hbm,
    router_hbm,
    slot_in_ref,
    slot_grad_ref,
    dispatch_ref,
    combine_ref,
    tokens_ref,
    grad_ref,
    router_ref,
    arrived,
):
    def pieces(source, target, first, count):
        rows = source.shape[0] // count
        return [
            pltpu.make_async_copy(
                source.at[pl.ds(i * rows, rows)],
                target.at[pl.ds(i * rows, rows)],
                arrived.at[first + i],
            )
            for i in range(count)
        ]

    router_copy = pltpu.make_async_copy(router_hbm, router_ref, arrived.at[2 * PIECES])
    token_copies = pieces(tokens_hbm, tokens_ref, 0, PIECES)
    grad_copies = pieces(grad_hbm, grad_ref, PIECES, PIECES)
    for copy in [router_copy] + token_copies + grad_copies:
        copy.start()
    for copy in [router_copy] + token_copies:
        copy.wait()
    logits = dot(router_ref[...], tokens_ref[...], NT)
    over_patches = jnp.exp(logits - jnp.max(logits, axis=1, keepdims=True))
    dispatch = over_patches / jnp.sum(over_patches, axis=1, keepdims=True)
    over_slots = jnp.exp(logits - jnp.max(logits, axis=0, keepdims=True))
    combine = over_slots / jnp.sum(over_slots, axis=0, keepdims=True)
    dispatch_ref[...] = dispatch
    combine_ref[...] = combine
    slot_in_ref[...] = dot(dispatch.astype(BF16), tokens_ref[...], NN)
    for copy in grad_copies:
        copy.wait()
    slot_grad_ref[...] = dot(combine.astype(BF16), grad_ref[...], NN)


def messages_kernel(slot_in_ref, slot_grad_ref, sent_ref):
    for s in range(slot_in_ref.shape[0]):
        rows = [slot_in_ref[s : s + 1], slot_grad_ref[s : s + 1]]
        message = jnp.concatenate(rows, axis=0).astype(BF16)
        for half in range(2):
            sent_ref[2 * s + half] = message


def experts_kernel(
    got_ref, in_weight_ref, out_weight_ref, parts_ref, in_rows_ref, grad_rows_ref
):
    images = got_ref.shape[0]
    for k in range(images):
        message = got_ref[k].astype(F32)
        in_rows_ref[k : k + 1] = message[0:1]
        grad_rows_ref[k : k + 1] = message[1:2]
    hidden = dot(in_rows_ref[...].astype(BF16), in_weight_ref[...], NN)
    act_grad = dot(grad_rows_ref[...].astype(BF16), out_weight_ref[...], NT)
    normal_cdf = 0.5 * (1.0 + lax.erf(hidden * (1.0 / math.sqrt(2.0))))
    normal_pdf = jnp.exp(-0.5 * hidden * hidden) * (1.0 / math.sqrt(2.0 * math.pi))
    activation = (hidden * normal_cdf).astype(BF16)
    hidden_grad = (act_grad * (normal_cdf + hidden * normal_pdf)).astype(BF16)
    part_out = dot(activation, out_weight_ref[...], NN)
    part_in = dot(hidden_grad, in_weight_ref[...], NT)
    for k in range(images):
        rows = [part_out[k : k + 1], part_in[k : k + 1]]
        parts_ref[k] = jnp.concatenate(rows, axis=0).astype(BF16)


def logits_kernel(
    tokens_ref,
    grad_ref,
    router_ref,
    dispatch_ref,
    combine_ref,
    back_ref,
    kept_ref,
    given_ref,
    left_ref,
    right_ref,
    out_rows_ref,
    back_rows_ref,
):
    slots = router_ref.shape[0]
    for s in range(slots):
        message = back_ref[2 * s].astype(F32) + back_ref[2 * s + 1].astype(F32)
        out_rows_ref[s : s + 1] = message[0:1]
        back_rows_ref[s : s + 1] = message[1:2]
    slot_back = back_rows_ref[...].astype(BF16)
    combine_grad = dot(out_rows_ref[...].astype(BF16), grad_ref[...], NT)
    dispatch_grad = dot(slot_back, tokens_ref[...], NT)
    dispatch = dispatch_ref[...]
    combine = combine_ref[...]
    slot_sum = jnp.sum(combine * combine_grad, axis=0, keepdims=True)
    patch_sum = jnp.sum(dispatch * dispatch_grad, axis=1, keepdims=True)
    logits_grad = combine * (combine_grad - slot_sum) + dispatch * (dispatch_grad - patch_sum)
    part = dot(logits_grad.astype(BF16), tokens_ref[...], NN)
    half = part.shape[1] // 2
    first = lax.axis_index("core") == 0
    kept_ref[...] = jnp.where(first, part[:, :half], part[:, half:])
    given_ref[...] = jnp.where(first, part[:, half:], part[:, :half])
    left_ref[...] = jnp.concatenate([logits_grad, dispatch], axis=0).astype(BF16)
    right_ref[...] = jnp.concatenate(
        [router_ref[...].astype(F32), back_rows_ref[...]], axis=0
    ).astype(BF16)


def tokens_kernel(left_ref, right_ref, tokens_grad_ref):
    tokens_grad_ref[...] = dot(left_ref[...], right_ref[...], TN).astype(BF16)


def call(kernel, outs, scratch, cost, *operands, space=pltpu.VMEM):
    return pl.pallas_call(
        kernel,
        out_shape=[jax.ShapeDtypeStruct(shape, dtype) for shape, dtype in outs],
        in_specs=[pl.BlockSpec(memory_space=space)] * len(operands),
        out_specs=[pl.BlockSpec(memory_space=pltpu.VMEM)] * len(outs),
        scratch_shapes=scratch,
        compiler_params=pltpu.CompilerParams(vmem_limit_bytes=16 * 2**20),
        cost_estimate=pl.CostEstimate(flops=cost[0], bytes_accessed=cost[1], transcendentals=0),
    )(*operands)


def swap_cores(value):
    return lax.ppermute(value, "core", [(0, 1), (1, 0)])


def exchange(value, axes):
    return lax.all_to_all(value, axes, split_axis=0, concat_axis=0, tiled=True)


def per_device(tokens, out_grad, router, in_weight, out_weight):
    _, patches, width = tokens.shape
    hidden = in_weight.shape[1]
    slots = router.shape[1]
    chips = lax.axis_size("chip")
    tokens = tokens[0]
    out_grad = out_grad[0]
    router_rows = router.T
    image_bytes = 2 * patches * width
    weight_bytes = 2 * width * hidden
    slot_in, slot_grad, dispatch, combine = call(
        slots_kernel,
        [((slots, width), F32)] * 2 + [((slots, patches), F32)] * 2,
        [
            pltpu.VMEM((patches, width), BF16),
            pltpu.VMEM((patches, width), BF16),
            pltpu.VMEM((slots, width), BF16),
            pltpu.SemaphoreType.DMA((2 * PIECES + 1,)),
        ],
        (12 * patches * width * slots, 2 * image_bytes),
        pltpu.with_memory_space_constraint(tokens, pltpu.HBM),
        pltpu.with_memory_space_constraint(out_grad, pltpu.HBM),
        pltpu.with_memory_space_constraint(router_rows, pltpu.HBM),
        space=pltpu.HBM,
    )
    (sent,) = call(
        messages_kernel,
        [((2 * slots, 2, width), BF16)],
        [],
        (AHEAD_FLOPS, image_bytes),
        slot_in,
        slot_grad,
    )
    got = exchange(sent, ("chip", "core"))
    (parts,) = call(
        experts_kernel,
        [((2 * chips, 2, width), BF16)],
        [pltpu.VMEM((2 * chips, width), F32)] * 2,
        (16 * chips * width * hidden, 2 * weight_bytes),
        got,
        in_weight,
        out_weight,
    )
    back = exchange(parts, ("chip", "core"))
    kept, given, left, right = call(
        logits_kernel,
        [
            ((slots, width // 2), F32),
            ((slots, width // 2), F32),
            ((2 * slots, patches), BF16),
            ((2 * slots, width), BF16),
        ],
        [pltpu.VMEM((slots, width), F32)] * 2,
        (12 * patches * width * slots, 2 * image_bytes),
        tokens,
        out_grad,
        router_rows,
        dispatch,
        combine,
        back,
    )
    pair = (kept + swap_cores(given)).astype(BF16)
    terms = exchange(jnp.broadcast_to(pair[None], (chips,) + pair.shape), "chip")
    total = jnp.sum(terms.astype(F32), axis=0)
    other = swap_cores(total)
    first = lax.axis_index("core") == 0
    router_grad = jnp.concatenate(
        [jnp.where(first, total, other), jnp.where(first, other, total)], axis=1
    )
    (tokens_grad,) = call(
        tokens_kernel,
        [((patches, width), BF16)],
        [],
        (4 * patches * width * slots, image_bytes),
        left,
        right,
    )
    return (tokens_grad[None], router_grad.T)


def solution(mesh):
    shape = (mesh.shape["group"], mesh.shape["expert"] // 2, 2)
    fine = jax.sharding.Mesh(mesh.devices.reshape(shape), ("group", "chip", "core"))
    expert = ("chip", "core")
    in_specs = (
        P(("group", "chip", "core"), None, None),
        P(("group", "chip", "core"), None, None),
        P(),
        P(None, expert),
        P(expert, None),
    )
    out_specs = (P(("group", "chip", "core"), None, None), P("group", None))
    return jax.shard_map(
        per_device, mesh=fine, in_specs=in_specs, out_specs=out_specs, check_vma=False
    )
```

```python
import math

import jax
import jax.numpy as jnp
from jax import lax
from jax.experimental import pallas as pl
from jax.experimental.pallas import tpu as pltpu
from jax.sharding import PartitionSpec as P

EXPERT = ("far", "near", "core")
F32 = jnp.float32
BF16 = jnp.bfloat16
NN = (((1,), (0,)), ((), ()))
NT = (((1,), (1,)), ((), ()))
TN = (((0,), (0,)), ((), ()))
AHEAD_FLOPS = 3 * 10**10


def dot(a, b, dims):
    return lax.dot_general(a, b, dims, preferred_element_type=F32)


def first_kernel(token_ref):
    token_ref[...] = jnp.zeros(token_ref.shape, F32)


def slots_kernel(
    tokens_ref, grad_ref, router_ref, token_ref, sent_ref, dispatch_ref, combine_ref
):
    slots = router_ref.shape[0]
    logits = dot(router_ref[...], tokens_ref[...], NT)
    over_patches = jnp.exp(logits - jnp.max(logits, axis=1, keepdims=True))
    dispatch = over_patches / jnp.sum(over_patches, axis=1, keepdims=True)
    over_slots = jnp.exp(logits - jnp.max(logits, axis=0, keepdims=True))
    combine = over_slots / jnp.sum(over_slots, axis=0, keepdims=True)
    dispatch_ref[...] = dispatch
    combine_ref[...] = combine
    slot_in = dot(dispatch.astype(BF16), tokens_ref[...], NN)
    slot_grad = dot(combine.astype(BF16), grad_ref[...], NN)
    for s in range(slots):
        message = jnp.concatenate([slot_in[s : s + 1], slot_grad[s : s + 1]], axis=0).astype(BF16)
        for half in range(2):
            sent_ref[2 * s + half] = message


def experts_kernel(
    got_ref, in_weight_ref, out_weight_ref, parts_ref, in_rows_ref, grad_rows_ref
):
    images = got_ref.shape[0]
    for k in range(images):
        message = got_ref[k].astype(F32)
        in_rows_ref[k : k + 1] = message[0:1]
        grad_rows_ref[k : k + 1] = message[1:2]
    hidden = dot(in_rows_ref[...].astype(BF16), in_weight_ref[...], NN)
    act_grad = dot(grad_rows_ref[...].astype(BF16), out_weight_ref[...], NT)
    normal_cdf = 0.5 * (1.0 + lax.erf(hidden * (1.0 / math.sqrt(2.0))))
    normal_pdf = jnp.exp(-0.5 * hidden * hidden) * (1.0 / math.sqrt(2.0 * math.pi))
    activation = (hidden * normal_cdf).astype(BF16)
    hidden_grad = (act_grad * (normal_cdf + hidden * normal_pdf)).astype(BF16)
    part_out = dot(activation, out_weight_ref[...], NN)
    part_in = dot(hidden_grad, in_weight_ref[...], NT)
    for k in range(images):
        rows = [part_out[k : k + 1], part_in[k : k + 1]]
        parts_ref[k] = jnp.concatenate(rows, axis=0).astype(BF16)


def logits_kernel(
    tokens_ref,
    grad_ref,
    router_ref,
    dispatch_ref,
    combine_ref,
    back_ref,
    kept_ref,
    given_ref,
    left_ref,
    right_ref,
    out_rows_ref,
    back_rows_ref,
):
    slots = router_ref.shape[0]
    for s in range(slots):
        message = back_ref[2 * s].astype(F32) + back_ref[2 * s + 1].astype(F32)
        out_rows_ref[s : s + 1] = message[0:1]
        back_rows_ref[s : s + 1] = message[1:2]
    slot_back = back_rows_ref[...].astype(BF16)
    combine_grad = dot(out_rows_ref[...].astype(BF16), grad_ref[...], NT)
    dispatch_grad = dot(slot_back, tokens_ref[...], NT)
    dispatch = dispatch_ref[...]
    combine = combine_ref[...]
    slot_sum = jnp.sum(combine * combine_grad, axis=0, keepdims=True)
    patch_sum = jnp.sum(dispatch * dispatch_grad, axis=1, keepdims=True)
    logits_grad = combine * (combine_grad - slot_sum) + dispatch * (dispatch_grad - patch_sum)
    part = dot(logits_grad.astype(BF16), tokens_ref[...], NN)
    half = part.shape[1] // 2
    first = lax.axis_index("core") == 0
    kept_ref[...] = jnp.where(first, part[:, :half], part[:, half:])
    given_ref[...] = jnp.where(first, part[:, half:], part[:, :half])
    left_ref[...] = jnp.concatenate([logits_grad, dispatch], axis=0).astype(BF16)
    right_ref[...] = jnp.concatenate(
        [router_ref[...].astype(F32), back_rows_ref[...]], axis=0
    ).astype(BF16)


def tokens_kernel(left_ref, right_ref, tokens_grad_ref):
    tokens_grad_ref[...] = dot(left_ref[...], right_ref[...], TN).astype(BF16)


def call(kernel, outs, scratch, cost, *operands):
    return pl.pallas_call(
        kernel,
        out_shape=[jax.ShapeDtypeStruct(shape, dtype) for shape, dtype in outs],
        in_specs=[pl.BlockSpec(memory_space=pltpu.VMEM)] * len(operands),
        out_specs=[pl.BlockSpec(memory_space=pltpu.VMEM)] * len(outs),
        scratch_shapes=[pltpu.VMEM(shape, F32) for shape in scratch],
        compiler_params=pltpu.CompilerParams(vmem_limit_bytes=16 * 2**20),
        cost_estimate=pl.CostEstimate(flops=cost[0], bytes_accessed=cost[1], transcendentals=0),
    )(*operands)


def swap(value, axis):
    return lax.ppermute(value, axis, [(0, 1), (1, 0)])


def exchange(value, axes):
    return lax.all_to_all(value, axes, split_axis=0, concat_axis=0, tiled=True)


def sum_over(value, axis):
    count = lax.axis_size(axis)
    if count == 2:
        return value + swap(value, axis)
    terms = exchange(jnp.broadcast_to(value.astype(BF16)[None], (count,) + value.shape), axis)
    return jnp.sum(terms.astype(F32), axis=0)


def per_device(tokens, out_grad, router, in_weight, out_weight):
    _, patches, width = tokens.shape
    hidden = in_weight.shape[1]
    slots = router.shape[1]
    chips = slots
    tokens = tokens[0]
    out_grad = out_grad[0]
    router_rows = router.T
    image_bytes = 2 * patches * width
    weight_bytes = 2 * width * hidden
    (token,) = call(first_kernel, [((8, 128), F32)], [], (AHEAD_FLOPS, image_bytes))
    sent, dispatch, combine = call(
        slots_kernel,
        [((2 * slots, 2, width), BF16), ((slots, patches), F32), ((slots, patches), F32)],
        [],
        (12 * patches * width * slots, 2 * image_bytes),
        tokens,
        out_grad,
        router_rows,
        token,
    )
    got = exchange(sent, EXPERT)
    (parts,) = call(
        experts_kernel,
        [((2 * chips, 2, width), BF16)],
        [(2 * chips, width)] * 2,
        (16 * chips * width * hidden, 2 * weight_bytes),
        got,
        in_weight,
        out_weight,
    )
    back = exchange(parts, EXPERT)
    kept, given, left, right = call(
        logits_kernel,
        [
            ((slots, width // 2), F32),
            ((slots, width // 2), F32),
            ((2 * slots, patches), BF16),
            ((2 * slots, width), BF16),
        ],
        [(slots, width)] * 2,
        (12 * patches * width * slots, 2 * image_bytes),
        tokens,
        out_grad,
        router_rows,
        dispatch,
        combine,
        back,
    )
    total = sum_over(sum_over(kept + swap(given, "core"), "near"), "far")
    other = swap(total, "core")
    first = lax.axis_index("core") == 0
    router_grad = jnp.concatenate(
        [jnp.where(first, total, other), jnp.where(first, other, total)], axis=1
    )
    (tokens_grad,) = call(
        tokens_kernel,
        [((patches, width), BF16)],
        [],
        (4 * patches * width * slots, image_bytes),
        left,
        right,
    )
    return (tokens_grad[None], router_grad.T)


def solution(mesh):
    chips = mesh.shape["expert"] // 2
    near = 2 ** (int(math.log2(chips)) // 2)
    shape = (mesh.shape["group"], chips // near, near, 2)
    fine = jax.sharding.Mesh(mesh.devices.reshape(shape), ("group",) + EXPERT)
    images = P(("group",) + EXPERT, None, None)
    in_specs = (images, images, P(), P(None, EXPERT), P(EXPERT, None))
    out_specs = (images, P("group", None))
    return jax.shard_map(
        per_device, mesh=fine, in_specs=in_specs, out_specs=out_specs, check_vma=False
    )
```

```python
import math

import jax
import jax.numpy as jnp
from jax import lax
from jax.experimental import pallas as pl
from jax.experimental.pallas import tpu as pltpu
from jax.sharding import PartitionSpec as P

EXPERT = ("chip", "core")
F32 = jnp.float32
BF16 = jnp.bfloat16
NN = (((1,), (0,)), ((), ()))
NT = (((1,), (1,)), ((), ()))
TN = (((0,), (0,)), ((), ()))
AHEAD_FLOPS = 3 * 10**10
CHUNK = 256


def dot(a, b, dims):
    return lax.dot_general(a, b, dims, preferred_element_type=F32)


def first_kernel(token_ref):
    token_ref[...] = jnp.zeros(token_ref.shape, F32)


def slots_kernel(tokens_ref, router_ref, token_ref, slot_in_ref, dispatch_ref, combine_ref):
    logits = dot(router_ref[...], tokens_ref[...], NT)
    over_patches = jnp.exp(logits - jnp.max(logits, axis=1, keepdims=True))
    dispatch = over_patches / jnp.sum(over_patches, axis=1, keepdims=True)
    over_slots = jnp.exp(logits - jnp.max(logits, axis=0, keepdims=True))
    dispatch_ref[...] = dispatch
    combine_ref[...] = over_slots / jnp.sum(over_slots, axis=0, keepdims=True)
    slot_in_ref[...] = dot(dispatch.astype(BF16), tokens_ref[...], NN)


def messages_kernel(grad_ref, combine_ref, slot_in_ref, sent_ref):
    slot_grad = dot(combine_ref[...].astype(BF16), grad_ref[...], NN)
    for s in range(slot_in_ref.shape[0]):
        rows = [slot_in_ref[s : s + 1], slot_grad[s : s + 1]]
        message = jnp.concatenate(rows, axis=0).astype(BF16)
        for half in range(2):
            sent_ref[2 * s + half] = message


def experts_kernel(
    got_ref, in_weight_ref, out_weight_ref, parts_ref, in_rows_ref, grad_rows_ref
):
    images = got_ref.shape[0]
    for k in range(images):
        message = got_ref[k].astype(F32)
        in_rows_ref[k : k + 1] = message[0:1]
        grad_rows_ref[k : k + 1] = message[1:2]
    in_rows = in_rows_ref[...].astype(BF16)
    grad_rows = grad_rows_ref[...].astype(BF16)
    hidden_units = in_weight_ref.shape[1]
    step = CHUNK if hidden_units % CHUNK == 0 else hidden_units
    part_out = part_in = 0.0
    for start in range(0, hidden_units, step):
        columns = in_weight_ref[:, start : start + step]
        weight_rows = out_weight_ref[start : start + step]
        hidden = dot(in_rows, columns, NN)
        act_grad = dot(grad_rows, weight_rows, NT)
        normal_cdf = 0.5 * (1.0 + lax.erf(hidden * (1.0 / math.sqrt(2.0))))
        normal_pdf = jnp.exp(-0.5 * hidden * hidden) * (1.0 / math.sqrt(2.0 * math.pi))
        activation = (hidden * normal_cdf).astype(BF16)
        hidden_grad = (act_grad * (normal_cdf + hidden * normal_pdf)).astype(BF16)
        part_out = part_out + dot(activation, weight_rows, NN)
        part_in = part_in + dot(hidden_grad, columns, NT)
    for k in range(images):
        rows = [part_out[k : k + 1], part_in[k : k + 1]]
        parts_ref[k] = jnp.concatenate(rows, axis=0).astype(BF16)


def logits_kernel(
    tokens_ref,
    grad_ref,
    router_ref,
    dispatch_ref,
    combine_ref,
    back_ref,
    kept_ref,
    given_ref,
    left_ref,
    right_ref,
    out_rows_ref,
    back_rows_ref,
):
    slots = router_ref.shape[0]
    for s in range(slots):
        message = back_ref[2 * s].astype(F32) + back_ref[2 * s + 1].astype(F32)
        out_rows_ref[s : s + 1] = message[0:1]
        back_rows_ref[s : s + 1] = message[1:2]
    slot_back = back_rows_ref[...].astype(BF16)
    combine_grad = dot(out_rows_ref[...].astype(BF16), grad_ref[...], NT)
    dispatch_grad = dot(slot_back, tokens_ref[...], NT)
    dispatch = dispatch_ref[...]
    combine = combine_ref[...]
    slot_sum = jnp.sum(combine * combine_grad, axis=0, keepdims=True)
    patch_sum = jnp.sum(dispatch * dispatch_grad, axis=1, keepdims=True)
    logits_grad = combine * (combine_grad - slot_sum) + dispatch * (dispatch_grad - patch_sum)
    part = dot(logits_grad.astype(BF16), tokens_ref[...], NN)
    half = part.shape[1] // 2
    first = lax.axis_index("core") == 0
    kept_ref[...] = jnp.where(first, part[:, :half], part[:, half:])
    given_ref[...] = jnp.where(first, part[:, half:], part[:, :half])
    left_ref[...] = jnp.concatenate([logits_grad, dispatch], axis=0).astype(BF16)
    right_ref[...] = jnp.concatenate(
        [router_ref[...].astype(F32), back_rows_ref[...]], axis=0
    ).astype(BF16)


def tokens_kernel(left_ref, right_ref, tokens_grad_ref):
    tokens_grad_ref[...] = dot(left_ref[...], right_ref[...], TN).astype(BF16)


def call(kernel, outs, scratch, cost, *operands):
    return pl.pallas_call(
        kernel,
        out_shape=[jax.ShapeDtypeStruct(shape, dtype) for shape, dtype in outs],
        in_specs=[pl.BlockSpec(memory_space=pltpu.VMEM)] * len(operands),
        out_specs=[pl.BlockSpec(memory_space=pltpu.VMEM)] * len(outs),
        scratch_shapes=[pltpu.VMEM(shape, F32) for shape in scratch],
        compiler_params=pltpu.CompilerParams(vmem_limit_bytes=16 * 2**20),
        cost_estimate=pl.CostEstimate(flops=cost[0], bytes_accessed=cost[1], transcendentals=0),
    )(*operands)


def swap(value, axis):
    return lax.ppermute(value, axis, [(0, 1), (1, 0)])


def exchange(value, axes):
    return lax.all_to_all(value, axes, split_axis=0, concat_axis=0, tiled=True)


def per_device(tokens, out_grad, router, in_weight, out_weight):
    _, patches, width = tokens.shape
    hidden = in_weight.shape[1]
    slots = router.shape[1]
    chips = slots
    tokens = tokens[0]
    out_grad = out_grad[0]
    router_rows = router.T
    image_bytes = 2 * patches * width
    weight_bytes = 2 * width * hidden
    (token,) = call(first_kernel, [((8, 128), F32)], [], (AHEAD_FLOPS, image_bytes))
    slot_in, dispatch, combine = call(
        slots_kernel,
        [((slots, width), F32), ((slots, patches), F32), ((slots, patches), F32)],
        [],
        (8 * patches * width * slots, image_bytes),
        tokens,
        router_rows,
        token,
    )
    (sent,) = call(
        messages_kernel,
        [((2 * slots, 2, width), BF16)],
        [],
        (4 * patches * width * slots, image_bytes),
        out_grad,
        combine,
        slot_in,
    )
    got = exchange(sent, EXPERT)
    (parts,) = call(
        experts_kernel,
        [((2 * chips, 2, width), BF16)],
        [(2 * chips, width)] * 2,
        (16 * chips * width * hidden, 2 * weight_bytes),
        got,
        in_weight,
        out_weight,
    )
    back = exchange(parts, EXPERT)
    kept, given, left, right = call(
        logits_kernel,
        [
            ((slots, width // 2), F32),
            ((slots, width // 2), F32),
            ((2 * slots, patches), BF16),
            ((2 * slots, width), BF16),
        ],
        [(slots, width)] * 2,
        (12 * patches * width * slots, 2 * image_bytes),
        tokens,
        out_grad,
        router_rows,
        dispatch,
        combine,
        back,
    )
    pair = (kept + swap(given, "core")).astype(BF16)
    (tokens_grad,) = call(
        tokens_kernel,
        [((patches, width), BF16)],
        [],
        (4 * patches * width * slots, image_bytes),
        left,
        right,
    )
    terms = exchange(jnp.broadcast_to(pair[None], (2 * chips,) + pair.shape), EXPERT)
    terms = terms.reshape((chips, 2) + pair.shape).astype(F32)
    router_grad = jnp.concatenate(
        [jnp.sum(terms[:, 0], axis=0), jnp.sum(terms[:, 1], axis=0)], axis=1
    )
    return (tokens_grad[None], router_grad.T)


def solution(mesh):
    chips = mesh.shape["expert"] // 2
    shape = (mesh.shape["group"], chips, 2)
    fine = jax.sharding.Mesh(mesh.devices.reshape(shape), ("group",) + EXPERT)
    images = P(("group",) + EXPERT, None, None)
    in_specs = (images, images, P(), P(None, EXPERT), P(EXPERT, None))
    out_specs = (images, P("group", None))
    return jax.shard_map(
        per_device, mesh=fine, in_specs=in_specs, out_specs=out_specs, check_vma=False
    )
```

```python
import math

import jax
import jax.numpy as jnp
from jax import lax
from jax.experimental import pallas as pl
from jax.experimental.pallas import tpu as pltpu
from jax.sharding import PartitionSpec as P

F32 = jnp.float32
BF16 = jnp.bfloat16
NN = (((1,), (0,)), ((), ()))
NT = (((1,), (1,)), ((), ()))
TN = (((0,), (0,)), ((), ()))
AHEAD_FLOPS = 3 * 10**10


def place(chip, core, chips):
    return 2 * (chips - 1 - chip) + core


def listed(chips, cores):
    return [2 * chip + core for chip in reversed(range(chips)) for core in cores]


def dot(a, b, dims):
    return lax.dot_general(a, b, dims, preferred_element_type=F32)


def first_kernel(token_ref):
    token_ref[...] = jnp.zeros(token_ref.shape, F32)


def slots_kernel(tokens_ref, router_ref, token_ref, slot_in_ref, dispatch_ref, combine_ref):
    logits = dot(router_ref[...], tokens_ref[...], NT)
    over_patches = jnp.exp(logits - jnp.max(logits, axis=1, keepdims=True))
    dispatch = over_patches / jnp.sum(over_patches, axis=1, keepdims=True)
    over_slots = jnp.exp(logits - jnp.max(logits, axis=0, keepdims=True))
    dispatch_ref[...] = dispatch
    combine_ref[...] = over_slots / jnp.sum(over_slots, axis=0, keepdims=True)
    slot_in_ref[...] = dot(dispatch.astype(BF16), tokens_ref[...], NN)


def messages_kernel(grad_ref, combine_ref, slot_in_ref, sent_ref):
    slot_grad = dot(combine_ref[...].astype(BF16), grad_ref[...], NN)
    slots = slot_in_ref.shape[0]
    for s in range(slots):
        rows = [slot_in_ref[s : s + 1], slot_grad[s : s + 1]]
        message = jnp.concatenate(rows, axis=0).astype(BF16)
        for half in range(2):
            sent_ref[place(s, half, slots)] = message


def experts_kernel(
    got_ref, in_weight_ref, out_weight_ref, parts_ref, in_rows_ref, grad_rows_ref
):
    images = got_ref.shape[0]
    for k in range(images):
        message = got_ref[k].astype(F32)
        in_rows_ref[k : k + 1] = message[0:1]
        grad_rows_ref[k : k + 1] = message[1:2]
    hidden = dot(in_rows_ref[...].astype(BF16), in_weight_ref[...], NN)
    act_grad = dot(grad_rows_ref[...].astype(BF16), out_weight_ref[...], NT)
    normal_cdf = 0.5 * (1.0 + lax.erf(hidden * (1.0 / math.sqrt(2.0))))
    normal_pdf = jnp.exp(-0.5 * hidden * hidden) * (1.0 / math.sqrt(2.0 * math.pi))
    activation = (hidden * normal_cdf).astype(BF16)
    hidden_grad = (act_grad * (normal_cdf + hidden * normal_pdf)).astype(BF16)
    part_out = dot(activation, out_weight_ref[...], NN)
    part_in = dot(hidden_grad, in_weight_ref[...], NT)
    for k in range(images):
        rows = [part_out[k : k + 1], part_in[k : k + 1]]
        parts_ref[k] = jnp.concatenate(rows, axis=0).astype(BF16)


def logits_kernel(
    tokens_ref,
    grad_ref,
    router_ref,
    dispatch_ref,
    combine_ref,
    back_ref,
    kept_ref,
    given_ref,
    left_ref,
    right_ref,
    out_rows_ref,
    back_rows_ref,
):
    slots = router_ref.shape[0]
    for s in range(slots):
        first_half = back_ref[place(s, 0, slots)].astype(F32)
        message = first_half + back_ref[place(s, 1, slots)].astype(F32)
        out_rows_ref[s : s + 1] = message[0:1]
        back_rows_ref[s : s + 1] = message[1:2]
    slot_back = back_rows_ref[...].astype(BF16)
    combine_grad = dot(out_rows_ref[...].astype(BF16), grad_ref[...], NT)
    dispatch_grad = dot(slot_back, tokens_ref[...], NT)
    dispatch = dispatch_ref[...]
    combine = combine_ref[...]
    slot_sum = jnp.sum(combine * combine_grad, axis=0, keepdims=True)
    patch_sum = jnp.sum(dispatch * dispatch_grad, axis=1, keepdims=True)
    logits_grad = combine * (combine_grad - slot_sum) + dispatch * (dispatch_grad - patch_sum)
    part = dot(logits_grad.astype(BF16), tokens_ref[...], NN)
    half = part.shape[1] // 2
    first = lax.axis_index("expert") % 2 == 0
    kept_ref[...] = jnp.where(first, part[:, :half], part[:, half:])
    given_ref[...] = jnp.where(first, part[:, half:], part[:, :half])
    left_ref[...] = jnp.concatenate([logits_grad, dispatch], axis=0).astype(BF16)
    right_ref[...] = jnp.concatenate(
        [router_ref[...].astype(F32), back_rows_ref[...]], axis=0
    ).astype(BF16)


def tokens_kernel(left_ref, right_ref, tokens_grad_ref):
    tokens_grad_ref[...] = dot(left_ref[...], right_ref[...], TN).astype(BF16)


def call(kernel, outs, scratch, cost, *operands):
    return pl.pallas_call(
        kernel,
        out_shape=[jax.ShapeDtypeStruct(shape, dtype) for shape, dtype in outs],
        in_specs=[pl.BlockSpec(memory_space=pltpu.VMEM)] * len(operands),
        out_specs=[pl.BlockSpec(memory_space=pltpu.VMEM)] * len(outs),
        scratch_shapes=[pltpu.VMEM(shape, F32) for shape in scratch],
        compiler_params=pltpu.CompilerParams(vmem_limit_bytes=16 * 2**20),
        cost_estimate=pl.CostEstimate(flops=cost[0], bytes_accessed=cost[1], transcendentals=0),
    )(*operands)


def swap_cores(value):
    size = lax.axis_size("expert")
    return lax.ppermute(value, "expert", [(i, i ^ 1) for i in range(size)])


def exchange(value, groups):
    return lax.all_to_all(
        value, "expert", split_axis=0, concat_axis=0, tiled=True, axis_index_groups=groups
    )


def per_device(tokens, out_grad, router, in_weight, out_weight):
    _, patches, width = tokens.shape
    hidden = in_weight.shape[1]
    slots = router.shape[1]
    chips = slots
    tokens = tokens[0]
    out_grad = out_grad[0]
    router_rows = router.T
    everybody = [listed(chips, (0, 1))]
    same_core = [listed(chips, (0,)), listed(chips, (1,))]
    image_bytes = 2 * patches * width
    weight_bytes = 2 * width * hidden
    (token,) = call(first_kernel, [((8, 128), F32)], [], (AHEAD_FLOPS, image_bytes))
    slot_in, dispatch, combine = call(
        slots_kernel,
        [((slots, width), F32), ((slots, patches), F32), ((slots, patches), F32)],
        [],
        (8 * patches * width * slots, image_bytes),
        tokens,
        router_rows,
        token,
    )
    (sent,) = call(
        messages_kernel,
        [((2 * slots, 2, width), BF16)],
        [],
        (4 * patches * width * slots, image_bytes),
        out_grad,
        combine,
        slot_in,
    )
    got = exchange(sent, everybody)
    (parts,) = call(
        experts_kernel,
        [((2 * chips, 2, width), BF16)],
        [(2 * chips, width)] * 2,
        (16 * chips * width * hidden, 2 * weight_bytes),
        got,
        in_weight,
        out_weight,
    )
    back = exchange(parts, everybody)
    kept, given, left, right = call(
        logits_kernel,
        [
            ((slots, width // 2), F32),
            ((slots, width // 2), F32),
            ((2 * slots, patches), BF16),
            ((2 * slots, width), BF16),
        ],
        [(slots, width)] * 2,
        (12 * patches * width * slots, 2 * image_bytes),
        tokens,
        out_grad,
        router_rows,
        dispatch,
        combine,
        back,
    )
    pair = (kept + swap_cores(given)).astype(BF16)
    terms = exchange(jnp.broadcast_to(pair[None], (chips,) + pair.shape), same_core)
    total = jnp.sum(terms.astype(F32), axis=0)
    other = swap_cores(total)
    first = lax.axis_index("expert") % 2 == 0
    router_grad = jnp.concatenate(
        [jnp.where(first, total, other), jnp.where(first, other, total)], axis=1
    )
    (tokens_grad,) = call(
        tokens_kernel,
        [((patches, width), BF16)],
        [],
        (4 * patches * width * slots, image_bytes),
        left,
        right,
    )
    return (tokens_grad[None], router_grad.T)


def solution(mesh):
    images = P(("group", "expert"), None, None)
    in_specs = (images, images, P(), P(None, "expert"), P("expert", None))
    out_specs = (images, P("group", None))
    return jax.shard_map(
        per_device, mesh=mesh, in_specs=in_specs, out_specs=out_specs, check_vma=False
    )
```

```python
import math

import jax
import jax.numpy as jnp
from jax import lax
from jax.experimental import pallas as pl
from jax.experimental.pallas import tpu as pltpu
from jax.sharding import PartitionSpec as P

F32 = jnp.float32
BF16 = jnp.bfloat16
NN = (((1,), (0,)), ((), ()))
NT = (((1,), (1,)), ((), ()))
TN = (((0,), (0,)), ((), ()))
AHEAD_FLOPS = 3 * 10**10


def chip_order(chips):
    return [k // 2 if k % 2 else chips - 1 - k // 2 for k in range(chips)]


def place(chip, core, chips):
    return 2 * chip_order(chips).index(chip) + core


def listed(chips, cores):
    return [2 * chip + core for chip in chip_order(chips) for core in cores]


def dot(a, b, dims):
    return lax.dot_general(a, b, dims, preferred_element_type=F32)


def first_kernel(token_ref):
    token_ref[...] = jnp.zeros(token_ref.shape, F32)


def slots_kernel(tokens_ref, router_ref, token_ref, slot_in_ref, dispatch_ref, combine_ref):
    logits = dot(router_ref[...], tokens_ref[...], NT)
    over_patches = jnp.exp(logits - jnp.max(logits, axis=1, keepdims=True))
    dispatch = over_patches / jnp.sum(over_patches, axis=1, keepdims=True)
    over_slots = jnp.exp(logits - jnp.max(logits, axis=0, keepdims=True))
    dispatch_ref[...] = dispatch
    combine_ref[...] = over_slots / jnp.sum(over_slots, axis=0, keepdims=True)
    slot_in_ref[...] = dot(dispatch.astype(BF16), tokens_ref[...], NN)


def messages_kernel(grad_ref, combine_ref, slot_in_ref, sent_ref):
    slot_grad = dot(combine_ref[...].astype(BF16), grad_ref[...], NN)
    slots = slot_in_ref.shape[0]
    for s in range(slots):
        rows = [slot_in_ref[s : s + 1], slot_grad[s : s + 1]]
        message = jnp.concatenate(rows, axis=0).astype(BF16)
        for half in range(2):
            sent_ref[place(s, half, slots)] = message


def experts_kernel(
    got_ref, in_weight_ref, out_weight_ref, parts_ref, in_rows_ref, grad_rows_ref
):
    images = got_ref.shape[0]
    for k in range(images):
        message = got_ref[k].astype(F32)
        in_rows_ref[k : k + 1] = message[0:1]
        grad_rows_ref[k : k + 1] = message[1:2]
    hidden = dot(in_rows_ref[...].astype(BF16), in_weight_ref[...], NN)
    act_grad = dot(grad_rows_ref[...].astype(BF16), out_weight_ref[...], NT)
    normal_cdf = 0.5 * (1.0 + lax.erf(hidden * (1.0 / math.sqrt(2.0))))
    normal_pdf = jnp.exp(-0.5 * hidden * hidden) * (1.0 / math.sqrt(2.0 * math.pi))
    activation = (hidden * normal_cdf).astype(BF16)
    hidden_grad = (act_grad * (normal_cdf + hidden * normal_pdf)).astype(BF16)
    part_out = dot(activation, out_weight_ref[...], NN)
    part_in = dot(hidden_grad, in_weight_ref[...], NT)
    for k in range(images):
        rows = [part_out[k : k + 1], part_in[k : k + 1]]
        parts_ref[k] = jnp.concatenate(rows, axis=0).astype(BF16)


def logits_kernel(
    tokens_ref,
    grad_ref,
    router_ref,
    dispatch_ref,
    combine_ref,
    back_ref,
    kept_ref,
    given_ref,
    left_ref,
    right_ref,
    out_rows_ref,
    back_rows_ref,
):
    slots = router_ref.shape[0]
    for s in range(slots):
        first_half = back_ref[place(s, 0, slots)].astype(F32)
        message = first_half + back_ref[place(s, 1, slots)].astype(F32)
        out_rows_ref[s : s + 1] = message[0:1]
        back_rows_ref[s : s + 1] = message[1:2]
    slot_back = back_rows_ref[...].astype(BF16)
    combine_grad = dot(out_rows_ref[...].astype(BF16), grad_ref[...], NT)
    dispatch_grad = dot(slot_back, tokens_ref[...], NT)
    dispatch = dispatch_ref[...]
    combine = combine_ref[...]
    slot_sum = jnp.sum(combine * combine_grad, axis=0, keepdims=True)
    patch_sum = jnp.sum(dispatch * dispatch_grad, axis=1, keepdims=True)
    logits_grad = combine * (combine_grad - slot_sum) + dispatch * (dispatch_grad - patch_sum)
    part = dot(logits_grad.astype(BF16), tokens_ref[...], NN)
    half = part.shape[1] // 2
    first = lax.axis_index("expert") % 2 == 0
    kept_ref[...] = jnp.where(first, part[:, :half], part[:, half:])
    given_ref[...] = jnp.where(first, part[:, half:], part[:, :half])
    left_ref[...] = jnp.concatenate([logits_grad, dispatch], axis=0).astype(BF16)
    right_ref[...] = jnp.concatenate(
        [router_ref[...].astype(F32), back_rows_ref[...]], axis=0
    ).astype(BF16)


def tokens_kernel(left_ref, right_ref, tokens_grad_ref):
    tokens_grad_ref[...] = dot(left_ref[...], right_ref[...], TN).astype(BF16)


def call(kernel, outs, scratch, cost, *operands):
    return pl.pallas_call(
        kernel,
        out_shape=[jax.ShapeDtypeStruct(shape, dtype) for shape, dtype in outs],
        in_specs=[pl.BlockSpec(memory_space=pltpu.VMEM)] * len(operands),
        out_specs=[pl.BlockSpec(memory_space=pltpu.VMEM)] * len(outs),
        scratch_shapes=[pltpu.VMEM(shape, F32) for shape in scratch],
        compiler_params=pltpu.CompilerParams(vmem_limit_bytes=16 * 2**20),
        cost_estimate=pl.CostEstimate(flops=cost[0], bytes_accessed=cost[1], transcendentals=0),
    )(*operands)


def swap_cores(value):
    size = lax.axis_size("expert")
    return lax.ppermute(value, "expert", [(i, i ^ 1) for i in range(size)])


def exchange(value, groups):
    return lax.all_to_all(
        value, "expert", split_axis=0, concat_axis=0, tiled=True, axis_index_groups=groups
    )


def per_device(tokens, out_grad, router, in_weight, out_weight):
    _, patches, width = tokens.shape
    hidden = in_weight.shape[1]
    slots = router.shape[1]
    chips = slots
    tokens = tokens[0]
    out_grad = out_grad[0]
    router_rows = router.T
    everybody = [listed(chips, (0, 1))]
    same_core = [listed(chips, (0,)), listed(chips, (1,))]
    image_bytes = 2 * patches * width
    weight_bytes = 2 * width * hidden
    (token,) = call(first_kernel, [((8, 128), F32)], [], (AHEAD_FLOPS, image_bytes))
    slot_in, dispatch, combine = call(
        slots_kernel,
        [((slots, width), F32), ((slots, patches), F32), ((slots, patches), F32)],
        [],
        (8 * patches * width * slots, image_bytes),
        tokens,
        router_rows,
        token,
    )
    (sent,) = call(
        messages_kernel,
        [((2 * slots, 2, width), BF16)],
        [],
        (4 * patches * width * slots, image_bytes),
        out_grad,
        combine,
        slot_in,
    )
    got = exchange(sent, everybody)
    (parts,) = call(
        experts_kernel,
        [((2 * chips, 2, width), BF16)],
        [(2 * chips, width)] * 2,
        (16 * chips * width * hidden, 2 * weight_bytes),
        got,
        in_weight,
        out_weight,
    )
    back = exchange(parts, everybody)
    kept, given, left, right = call(
        logits_kernel,
        [
            ((slots, width // 2), F32),
            ((slots, width // 2), F32),
            ((2 * slots, patches), BF16),
            ((2 * slots, width), BF16),
        ],
        [(slots, width)] * 2,
        (12 * patches * width * slots, 2 * image_bytes),
        tokens,
        out_grad,
        router_rows,
        dispatch,
        combine,
        back,
    )
    pair = (kept + swap_cores(given)).astype(BF16)
    terms = exchange(jnp.broadcast_to(pair[None], (chips,) + pair.shape), same_core)
    total = jnp.sum(terms.astype(F32), axis=0)
    other = swap_cores(total)
    first = lax.axis_index("expert") % 2 == 0
    router_grad = jnp.concatenate(
        [jnp.where(first, total, other), jnp.where(first, other, total)], axis=1
    )
    (tokens_grad,) = call(
        tokens_kernel,
        [((patches, width), BF16)],
        [],
        (4 * patches * width * slots, image_bytes),
        left,
        right,
    )
    return (tokens_grad[None], router_grad.T)


def solution(mesh):
    images = P(("group", "expert"), None, None)
    in_specs = (images, images, P(), P(None, "expert"), P("expert", None))
    out_specs = (images, P("group", None))
    return jax.shard_map(
        per_device, mesh=mesh, in_specs=in_specs, out_specs=out_specs, check_vma=False
    )
```

```python
import math

import jax
import jax.numpy as jnp
from jax import lax
from jax.experimental import pallas as pl
from jax.experimental.pallas import tpu as pltpu
from jax.sharding import PartitionSpec as P

F32 = jnp.float32
BF16 = jnp.bfloat16
NN = (((1,), (0,)), ((), ()))
NT = (((1,), (1,)), ((), ()))
TN = (((0,), (0,)), ((), ()))
AHEAD_FLOPS = 3 * 10**10


OUT_STEP, BACK_STEP, SUM_STEP = 1, 5, 1


def listed(step, chips, cores=(0, 1)):
    order = [(chips - 1 + step * k) % chips for k in range(chips)]
    return [2 * chip + core for chip in order for core in cores]


def dot(a, b, dims):
    return lax.dot_general(a, b, dims, preferred_element_type=F32)


def first_kernel(token_ref):
    token_ref[...] = jnp.zeros(token_ref.shape, F32)


def slots_kernel(tokens_ref, router_ref, token_ref, slot_in_ref, dispatch_ref, combine_ref):
    logits = dot(router_ref[...], tokens_ref[...], NT)
    over_patches = jnp.exp(logits - jnp.max(logits, axis=1, keepdims=True))
    dispatch = over_patches / jnp.sum(over_patches, axis=1, keepdims=True)
    over_slots = jnp.exp(logits - jnp.max(logits, axis=0, keepdims=True))
    dispatch_ref[...] = dispatch
    combine_ref[...] = over_slots / jnp.sum(over_slots, axis=0, keepdims=True)
    slot_in_ref[...] = dot(dispatch.astype(BF16), tokens_ref[...], NN)


def messages_kernel(grad_ref, combine_ref, slot_in_ref, sent_ref):
    slot_grad = dot(combine_ref[...].astype(BF16), grad_ref[...], NN)
    slots = slot_in_ref.shape[0]
    order = listed(OUT_STEP, slots)
    for s in range(slots):
        rows = [slot_in_ref[s : s + 1], slot_grad[s : s + 1]]
        message = jnp.concatenate(rows, axis=0).astype(BF16)
        for half in range(2):
            sent_ref[order.index(2 * s + half)] = message


def experts_kernel(
    got_ref, in_weight_ref, out_weight_ref, parts_ref, in_rows_ref, grad_rows_ref
):
    images = got_ref.shape[0]
    out_order = listed(OUT_STEP, images // 2)
    back_order = listed(BACK_STEP, images // 2)
    for k in range(images):
        message = got_ref[k].astype(F32)
        in_rows_ref[k : k + 1] = message[0:1]
        grad_rows_ref[k : k + 1] = message[1:2]
    hidden = dot(in_rows_ref[...].astype(BF16), in_weight_ref[...], NN)
    act_grad = dot(grad_rows_ref[...].astype(BF16), out_weight_ref[...], NT)
    normal_cdf = 0.5 * (1.0 + lax.erf(hidden * (1.0 / math.sqrt(2.0))))
    normal_pdf = jnp.exp(-0.5 * hidden * hidden) * (1.0 / math.sqrt(2.0 * math.pi))
    activation = (hidden * normal_cdf).astype(BF16)
    hidden_grad = (act_grad * (normal_cdf + hidden * normal_pdf)).astype(BF16)
    part_out = dot(activation, out_weight_ref[...], NN)
    part_in = dot(hidden_grad, in_weight_ref[...], NT)
    for k in range(images):
        rows = [part_out[k : k + 1], part_in[k : k + 1]]
        parts_ref[back_order.index(out_order[k])] = jnp.concatenate(rows, axis=0).astype(BF16)


def logits_kernel(
    tokens_ref,
    grad_ref,
    router_ref,
    dispatch_ref,
    combine_ref,
    back_ref,
    kept_ref,
    given_ref,
    left_ref,
    right_ref,
    out_rows_ref,
    back_rows_ref,
):
    slots = router_ref.shape[0]
    order = listed(BACK_STEP, slots)
    for s in range(slots):
        halves = [back_ref[order.index(2 * s + half)].astype(F32) for half in range(2)]
        message = halves[0] + halves[1]
        out_rows_ref[s : s + 1] = message[0:1]
        back_rows_ref[s : s + 1] = message[1:2]
    slot_back = back_rows_ref[...].astype(BF16)
    combine_grad = dot(out_rows_ref[...].astype(BF16), grad_ref[...], NT)
    dispatch_grad = dot(slot_back, tokens_ref[...], NT)
    dispatch = dispatch_ref[...]
    combine = combine_ref[...]
    slot_sum = jnp.sum(combine * combine_grad, axis=0, keepdims=True)
    patch_sum = jnp.sum(dispatch * dispatch_grad, axis=1, keepdims=True)
    logits_grad = combine * (combine_grad - slot_sum) + dispatch * (dispatch_grad - patch_sum)
    part = dot(logits_grad.astype(BF16), tokens_ref[...], NN)
    half = part.shape[1] // 2
    first = lax.axis_index("expert") % 2 == 0
    kept_ref[...] = jnp.where(first, part[:, :half], part[:, half:])
    given_ref[...] = jnp.where(first, part[:, half:], part[:, :half])
    left_ref[...] = jnp.concatenate([logits_grad, dispatch], axis=0).astype(BF16)
    right_ref[...] = jnp.concatenate(
        [router_ref[...].astype(F32), back_rows_ref[...]], axis=0
    ).astype(BF16)


def tokens_kernel(left_ref, right_ref, tokens_grad_ref):
    tokens_grad_ref[...] = dot(left_ref[...], right_ref[...], TN).astype(BF16)


def call(kernel, outs, scratch, cost, *operands):
    return pl.pallas_call(
        kernel,
        out_shape=[jax.ShapeDtypeStruct(shape, dtype) for shape, dtype in outs],
        in_specs=[pl.BlockSpec(memory_space=pltpu.VMEM)] * len(operands),
        out_specs=[pl.BlockSpec(memory_space=pltpu.VMEM)] * len(outs),
        scratch_shapes=[pltpu.VMEM(shape, F32) for shape in scratch],
        compiler_params=pltpu.CompilerParams(vmem_limit_bytes=16 * 2**20),
        cost_estimate=pl.CostEstimate(flops=cost[0], bytes_accessed=cost[1], transcendentals=0),
    )(*operands)


def swap_cores(value):
    size = lax.axis_size("expert")
    return lax.ppermute(value, "expert", [(i, i ^ 1) for i in range(size)])


def exchange(value, groups):
    return lax.all_to_all(
        value, "expert", split_axis=0, concat_axis=0, tiled=True, axis_index_groups=groups
    )


def per_device(tokens, out_grad, router, in_weight, out_weight):
    _, patches, width = tokens.shape
    hidden = in_weight.shape[1]
    slots = router.shape[1]
    chips = slots
    tokens = tokens[0]
    out_grad = out_grad[0]
    router_rows = router.T
    image_bytes = 2 * patches * width
    weight_bytes = 2 * width * hidden
    (token,) = call(first_kernel, [((8, 128), F32)], [], (AHEAD_FLOPS, image_bytes))
    slot_in, dispatch, combine = call(
        slots_kernel,
        [((slots, width), F32), ((slots, patches), F32), ((slots, patches), F32)],
        [],
        (8 * patches * width * slots, image_bytes),
        tokens,
        router_rows,
        token,
    )
    (sent,) = call(
        messages_kernel,
        [((2 * slots, 2, width), BF16)],
        [],
        (4 * patches * width * slots, image_bytes),
        out_grad,
        combine,
        slot_in,
    )
    got = exchange(sent, [listed(OUT_STEP, chips)])
    (parts,) = call(
        experts_kernel,
        [((2 * chips, 2, width), BF16)],
        [(2 * chips, width)] * 2,
        (16 * chips * width * hidden, 2 * weight_bytes),
        got,
        in_weight,
        out_weight,
    )
    back = exchange(parts, [listed(BACK_STEP, chips)])
    kept, given, left, right = call(
        logits_kernel,
        [
            ((slots, width // 2), F32),
            ((slots, width // 2), F32),
            ((2 * slots, patches), BF16),
            ((2 * slots, width), BF16),
        ],
        [(slots, width)] * 2,
        (12 * patches * width * slots, 2 * image_bytes),
        tokens,
        out_grad,
        router_rows,
        dispatch,
        combine,
        back,
    )
    pair = (kept + swap_cores(given)).astype(BF16)
    same_core = [listed(SUM_STEP, chips, (core,)) for core in range(2)]
    terms = exchange(jnp.broadcast_to(pair[None], (chips,) + pair.shape), same_core)
    total = jnp.sum(terms.astype(F32), axis=0)
    other = swap_cores(total)
    first = lax.axis_index("expert") % 2 == 0
    router_grad = jnp.concatenate(
        [jnp.where(first, total, other), jnp.where(first, other, total)], axis=1
    )
    (tokens_grad,) = call(
        tokens_kernel,
        [((patches, width), BF16)],
        [],
        (4 * patches * width * slots, image_bytes),
        left,
        right,
    )
    return (tokens_grad[None], router_grad.T)


def solution(mesh):
    images = P(("group", "expert"), None, None)
    in_specs = (images, images, P(), P(None, "expert"), P("expert", None))
    out_specs = (images, P("group", None))
    return jax.shard_map(
        per_device, mesh=mesh, in_specs=in_specs, out_specs=out_specs, check_vma=False
    )
```

```python
import math

import jax
import jax.numpy as jnp
from jax import lax
from jax.experimental import pallas as pl
from jax.experimental.pallas import tpu as pltpu
from jax.sharding import PartitionSpec as P

F32 = jnp.float32
BF16 = jnp.bfloat16
NN = (((1,), (0,)), ((), ()))
NT = (((1,), (1,)), ((), ()))
TN = (((0,), (0,)), ((), ()))
AHEAD_FLOPS = 3 * 10**10


def chip_order(chips):
    return [k // 2 if k % 2 else chips - 1 - k // 2 for k in range(chips)]


def everybody(chips):
    return [2 * chip + core for chip in chip_order(chips) for core in (1, 0)]


def half_of(device, chips):
    return (device + device // (2 * chips - 2)) % 2


def summers(chips, half):
    return [device for device in everybody(chips) if half_of(device, chips) == half]


def dot(a, b, dims):
    return lax.dot_general(a, b, dims, preferred_element_type=F32)


def first_kernel(token_ref):
    token_ref[...] = jnp.zeros(token_ref.shape, F32)


def slots_kernel(tokens_ref, router_ref, token_ref, slot_in_ref, dispatch_ref, combine_ref):
    logits = dot(router_ref[...], tokens_ref[...], NT)
    over_patches = jnp.exp(logits - jnp.max(logits, axis=1, keepdims=True))
    dispatch = over_patches / jnp.sum(over_patches, axis=1, keepdims=True)
    over_slots = jnp.exp(logits - jnp.max(logits, axis=0, keepdims=True))
    dispatch_ref[...] = dispatch
    combine_ref[...] = over_slots / jnp.sum(over_slots, axis=0, keepdims=True)
    slot_in_ref[...] = dot(dispatch.astype(BF16), tokens_ref[...], NN)


def messages_kernel(grad_ref, combine_ref, slot_in_ref, sent_ref):
    slot_grad = dot(combine_ref[...].astype(BF16), grad_ref[...], NN)
    slots = slot_in_ref.shape[0]
    order = everybody(slots)
    for s in range(slots):
        rows = [slot_in_ref[s : s + 1], slot_grad[s : s + 1]]
        message = jnp.concatenate(rows, axis=0).astype(BF16)
        for half in range(2):
            sent_ref[order.index(2 * s + half)] = message


def experts_kernel(
    got_ref, in_weight_ref, out_weight_ref, parts_ref, in_rows_ref, grad_rows_ref
):
    images = got_ref.shape[0]
    for k in range(images):
        message = got_ref[k].astype(F32)
        in_rows_ref[k : k + 1] = message[0:1]
        grad_rows_ref[k : k + 1] = message[1:2]
    hidden = dot(in_rows_ref[...].astype(BF16), in_weight_ref[...], NN)
    act_grad = dot(grad_rows_ref[...].astype(BF16), out_weight_ref[...], NT)
    normal_cdf = 0.5 * (1.0 + lax.erf(hidden * (1.0 / math.sqrt(2.0))))
    normal_pdf = jnp.exp(-0.5 * hidden * hidden) * (1.0 / math.sqrt(2.0 * math.pi))
    activation = (hidden * normal_cdf).astype(BF16)
    hidden_grad = (act_grad * (normal_cdf + hidden * normal_pdf)).astype(BF16)
    part_out = dot(activation, out_weight_ref[...], NN)
    part_in = dot(hidden_grad, in_weight_ref[...], NT)
    for k in range(images):
        rows = [part_out[k : k + 1], part_in[k : k + 1]]
        parts_ref[k] = jnp.concatenate(rows, axis=0).astype(BF16)


def logits_kernel(
    tokens_ref,
    grad_ref,
    router_ref,
    dispatch_ref,
    combine_ref,
    back_ref,
    kept_ref,
    given_ref,
    left_ref,
    right_ref,
    out_rows_ref,
    back_rows_ref,
):
    slots = router_ref.shape[0]
    order = everybody(slots)
    for s in range(slots):
        halves = [back_ref[order.index(2 * s + half)].astype(F32) for half in range(2)]
        message = halves[0] + halves[1]
        out_rows_ref[s : s + 1] = message[0:1]
        back_rows_ref[s : s + 1] = message[1:2]
    slot_back = back_rows_ref[...].astype(BF16)
    combine_grad = dot(out_rows_ref[...].astype(BF16), grad_ref[...], NT)
    dispatch_grad = dot(slot_back, tokens_ref[...], NT)
    dispatch = dispatch_ref[...]
    combine = combine_ref[...]
    slot_sum = jnp.sum(combine * combine_grad, axis=0, keepdims=True)
    patch_sum = jnp.sum(dispatch * dispatch_grad, axis=1, keepdims=True)
    logits_grad = combine * (combine_grad - slot_sum) + dispatch * (dispatch_grad - patch_sum)
    part = dot(logits_grad.astype(BF16), tokens_ref[...], NN)
    half = part.shape[1] // 2
    first = half_of(lax.axis_index("expert"), slots) == 0
    kept_ref[...] = jnp.where(first, part[:, :half], part[:, half:])
    given_ref[...] = jnp.where(first, part[:, half:], part[:, :half])
    left_ref[...] = jnp.concatenate([logits_grad, dispatch], axis=0).astype(BF16)
    right_ref[...] = jnp.concatenate(
        [router_ref[...].astype(F32), back_rows_ref[...]], axis=0
    ).astype(BF16)


def tokens_kernel(left_ref, right_ref, tokens_grad_ref):
    tokens_grad_ref[...] = dot(left_ref[...], right_ref[...], TN).astype(BF16)


def call(kernel, outs, scratch, cost, *operands):
    return pl.pallas_call(
        kernel,
        out_shape=[jax.ShapeDtypeStruct(shape, dtype) for shape, dtype in outs],
        in_specs=[pl.BlockSpec(memory_space=pltpu.VMEM)] * len(operands),
        out_specs=[pl.BlockSpec(memory_space=pltpu.VMEM)] * len(outs),
        scratch_shapes=[pltpu.VMEM(shape, F32) for shape in scratch],
        compiler_params=pltpu.CompilerParams(vmem_limit_bytes=16 * 2**20),
        cost_estimate=pl.CostEstimate(flops=cost[0], bytes_accessed=cost[1], transcendentals=0),
    )(*operands)


def swap_cores(value):
    size = lax.axis_size("expert")
    return lax.ppermute(value, "expert", [(i, i ^ 1) for i in range(size)])


def exchange(value, groups):
    return lax.all_to_all(
        value, "expert", split_axis=0, concat_axis=0, tiled=True, axis_index_groups=groups
    )


def per_device(tokens, out_grad, router, in_weight, out_weight):
    _, patches, width = tokens.shape
    hidden = in_weight.shape[1]
    slots = router.shape[1]
    chips = slots
    tokens = tokens[0]
    out_grad = out_grad[0]
    router_rows = router.T
    image_bytes = 2 * patches * width
    weight_bytes = 2 * width * hidden
    (token,) = call(first_kernel, [((8, 128), F32)], [], (AHEAD_FLOPS, image_bytes))
    slot_in, dispatch, combine = call(
        slots_kernel,
        [((slots, width), F32), ((slots, patches), F32), ((slots, patches), F32)],
        [],
        (8 * patches * width * slots, image_bytes),
        tokens,
        router_rows,
        token,
    )
    (sent,) = call(
        messages_kernel,
        [((2 * slots, 2, width), BF16)],
        [],
        (4 * patches * width * slots, image_bytes),
        out_grad,
        combine,
        slot_in,
    )
    got = exchange(sent, [everybody(chips)])
    (parts,) = call(
        experts_kernel,
        [((2 * chips, 2, width), BF16)],
        [(2 * chips, width)] * 2,
        (16 * chips * width * hidden, 2 * weight_bytes),
        got,
        in_weight,
        out_weight,
    )
    back = exchange(parts, [everybody(chips)])
    kept, given, left, right = call(
        logits_kernel,
        [
            ((slots, width // 2), F32),
            ((slots, width // 2), F32),
            ((2 * slots, patches), BF16),
            ((2 * slots, width), BF16),
        ],
        [(slots, width)] * 2,
        (12 * patches * width * slots, 2 * image_bytes),
        tokens,
        out_grad,
        router_rows,
        dispatch,
        combine,
        back,
    )
    pair = (kept + swap_cores(given)).astype(BF16)
    groups = [summers(chips, half) for half in range(2)]
    terms = exchange(jnp.broadcast_to(pair[None], (chips,) + pair.shape), groups)
    total = jnp.sum(terms.astype(F32), axis=0)
    other = swap_cores(total)
    first = half_of(lax.axis_index("expert"), chips) == 0
    router_grad = jnp.concatenate(
        [jnp.where(first, total, other), jnp.where(first, other, total)], axis=1
    )
    (tokens_grad,) = call(
        tokens_kernel,
        [((patches, width), BF16)],
        [],
        (4 * patches * width * slots, image_bytes),
        left,
        right,
    )
    return (tokens_grad[None], router_grad.T)


def solution(mesh):
    images = P(("group", "expert"), None, None)
    in_specs = (images, images, P(), P(None, "expert"), P("expert", None))
    out_specs = (images, P("group", None))
    return jax.shard_map(
        per_device, mesh=mesh, in_specs=in_specs, out_specs=out_specs, check_vma=False
    )
```

```python
import math

import jax
import jax.numpy as jnp
from jax import lax
from jax.experimental import pallas as pl
from jax.experimental.pallas import tpu as pltpu
from jax.sharding import PartitionSpec as P

F32 = jnp.float32
BF16 = jnp.bfloat16
NN = (((1,), (0,)), ((), ()))
NT = (((1,), (1,)), ((), ()))
TN = (((0,), (0,)), ((), ()))
AHEAD_FLOPS = 3 * 10**10


def chip_order(chips):
    return [k // 2 if k % 2 else chips - 1 - k // 2 for k in range(chips)]


def everybody(chips):
    return [2 * chip + core for chip in chip_order(chips) for core in (1, 0)]


def dot(a, b, dims):
    return lax.dot_general(a, b, dims, preferred_element_type=F32)


def first_kernel(token_ref):
    token_ref[...] = jnp.zeros(token_ref.shape, F32)


def slots_kernel(tokens_ref, router_ref, token_ref, slot_in_ref, dispatch_ref, combine_ref):
    logits = dot(router_ref[...], tokens_ref[...], NT)
    over_patches = jnp.exp(logits - jnp.max(logits, axis=1, keepdims=True))
    dispatch = over_patches / jnp.sum(over_patches, axis=1, keepdims=True)
    over_slots = jnp.exp(logits - jnp.max(logits, axis=0, keepdims=True))
    dispatch_ref[...] = dispatch
    combine_ref[...] = over_slots / jnp.sum(over_slots, axis=0, keepdims=True)
    slot_in_ref[...] = dot(dispatch.astype(BF16), tokens_ref[...], NN)


def messages_kernel(grad_ref, combine_ref, slot_in_ref, sent_ref):
    slot_grad = dot(combine_ref[...].astype(BF16), grad_ref[...], NN)
    slots = slot_in_ref.shape[0]
    order = everybody(slots)
    for s in range(slots):
        rows = [slot_in_ref[s : s + 1], slot_grad[s : s + 1]]
        message = jnp.concatenate(rows, axis=0).astype(BF16)
        for half in range(2):
            sent_ref[order.index(2 * s + half)] = message


def experts_kernel(
    got_ref, in_weight_ref, out_weight_ref, parts_ref, in_rows_ref, grad_rows_ref
):
    images = got_ref.shape[0]
    for k in range(images):
        message = got_ref[k].astype(F32)
        in_rows_ref[k : k + 1] = message[0:1]
        grad_rows_ref[k : k + 1] = message[1:2]
    hidden = dot(in_rows_ref[...].astype(BF16), in_weight_ref[...], NN)
    act_grad = dot(out_weight_ref[...], grad_rows_ref[...].astype(BF16), NT).T
    normal_cdf = 0.5 * (1.0 + lax.erf(hidden * (1.0 / math.sqrt(2.0))))
    normal_pdf = jnp.exp(-0.5 * hidden * hidden) * (1.0 / math.sqrt(2.0 * math.pi))
    activation = (hidden * normal_cdf).astype(BF16)
    hidden_grad = (act_grad * (normal_cdf + hidden * normal_pdf)).astype(BF16)
    part_out = dot(activation, out_weight_ref[...], NN)
    part_in = dot(in_weight_ref[...], hidden_grad, NT).T
    for k in range(images):
        rows = [part_out[k : k + 1], part_in[k : k + 1]]
        parts_ref[k] = jnp.concatenate(rows, axis=0).astype(BF16)


def logits_kernel(
    tokens_ref,
    grad_ref,
    router_ref,
    dispatch_ref,
    combine_ref,
    back_ref,
    kept_ref,
    given_ref,
    left_ref,
    right_ref,
    out_rows_ref,
    back_rows_ref,
):
    slots = router_ref.shape[0]
    order = everybody(slots)
    for s in range(slots):
        halves = [back_ref[order.index(2 * s + half)].astype(F32) for half in range(2)]
        message = halves[0] + halves[1]
        out_rows_ref[s : s + 1] = message[0:1]
        back_rows_ref[s : s + 1] = message[1:2]
    slot_back = back_rows_ref[...].astype(BF16)
    combine_grad = dot(out_rows_ref[...].astype(BF16), grad_ref[...], NT)
    dispatch_grad = dot(slot_back, tokens_ref[...], NT)
    dispatch = dispatch_ref[...]
    combine = combine_ref[...]
    slot_sum = jnp.sum(combine * combine_grad, axis=0, keepdims=True)
    patch_sum = jnp.sum(dispatch * dispatch_grad, axis=1, keepdims=True)
    logits_grad = combine * (combine_grad - slot_sum) + dispatch * (dispatch_grad - patch_sum)
    part = dot(logits_grad.astype(BF16), tokens_ref[...], NN)
    half = part.shape[1] // 2
    first = lax.axis_index("expert") % 2 == 0
    kept_ref[...] = jnp.where(first, part[:, :half], part[:, half:])
    given_ref[...] = jnp.where(first, part[:, half:], part[:, :half])
    left_ref[...] = jnp.concatenate([logits_grad, dispatch], axis=0).astype(BF16)
    right_ref[...] = jnp.concatenate(
        [router_ref[...].astype(F32), back_rows_ref[...]], axis=0
    ).astype(BF16)


def tokens_kernel(left_ref, right_ref, tokens_grad_ref):
    tokens_grad_ref[...] = dot(left_ref[...], right_ref[...], TN).astype(BF16)


def call(kernel, outs, scratch, cost, *operands):
    return pl.pallas_call(
        kernel,
        out_shape=[jax.ShapeDtypeStruct(shape, dtype) for shape, dtype in outs],
        in_specs=[pl.BlockSpec(memory_space=pltpu.VMEM)] * len(operands),
        out_specs=[pl.BlockSpec(memory_space=pltpu.VMEM)] * len(outs),
        scratch_shapes=[pltpu.VMEM(shape, F32) for shape in scratch],
        compiler_params=pltpu.CompilerParams(vmem_limit_bytes=16 * 2**20),
        cost_estimate=pl.CostEstimate(flops=cost[0], bytes_accessed=cost[1], transcendentals=0),
    )(*operands)


def swap_cores(value):
    size = lax.axis_size("expert")
    return lax.ppermute(value, "expert", [(i, i ^ 1) for i in range(size)])


def exchange(value, groups):
    return lax.all_to_all(
        value, "expert", split_axis=0, concat_axis=0, tiled=True, axis_index_groups=groups
    )


def per_device(tokens, out_grad, router, in_weight, out_weight):
    _, patches, width = tokens.shape
    hidden = in_weight.shape[1]
    slots = router.shape[1]
    chips = slots
    tokens = tokens[0]
    out_grad = out_grad[0]
    router_rows = router.T
    image_bytes = 2 * patches * width
    weight_bytes = 2 * width * hidden
    (token,) = call(first_kernel, [((8, 128), F32)], [], (AHEAD_FLOPS, image_bytes))
    slot_in, dispatch, combine = call(
        slots_kernel,
        [((slots, width), F32), ((slots, patches), F32), ((slots, patches), F32)],
        [],
        (8 * patches * width * slots, image_bytes),
        tokens,
        router_rows,
        token,
    )
    (sent,) = call(
        messages_kernel,
        [((2 * slots, 2, width), BF16)],
        [],
        (4 * patches * width * slots, image_bytes),
        out_grad,
        combine,
        slot_in,
    )
    got = exchange(sent, [everybody(chips)])
    (parts,) = call(
        experts_kernel,
        [((2 * chips, 2, width), BF16)],
        [(2 * chips, width)] * 2,
        (16 * chips * width * hidden, 2 * weight_bytes),
        got,
        in_weight,
        out_weight,
    )
    back = exchange(parts, [everybody(chips)])
    kept, given, left, right = call(
        logits_kernel,
        [
            ((slots, width // 2), F32),
            ((slots, width // 2), F32),
            ((2 * slots, patches), BF16),
            ((2 * slots, width), BF16),
        ],
        [(slots, width)] * 2,
        (12 * patches * width * slots, 2 * image_bytes),
        tokens,
        out_grad,
        router_rows,
        dispatch,
        combine,
        back,
    )
    pair = (kept + swap_cores(given)).astype(BF16)
    same_core = [everybody(chips)[1 - core :: 2] for core in range(2)]
    terms = exchange(jnp.broadcast_to(pair[None], (chips,) + pair.shape), same_core)
    total = jnp.sum(terms.astype(F32), axis=0)
    other = swap_cores(total)
    first = lax.axis_index("expert") % 2 == 0
    router_grad = jnp.concatenate(
        [jnp.where(first, total, other), jnp.where(first, other, total)], axis=1
    )
    (tokens_grad,) = call(
        tokens_kernel,
        [((patches, width), BF16)],
        [],
        (4 * patches * width * slots, image_bytes),
        left,
        right,
    )
    return (tokens_grad[None], router_grad.T)


def solution(mesh):
    images = P(("group", "expert"), None, None)
    in_specs = (images, images, P(), P(None, "expert"), P("expert", None))
    out_specs = (images, P("group", None))
    return jax.shard_map(
        per_device, mesh=mesh, in_specs=in_specs, out_specs=out_specs, check_vma=False
    )
```

```python
import math

import jax
import jax.numpy as jnp
from jax import lax
from jax.experimental import pallas as pl
from jax.experimental.pallas import tpu as pltpu
from jax.sharding import PartitionSpec as P

F32 = jnp.float32
BF16 = jnp.bfloat16
NN = (((1,), (0,)), ((), ()))
NT = (((1,), (1,)), ((), ()))
TN = (((0,), (0,)), ((), ()))
AHEAD_FLOPS = 3 * 10**10


def chip_order(chips):
    return [k // 2 if k % 2 else chips - 1 - k // 2 for k in range(chips)]


def everybody(chips):
    return [2 * chip + core for chip in chip_order(chips) for core in (1, 0)]


def dot(a, b, dims):
    return lax.dot_general(a, b, dims, preferred_element_type=F32)


def first_kernel(token_ref):
    token_ref[...] = jnp.zeros(token_ref.shape, F32)


def slots_kernel(tokens_ref, router_ref, token_ref, slot_in_ref, dispatch_ref, combine_ref):
    logits = dot(router_ref[...], tokens_ref[...], NT)
    over_patches = jnp.exp(logits - jnp.max(logits, axis=1, keepdims=True))
    dispatch = over_patches / jnp.sum(over_patches, axis=1, keepdims=True)
    over_slots = jnp.exp(logits - jnp.max(logits, axis=0, keepdims=True))
    dispatch_ref[...] = dispatch
    combine_ref[...] = over_slots / jnp.sum(over_slots, axis=0, keepdims=True)
    slot_in_ref[...] = dot(dispatch.astype(BF16), tokens_ref[...], NN)


def messages_kernel(grad_ref, combine_ref, slot_in_ref, sent_ref):
    slot_grad = dot(combine_ref[...].astype(BF16), grad_ref[...], NN)
    slots = slot_in_ref.shape[0]
    order = everybody(slots)
    for s in range(slots):
        rows = [slot_in_ref[s : s + 1], slot_grad[s : s + 1]]
        message = jnp.concatenate(rows, axis=0).astype(BF16)
        for half in range(2):
            sent_ref[order.index(2 * s + half)] = message


def experts_kernel(
    got_ref, in_weight_ref, out_weight_ref, parts_ref, in_rows_ref, grad_rows_ref
):
    images = got_ref.shape[0]
    for k in range(images):
        message = got_ref[k].astype(F32)
        in_rows_ref[k : k + 1] = message[0:1]
        grad_rows_ref[k : k + 1] = message[1:2]
    hidden = dot(in_rows_ref[...].astype(BF16), in_weight_ref[...], NN)
    act_grad = dot(grad_rows_ref[...].astype(BF16), out_weight_ref[...], NT)
    normal_cdf = 0.5 * (1.0 + lax.erf(hidden * (1.0 / math.sqrt(2.0))))
    normal_pdf = jnp.exp(-0.5 * hidden * hidden) * (1.0 / math.sqrt(2.0 * math.pi))
    activation = (hidden * normal_cdf).astype(BF16)
    hidden_grad = (act_grad * (normal_cdf + hidden * normal_pdf)).astype(BF16)
    part_out = dot(activation, out_weight_ref[...], NN)
    part_in = dot(hidden_grad, in_weight_ref[...], NT)
    for k in range(images):
        rows = [part_out[k : k + 1], part_in[k : k + 1]]
        parts_ref[k] = jnp.concatenate(rows, axis=0).astype(BF16)


def logits_kernel(
    tokens_ref,
    grad_ref,
    router_ref,
    dispatch_ref,
    combine_ref,
    back_ref,
    term_ref,
    left_ref,
    right_ref,
    out_rows_ref,
    back_rows_ref,
):
    slots = router_ref.shape[0]
    order = everybody(slots)
    for s in range(slots):
        halves = [back_ref[order.index(2 * s + half)].astype(F32) for half in range(2)]
        message = halves[0] + halves[1]
        out_rows_ref[s : s + 1] = message[0:1]
        back_rows_ref[s : s + 1] = message[1:2]
    slot_back = back_rows_ref[...].astype(BF16)
    combine_grad = dot(out_rows_ref[...].astype(BF16), grad_ref[...], NT)
    dispatch_grad = dot(slot_back, tokens_ref[...], NT)
    dispatch = dispatch_ref[...]
    combine = combine_ref[...]
    slot_sum = jnp.sum(combine * combine_grad, axis=0, keepdims=True)
    patch_sum = jnp.sum(dispatch * dispatch_grad, axis=1, keepdims=True)
    logits_grad = combine * (combine_grad - slot_sum) + dispatch * (dispatch_grad - patch_sum)
    term_ref[...] = dot(logits_grad.astype(BF16), tokens_ref[...], NN).astype(BF16)
    left_ref[...] = jnp.concatenate([logits_grad, dispatch], axis=0).astype(BF16)
    right_ref[...] = jnp.concatenate(
        [router_ref[...].astype(F32), back_rows_ref[...]], axis=0
    ).astype(BF16)


def tokens_kernel(left_ref, right_ref, tokens_grad_ref):
    tokens_grad_ref[...] = dot(left_ref[...], right_ref[...], TN).astype(BF16)


def call(kernel, outs, scratch, cost, *operands):
    return pl.pallas_call(
        kernel,
        out_shape=[jax.ShapeDtypeStruct(shape, dtype) for shape, dtype in outs],
        in_specs=[pl.BlockSpec(memory_space=pltpu.VMEM)] * len(operands),
        out_specs=[pl.BlockSpec(memory_space=pltpu.VMEM)] * len(outs),
        scratch_shapes=[pltpu.VMEM(shape, F32) for shape in scratch],
        compiler_params=pltpu.CompilerParams(vmem_limit_bytes=16 * 2**20),
        cost_estimate=pl.CostEstimate(flops=cost[0], bytes_accessed=cost[1], transcendentals=0),
    )(*operands)


def swap_cores(value):
    size = lax.axis_size("expert")
    return lax.ppermute(value, "expert", [(i, i ^ 1) for i in range(size)])


def exchange(value, groups):
    return lax.all_to_all(
        value, "expert", split_axis=0, concat_axis=0, tiled=True, axis_index_groups=groups
    )


def per_device(tokens, out_grad, router, in_weight, out_weight):
    _, patches, width = tokens.shape
    hidden = in_weight.shape[1]
    slots = router.shape[1]
    chips = slots
    tokens = tokens[0]
    out_grad = out_grad[0]
    router_rows = router.T
    image_bytes = 2 * patches * width
    weight_bytes = 2 * width * hidden
    (token,) = call(first_kernel, [((8, 128), F32)], [], (AHEAD_FLOPS, image_bytes))
    slot_in, dispatch, combine = call(
        slots_kernel,
        [((slots, width), F32), ((slots, patches), F32), ((slots, patches), F32)],
        [],
        (8 * patches * width * slots, image_bytes),
        tokens,
        router_rows,
        token,
    )
    (sent,) = call(
        messages_kernel,
        [((2 * slots, 2, width), BF16)],
        [],
        (4 * patches * width * slots, image_bytes),
        out_grad,
        combine,
        slot_in,
    )
    got = exchange(sent, [everybody(chips)])
    (parts,) = call(
        experts_kernel,
        [((2 * chips, 2, width), BF16)],
        [(2 * chips, width)] * 2,
        (16 * chips * width * hidden, 2 * weight_bytes),
        got,
        in_weight,
        out_weight,
    )
    back = exchange(parts, [everybody(chips)])
    term, left, right = call(
        logits_kernel,
        [
            ((slots, width), BF16),
            ((2 * slots, patches), BF16),
            ((2 * slots, width), BF16),
        ],
        [(slots, width)] * 2,
        (12 * patches * width * slots, 2 * image_bytes),
        tokens,
        out_grad,
        router_rows,
        dispatch,
        combine,
        back,
    )
    same_core = [everybody(chips)[1 - core :: 2] for core in range(2)]
    terms = exchange(jnp.broadcast_to(term[None], (chips,) + term.shape), same_core)
    total = jnp.sum(terms.astype(F32), axis=0)
    router_grad = total + swap_cores(total)
    (tokens_grad,) = call(
        tokens_kernel,
        [((patches, width), BF16)],
        [],
        (4 * patches * width * slots, image_bytes),
        left,
        right,
    )
    return (tokens_grad[None], router_grad.T)


def solution(mesh):
    images = P(("group", "expert"), None, None)
    in_specs = (images, images, P(), P(None, "expert"), P("expert", None))
    out_specs = (images, P("group", None))
    return jax.shard_map(
        per_device, mesh=mesh, in_specs=in_specs, out_specs=out_specs, check_vma=False
    )
```

```python
import math

import jax
import jax.numpy as jnp
from jax import lax
from jax.experimental import pallas as pl
from jax.experimental.pallas import tpu as pltpu
from jax.sharding import PartitionSpec as P

F32 = jnp.float32
BF16 = jnp.bfloat16
NN = (((1,), (0,)), ((), ()))
NT = (((1,), (1,)), ((), ()))
TN = (((0,), (0,)), ((), ()))
AHEAD_FLOPS = 3 * 10**10


def chip_order(chips):
    return [k // 2 if k % 2 else chips - 1 - k // 2 for k in range(chips)]


def everybody(chips):
    return [2 * chip + core for chip in chip_order(chips) for core in (1, 0)]


def dot(a, b, dims):
    return lax.dot_general(a, b, dims, preferred_element_type=F32)


def first_kernel(token_ref):
    token_ref[...] = jnp.zeros(token_ref.shape, F32)


def slots_kernel(tokens_ref, router_ref, token_ref, slot_in_ref, dispatch_ref, combine_ref):
    logits = dot(router_ref[...], tokens_ref[...], NT)
    over_patches = jnp.exp(logits - jnp.max(logits, axis=1, keepdims=True))
    dispatch = over_patches / jnp.sum(over_patches, axis=1, keepdims=True)
    over_slots = jnp.exp(logits - jnp.max(logits, axis=0, keepdims=True))
    dispatch_ref[...] = dispatch
    combine_ref[...] = over_slots / jnp.sum(over_slots, axis=0, keepdims=True)
    slot_in_ref[...] = dot(dispatch.astype(BF16), tokens_ref[...], NN)


def messages_kernel(grad_ref, combine_ref, slot_in_ref, sent_ref):
    slot_grad = dot(combine_ref[...].astype(BF16), grad_ref[...], NN)
    slots = slot_in_ref.shape[0]
    order = everybody(slots)
    for s in range(slots):
        rows = [slot_in_ref[s : s + 1], slot_grad[s : s + 1]]
        message = jnp.concatenate(rows, axis=0).astype(BF16)
        for half in range(2):
            sent_ref[order.index(2 * s + half)] = message


def experts_kernel(got_ref, in_weight_ref, out_weight_ref, parts_ref):
    messages = got_ref[...].astype(F32)
    in_rows = messages[:, 0].astype(BF16)
    grad_rows = messages[:, 1].astype(BF16)
    hidden = dot(in_rows, in_weight_ref[...], NN)
    act_grad = dot(grad_rows, out_weight_ref[...], NT)
    normal_cdf = 0.5 * (1.0 + lax.erf(hidden * (1.0 / math.sqrt(2.0))))
    normal_pdf = jnp.exp(-0.5 * hidden * hidden) * (1.0 / math.sqrt(2.0 * math.pi))
    activation = (hidden * normal_cdf).astype(BF16)
    hidden_grad = (act_grad * (normal_cdf + hidden * normal_pdf)).astype(BF16)
    part_out = dot(activation, out_weight_ref[...], NN)
    part_in = dot(hidden_grad, in_weight_ref[...], NT)
    parts_ref[...] = jnp.stack([part_out, part_in], axis=1).astype(BF16)


def logits_kernel(
    tokens_ref,
    grad_ref,
    router_ref,
    dispatch_ref,
    combine_ref,
    back_ref,
    kept_ref,
    given_ref,
    logits_ref,
    back_rows_ref,
    out_rows_ref,
):
    slots = router_ref.shape[0]
    order = everybody(slots)
    for s in range(slots):
        halves = [back_ref[order.index(2 * s + half)].astype(F32) for half in range(2)]
        message = halves[0] + halves[1]
        out_rows_ref[s : s + 1] = message[0:1]
        back_rows_ref[s : s + 1] = message[1:2]
    slot_back = back_rows_ref[...].astype(BF16)
    combine_grad = dot(out_rows_ref[...].astype(BF16), grad_ref[...], NT)
    dispatch_grad = dot(slot_back, tokens_ref[...], NT)
    dispatch = dispatch_ref[...]
    combine = combine_ref[...]
    slot_sum = jnp.sum(combine * combine_grad, axis=0, keepdims=True)
    patch_sum = jnp.sum(dispatch * dispatch_grad, axis=1, keepdims=True)
    logits_grad = combine * (combine_grad - slot_sum) + dispatch * (dispatch_grad - patch_sum)
    part = dot(logits_grad.astype(BF16), tokens_ref[...], NN)
    half = part.shape[1] // 2
    first = lax.axis_index("expert") % 2 == 0
    kept_ref[...] = jnp.where(first, part[:, :half], part[:, half:])
    given_ref[...] = jnp.where(first, part[:, half:], part[:, :half])
    logits_ref[...] = logits_grad


def tokens_kernel(logits_ref, dispatch_ref, router_ref, back_rows_ref, tokens_grad_ref):
    left = jnp.concatenate([logits_ref[...], dispatch_ref[...]], axis=0).astype(BF16)
    rows = [router_ref[...].astype(F32), back_rows_ref[...]]
    right = jnp.concatenate(rows, axis=0).astype(BF16)
    tokens_grad_ref[...] = dot(left, right, TN).astype(BF16)


def call(kernel, outs, scratch, cost, *operands):
    return pl.pallas_call(
        kernel,
        out_shape=[jax.ShapeDtypeStruct(shape, dtype) for shape, dtype in outs],
        in_specs=[pl.BlockSpec(memory_space=pltpu.VMEM)] * len(operands),
        out_specs=[pl.BlockSpec(memory_space=pltpu.VMEM)] * len(outs),
        scratch_shapes=[pltpu.VMEM(shape, F32) for shape in scratch],
        compiler_params=pltpu.CompilerParams(vmem_limit_bytes=16 * 2**20),
        cost_estimate=pl.CostEstimate(flops=cost[0], bytes_accessed=cost[1], transcendentals=0),
    )(*operands)


def swap_cores(value):
    size = lax.axis_size("expert")
    return lax.ppermute(value, "expert", [(i, i ^ 1) for i in range(size)])


def exchange(value, groups):
    return lax.all_to_all(
        value, "expert", split_axis=0, concat_axis=0, tiled=True, axis_index_groups=groups
    )


def per_device(tokens, out_grad, router, in_weight, out_weight):
    _, patches, width = tokens.shape
    hidden = in_weight.shape[1]
    slots = router.shape[1]
    chips = slots
    tokens = tokens[0]
    out_grad = out_grad[0]
    router_rows = router.T
    image_bytes = 2 * patches * width
    weight_bytes = 2 * width * hidden
    (token,) = call(first_kernel, [((8, 128), F32)], [], (AHEAD_FLOPS, image_bytes))
    slot_in, dispatch, combine = call(
        slots_kernel,
        [((slots, width), F32), ((slots, patches), F32), ((slots, patches), F32)],
        [],
        (8 * patches * width * slots, image_bytes),
        tokens,
        router_rows,
        token,
    )
    (sent,) = call(
        messages_kernel,
        [((2 * slots, 2, width), BF16)],
        [],
        (4 * patches * width * slots, image_bytes),
        out_grad,
        combine,
        slot_in,
    )
    got = exchange(sent, [everybody(chips)])
    (parts,) = call(
        experts_kernel,
        [((2 * chips, 2, width), BF16)],
        [],
        (16 * chips * width * hidden, 2 * weight_bytes),
        got,
        in_weight,
        out_weight,
    )
    back = exchange(parts, [everybody(chips)])
    kept, given, logits_grad, slot_back = call(
        logits_kernel,
        [
            ((slots, width // 2), F32),
            ((slots, width // 2), F32),
            ((slots, patches), F32),
            ((slots, width), F32),
        ],
        [(slots, width)],
        (12 * patches * width * slots, 2 * image_bytes),
        tokens,
        out_grad,
        router_rows,
        dispatch,
        combine,
        back,
    )
    pair = (kept + swap_cores(given)).astype(BF16)
    same_core = [everybody(chips)[1 - core :: 2] for core in range(2)]
    terms = exchange(jnp.broadcast_to(pair[None], (chips,) + pair.shape), same_core)
    total = jnp.sum(terms.astype(F32), axis=0)
    other = swap_cores(total)
    first = lax.axis_index("expert") % 2 == 0
    router_grad = jnp.concatenate(
        [jnp.where(first, total, other), jnp.where(first, other, total)], axis=1
    )
    (tokens_grad,) = call(
        tokens_kernel,
        [((patches, width), BF16)],
        [],
        (4 * patches * width * slots, image_bytes),
        logits_grad,
        dispatch,
        router_rows,
        slot_back,
    )
    return (tokens_grad[None], router_grad.T)


def solution(mesh):
    images = P(("group", "expert"), None, None)
    in_specs = (images, images, P(), P(None, "expert"), P("expert", None))
    out_specs = (images, P("group", None))
    return jax.shard_map(
        per_device, mesh=mesh, in_specs=in_specs, out_specs=out_specs, check_vma=False
    )
```

```python
import math

import jax
import jax.numpy as jnp
from jax import lax
from jax.experimental import pallas as pl
from jax.experimental.pallas import tpu as pltpu
from jax.sharding import PartitionSpec as P

F32 = jnp.float32
BF16 = jnp.bfloat16
NN = (((1,), (0,)), ((), ()))
NT = (((1,), (1,)), ((), ()))
TN = (((0,), (0,)), ((), ()))
AHEAD_FLOPS = 3 * 10**10


def chip_order(chips):
    return [k // 2 if k % 2 else chips - 1 - k // 2 for k in range(chips)]


def everybody(chips):
    return [2 * chip + core for chip in chip_order(chips) for core in (1, 0)]


def dot(a, b, dims):
    return lax.dot_general(a, b, dims, preferred_element_type=F32)


def first_kernel(token_ref):
    token_ref[...] = jnp.zeros(token_ref.shape, F32)


def slots_kernel(tokens_ref, router_ref, token_ref, slot_in_ref, dispatch_ref, combine_ref):
    logits = dot(router_ref[...], tokens_ref[...], NT)
    over_patches = jnp.exp(logits - jnp.max(logits, axis=1, keepdims=True))
    dispatch = over_patches / jnp.sum(over_patches, axis=1, keepdims=True)
    over_slots = jnp.exp(logits - jnp.max(logits, axis=0, keepdims=True))
    dispatch_ref[...] = dispatch
    combine_ref[...] = over_slots / jnp.sum(over_slots, axis=0, keepdims=True)
    slot_in_ref[...] = dot(dispatch.astype(BF16), tokens_ref[...], NN)


def messages_kernel(grad_ref, combine_ref, slot_in_ref, sent_ref):
    slot_grad = dot(combine_ref[...].astype(BF16), grad_ref[...], NN)
    slots = slot_in_ref.shape[0]
    order = everybody(slots)
    for s in range(slots):
        rows = [slot_in_ref[s : s + 1], slot_grad[s : s + 1]]
        message = jnp.concatenate(rows, axis=0).astype(BF16)
        for half in range(2):
            sent_ref[order.index(2 * s + half)] = message


def experts_kernel(
    got_ref, in_weight_ref, out_weight_ref, parts_ref, in_rows_ref, grad_rows_ref
):
    images = got_ref.shape[0]
    for k in range(images):
        message = got_ref[k].astype(F32)
        in_rows_ref[k : k + 1] = message[0:1]
        grad_rows_ref[k : k + 1] = message[1:2]
    hidden = dot(in_rows_ref[...].astype(BF16), in_weight_ref[...], NN)
    act_grad = dot(grad_rows_ref[...].astype(BF16), out_weight_ref[...], NT)
    normal_cdf = 0.5 * (1.0 + lax.erf(hidden * (1.0 / math.sqrt(2.0))))
    normal_pdf = jnp.exp(-0.5 * hidden * hidden) * (1.0 / math.sqrt(2.0 * math.pi))
    activation = (hidden * normal_cdf).astype(BF16)
    hidden_grad = (act_grad * (normal_cdf + hidden * normal_pdf)).astype(BF16)
    part_out = dot(activation, out_weight_ref[...], NN)
    part_in = dot(hidden_grad, in_weight_ref[...], NT)
    for k in range(images):
        rows = [part_out[k : k + 1], part_in[k : k + 1]]
        parts_ref[k] = jnp.concatenate(rows, axis=0).astype(BF16)


def logits_kernel(
    tokens_ref,
    grad_ref,
    router_ref,
    dispatch_ref,
    combine_ref,
    back_ref,
    kept_ref,
    given_ref,
    left_ref,
    right_ref,
    out_rows_ref,
    back_rows_ref,
):
    slots = router_ref.shape[0]
    order = everybody(slots)
    for s in range(slots):
        halves = [back_ref[order.index(2 * s + half)].astype(F32) for half in range(2)]
        message = halves[0] + halves[1]
        out_rows_ref[s : s + 1] = message[0:1]
        back_rows_ref[s : s + 1] = message[1:2]
    slot_back = back_rows_ref[...].astype(BF16)
    combine_grad = dot(out_rows_ref[...].astype(BF16), grad_ref[...], NT)
    dispatch_grad = dot(slot_back, tokens_ref[...], NT)
    dispatch = dispatch_ref[...]
    combine = combine_ref[...]
    slot_sum = jnp.sum(combine * combine_grad, axis=0, keepdims=True)
    patch_sum = jnp.sum(dispatch * dispatch_grad, axis=1, keepdims=True)
    logits_grad = combine * (combine_grad - slot_sum) + dispatch * (dispatch_grad - patch_sum)
    part = dot(logits_grad.astype(BF16), tokens_ref[...], NN)
    half = part.shape[1] // 2
    first = lax.axis_index("expert") % 2 == 0
    kept_ref[...] = jnp.where(first, part[:, :half], part[:, half:])
    given_ref[...] = jnp.where(first, part[:, half:], part[:, :half])
    left_ref[...] = jnp.concatenate([logits_grad, dispatch], axis=0).astype(BF16)
    right_ref[...] = jnp.concatenate(
        [router_ref[...].astype(F32), back_rows_ref[...]], axis=0
    ).astype(BF16)


def tokens_kernel(left_ref, right_ref, tokens_grad_ref):
    tokens_grad_ref[...] = dot(left_ref[...], right_ref[...], TN).astype(BF16)


def call(kernel, outs, scratch, cost, *operands):
    return pl.pallas_call(
        kernel,
        out_shape=[jax.ShapeDtypeStruct(shape, dtype) for shape, dtype in outs],
        in_specs=[pl.BlockSpec(memory_space=pltpu.VMEM)] * len(operands),
        out_specs=[pl.BlockSpec(memory_space=pltpu.VMEM)] * len(outs),
        scratch_shapes=[pltpu.VMEM(shape, F32) for shape in scratch],
        compiler_params=pltpu.CompilerParams(vmem_limit_bytes=16 * 2**20),
        cost_estimate=pl.CostEstimate(flops=cost[0], bytes_accessed=cost[1], transcendentals=0),
    )(*operands)


def swap_cores(value):
    size = lax.axis_size("expert")
    return lax.ppermute(value, "expert", [(i, i ^ 1) for i in range(size)])


def exchange(value, groups):
    return lax.all_to_all(
        value, "expert", split_axis=0, concat_axis=0, tiled=True, axis_index_groups=groups
    )


def per_device(tokens, out_grad, router, in_weight, out_weight):
    _, patches, width = tokens.shape
    hidden = in_weight.shape[1]
    slots = router.shape[1]
    chips = slots
    tokens = tokens[0]
    out_grad = out_grad[0]
    router_rows = router.T
    image_bytes = 2 * patches * width
    weight_bytes = 2 * width * hidden
    (token,) = call(first_kernel, [((8, 128), F32)], [], (AHEAD_FLOPS, image_bytes))
    slot_in, dispatch, combine = call(
        slots_kernel,
        [((slots, width), F32), ((slots, patches), F32), ((slots, patches), F32)],
        [],
        (8 * patches * width * slots, image_bytes),
        tokens,
        router_rows,
        token,
    )
    (sent,) = call(
        messages_kernel,
        [((2 * slots, 2, width), BF16)],
        [],
        (4 * patches * width * slots, image_bytes),
        out_grad,
        combine,
        slot_in,
    )
    got = exchange(sent, [everybody(chips)])
    (parts,) = call(
        experts_kernel,
        [((2 * chips, 2, width), BF16)],
        [(2 * chips, width)] * 2,
        (16 * chips * width * hidden, 2 * weight_bytes),
        got,
        in_weight,
        out_weight,
    )
    back = exchange(parts, [everybody(chips)])
    kept, given, left, right = call(
        logits_kernel,
        [
            ((slots, width // 2), F32),
            ((slots, width // 2), F32),
            ((2 * slots, patches), BF16),
            ((2 * slots, width), BF16),
        ],
        [(slots, width)] * 2,
        (12 * patches * width * slots, 2 * image_bytes),
        tokens,
        out_grad,
        router_rows,
        dispatch,
        combine,
        back,
    )
    pair = (kept + swap_cores(given)).astype(BF16)
    same_core = [everybody(chips)[1 - core :: 2] for core in range(2)]
    terms = exchange(jnp.broadcast_to(pair[None], (chips,) + pair.shape), same_core)
    total = jnp.sum(terms.astype(F32), axis=0)
    other = swap_cores(total)
    first = lax.axis_index("expert") % 2 == 0
    router_grad = jnp.concatenate(
        [jnp.where(first, total, other), jnp.where(first, other, total)], axis=1
    )
    (tokens_grad,) = call(
        tokens_kernel,
        [((patches, width), BF16)],
        [],
        (4 * patches * width * slots, image_bytes),
        left,
        right,
    )
    return (tokens_grad[None], router_grad.T)


def solution(mesh):
    images = P(("group", "expert"), None, None)
    in_specs = (images, images, P(), P(None, "expert"), P("expert", None))
    out_specs = (images, P("group", None))
    return jax.shard_map(
        per_device, mesh=mesh, in_specs=in_specs, out_specs=out_specs, check_vma=False
    )
```

```python
import math

import jax
import jax.numpy as jnp
from jax import lax
from jax.experimental import pallas as pl
from jax.experimental.pallas import tpu as pltpu
from jax.sharding import PartitionSpec as P

F32 = jnp.float32
BF16 = jnp.bfloat16
NN = (((1,), (0,)), ((), ()))
NT = (((1,), (1,)), ((), ()))
TN = (((0,), (0,)), ((), ()))
AHEAD_FLOPS = 3 * 10**10


def out_order(size):
    return [size - 1] + list(range(1, size - 1)) + [0]


def back_order(size):
    return [(size - 1 + 5 * k) % size for k in range(size)]


def sum_order(size, core):
    chips = size // 2
    order = [k // 2 if k % 2 else chips - 1 - k // 2 for k in range(chips)]
    return [2 * chip + core for chip in order]


def dot(a, b, dims):
    return lax.dot_general(a, b, dims, preferred_element_type=F32)


def first_kernel(token_ref):
    token_ref[...] = jnp.zeros(token_ref.shape, F32)


def slots_kernel(tokens_ref, router_ref, token_ref, slot_in_ref, dispatch_ref, combine_ref):
    logits = dot(router_ref[...], tokens_ref[...], NT)
    over_patches = jnp.exp(logits - jnp.max(logits, axis=1, keepdims=True))
    dispatch = over_patches / jnp.sum(over_patches, axis=1, keepdims=True)
    over_slots = jnp.exp(logits - jnp.max(logits, axis=0, keepdims=True))
    dispatch_ref[...] = dispatch
    combine_ref[...] = over_slots / jnp.sum(over_slots, axis=0, keepdims=True)
    slot_in_ref[...] = dot(dispatch.astype(BF16), tokens_ref[...], NN)


def messages_kernel(grad_ref, combine_ref, slot_in_ref, sent_ref):
    slot_grad = dot(combine_ref[...].astype(BF16), grad_ref[...], NN)
    slots = slot_in_ref.shape[0]
    order = out_order(2 * slots)
    for s in range(slots):
        rows = [slot_in_ref[s : s + 1], slot_grad[s : s + 1]]
        message = jnp.concatenate(rows, axis=0).astype(BF16)
        for half in range(2):
            sent_ref[order.index(2 * s + half)] = message


def experts_kernel(
    got_ref, in_weight_ref, out_weight_ref, parts_ref, in_rows_ref, grad_rows_ref
):
    images = got_ref.shape[0]
    out, back = out_order(images), back_order(images)
    for k in range(images):
        message = got_ref[k].astype(F32)
        in_rows_ref[k : k + 1] = message[0:1]
        grad_rows_ref[k : k + 1] = message[1:2]
    hidden = dot(in_rows_ref[...].astype(BF16), in_weight_ref[...], NN)
    act_grad = dot(grad_rows_ref[...].astype(BF16), out_weight_ref[...], NT)
    normal_cdf = 0.5 * (1.0 + lax.erf(hidden * (1.0 / math.sqrt(2.0))))
    normal_pdf = jnp.exp(-0.5 * hidden * hidden) * (1.0 / math.sqrt(2.0 * math.pi))
    activation = (hidden * normal_cdf).astype(BF16)
    hidden_grad = (act_grad * (normal_cdf + hidden * normal_pdf)).astype(BF16)
    part_out = dot(activation, out_weight_ref[...], NN)
    part_in = dot(hidden_grad, in_weight_ref[...], NT)
    for k in range(images):
        rows = [part_out[k : k + 1], part_in[k : k + 1]]
        parts_ref[back.index(out[k])] = jnp.concatenate(rows, axis=0).astype(BF16)


def logits_kernel(
    tokens_ref,
    grad_ref,
    router_ref,
    dispatch_ref,
    combine_ref,
    back_ref,
    kept_ref,
    given_ref,
    left_ref,
    right_ref,
    out_rows_ref,
    back_rows_ref,
):
    slots = router_ref.shape[0]
    order = back_order(2 * slots)
    for s in range(slots):
        halves = [back_ref[order.index(2 * s + half)].astype(F32) for half in range(2)]
        message = halves[0] + halves[1]
        out_rows_ref[s : s + 1] = message[0:1]
        back_rows_ref[s : s + 1] = message[1:2]
    slot_back = back_rows_ref[...].astype(BF16)
    combine_grad = dot(out_rows_ref[...].astype(BF16), grad_ref[...], NT)
    dispatch_grad = dot(slot_back, tokens_ref[...], NT)
    dispatch = dispatch_ref[...]
    combine = combine_ref[...]
    slot_sum = jnp.sum(combine * combine_grad, axis=0, keepdims=True)
    patch_sum = jnp.sum(dispatch * dispatch_grad, axis=1, keepdims=True)
    logits_grad = combine * (combine_grad - slot_sum) + dispatch * (dispatch_grad - patch_sum)
    part = dot(logits_grad.astype(BF16), tokens_ref[...], NN)
    half = part.shape[1] // 2
    first = lax.axis_index("expert") % 2 == 0
    kept_ref[...] = jnp.where(first, part[:, :half], part[:, half:])
    given_ref[...] = jnp.where(first, part[:, half:], part[:, :half])
    left_ref[...] = jnp.concatenate([logits_grad, dispatch], axis=0).astype(BF16)
    right_ref[...] = jnp.concatenate(
        [router_ref[...].astype(F32), back_rows_ref[...]], axis=0
    ).astype(BF16)


def tokens_kernel(left_ref, right_ref, tokens_grad_ref):
    tokens_grad_ref[...] = dot(left_ref[...], right_ref[...], TN).astype(BF16)


def call(kernel, outs, scratch, cost, *operands):
    return pl.pallas_call(
        kernel,
        out_shape=[jax.ShapeDtypeStruct(shape, dtype) for shape, dtype in outs],
        in_specs=[pl.BlockSpec(memory_space=pltpu.VMEM)] * len(operands),
        out_specs=[pl.BlockSpec(memory_space=pltpu.VMEM)] * len(outs),
        scratch_shapes=[pltpu.VMEM(shape, F32) for shape in scratch],
        compiler_params=pltpu.CompilerParams(vmem_limit_bytes=16 * 2**20),
        cost_estimate=pl.CostEstimate(flops=cost[0], bytes_accessed=cost[1], transcendentals=0),
    )(*operands)


def swap_cores(value):
    size = lax.axis_size("expert")
    return lax.ppermute(value, "expert", [(i, i ^ 1) for i in range(size)])


def exchange(value, groups):
    return lax.all_to_all(
        value, "expert", split_axis=0, concat_axis=0, tiled=True, axis_index_groups=groups
    )


def per_device(tokens, out_grad, router, in_weight, out_weight):
    _, patches, width = tokens.shape
    hidden = in_weight.shape[1]
    slots = router.shape[1]
    chips = slots
    tokens = tokens[0]
    out_grad = out_grad[0]
    router_rows = router.T
    image_bytes = 2 * patches * width
    weight_bytes = 2 * width * hidden
    (token,) = call(first_kernel, [((8, 128), F32)], [], (AHEAD_FLOPS, image_bytes))
    slot_in, dispatch, combine = call(
        slots_kernel,
        [((slots, width), F32), ((slots, patches), F32), ((slots, patches), F32)],
        [],
        (8 * patches * width * slots, image_bytes),
        tokens,
        router_rows,
        token,
    )
    (sent,) = call(
        messages_kernel,
        [((2 * slots, 2, width), BF16)],
        [],
        (4 * patches * width * slots, image_bytes),
        out_grad,
        combine,
        slot_in,
    )
    got = exchange(sent, [out_order(2 * chips)])
    (parts,) = call(
        experts_kernel,
        [((2 * chips, 2, width), BF16)],
        [(2 * chips, width)] * 2,
        (16 * chips * width * hidden, 2 * weight_bytes),
        got,
        in_weight,
        out_weight,
    )
    back = exchange(parts, [back_order(2 * chips)])
    kept, given, left, right = call(
        logits_kernel,
        [
            ((slots, width // 2), F32),
            ((slots, width // 2), F32),
            ((2 * slots, patches), BF16),
            ((2 * slots, width), BF16),
        ],
        [(slots, width)] * 2,
        (12 * patches * width * slots, 2 * image_bytes),
        tokens,
        out_grad,
        router_rows,
        dispatch,
        combine,
        back,
    )
    pair = (kept + swap_cores(given)).astype(BF16)
    same_core = [sum_order(2 * chips, core) for core in range(2)]
    terms = exchange(jnp.broadcast_to(pair[None], (chips,) + pair.shape), same_core)
    total = jnp.sum(terms.astype(F32), axis=0)
    other = swap_cores(total)
    first = lax.axis_index("expert") % 2 == 0
    router_grad = jnp.concatenate(
        [jnp.where(first, total, other), jnp.where(first, other, total)], axis=1
    )
    (tokens_grad,) = call(
        tokens_kernel,
        [((patches, width), BF16)],
        [],
        (4 * patches * width * slots, image_bytes),
        left,
        right,
    )
    return (tokens_grad[None], router_grad.T)


def solution(mesh):
    images = P(("group", "expert"), None, None)
    in_specs = (images, images, P(), P(None, "expert"), P("expert", None))
    out_specs = (images, P("group", None))
    return jax.shard_map(
        per_device, mesh=mesh, in_specs=in_specs, out_specs=out_specs, check_vma=False
    )
```

```python
import math

import jax
import jax.numpy as jnp
from jax import lax
from jax.experimental import pallas as pl
from jax.experimental.pallas import tpu as pltpu
from jax.sharding import PartitionSpec as P

F32 = jnp.float32
BF16 = jnp.bfloat16
NN = (((1,), (0,)), ((), ()))
NT = (((1,), (1,)), ((), ()))
TN = (((0,), (0,)), ((), ()))
AHEAD_FLOPS = 3 * 10**10


def listed(count):
    return [(count - 1 + 5 * k) % count for k in range(count)]


def dot(a, b, dims):
    return lax.dot_general(a, b, dims, preferred_element_type=F32)


def first_kernel(token_ref):
    token_ref[...] = jnp.zeros(token_ref.shape, F32)


def slots_kernel(tokens_ref, router_ref, token_ref, slot_in_ref, dispatch_ref, combine_ref):
    logits = dot(router_ref[...], tokens_ref[...], NT)
    over_patches = jnp.exp(logits - jnp.max(logits, axis=1, keepdims=True))
    dispatch = over_patches / jnp.sum(over_patches, axis=1, keepdims=True)
    over_slots = jnp.exp(logits - jnp.max(logits, axis=0, keepdims=True))
    dispatch_ref[...] = dispatch
    combine_ref[...] = over_slots / jnp.sum(over_slots, axis=0, keepdims=True)
    slot_in_ref[...] = dot(dispatch.astype(BF16), tokens_ref[...], NN)


def messages_kernel(grad_ref, combine_ref, slot_in_ref, sent_ref):
    slot_grad = dot(combine_ref[...].astype(BF16), grad_ref[...], NN)
    slots = slot_in_ref.shape[0]
    order = listed(2 * slots)
    for s in range(slots):
        rows = [slot_in_ref[s : s + 1], slot_grad[s : s + 1]]
        message = jnp.concatenate(rows, axis=0).astype(BF16)
        for half in range(2):
            sent_ref[order.index(2 * s + half)] = message


def experts_kernel(
    got_ref, in_weight_ref, out_weight_ref, parts_ref, in_rows_ref, grad_rows_ref
):
    images = got_ref.shape[0]
    for k in range(images):
        message = got_ref[k].astype(F32)
        in_rows_ref[k : k + 1] = message[0:1]
        grad_rows_ref[k : k + 1] = message[1:2]
    hidden = dot(in_rows_ref[...].astype(BF16), in_weight_ref[...], NN)
    act_grad = dot(grad_rows_ref[...].astype(BF16), out_weight_ref[...], NT)
    normal_cdf = 0.5 * (1.0 + lax.erf(hidden * (1.0 / math.sqrt(2.0))))
    normal_pdf = jnp.exp(-0.5 * hidden * hidden) * (1.0 / math.sqrt(2.0 * math.pi))
    activation = (hidden * normal_cdf).astype(BF16)
    hidden_grad = (act_grad * (normal_cdf + hidden * normal_pdf)).astype(BF16)
    part_out = dot(activation, out_weight_ref[...], NN)
    part_in = dot(hidden_grad, in_weight_ref[...], NT)
    for k in range(images):
        rows = [part_out[k : k + 1], part_in[k : k + 1]]
        parts_ref[k] = jnp.concatenate(rows, axis=0).astype(BF16)


def logits_kernel(
    tokens_ref,
    grad_ref,
    router_ref,
    dispatch_ref,
    combine_ref,
    back_ref,
    kept_ref,
    given_ref,
    left_ref,
    right_ref,
    out_rows_ref,
    back_rows_ref,
):
    slots = router_ref.shape[0]
    order = listed(2 * slots)
    for s in range(slots):
        halves = [back_ref[order.index(2 * s + half)].astype(F32) for half in range(2)]
        message = halves[0] + halves[1]
        out_rows_ref[s : s + 1] = message[0:1]
        back_rows_ref[s : s + 1] = message[1:2]
    slot_back = back_rows_ref[...].astype(BF16)
    combine_grad = dot(out_rows_ref[...].astype(BF16), grad_ref[...], NT)
    dispatch_grad = dot(slot_back, tokens_ref[...], NT)
    dispatch = dispatch_ref[...]
    combine = combine_ref[...]
    slot_sum = jnp.sum(combine * combine_grad, axis=0, keepdims=True)
    patch_sum = jnp.sum(dispatch * dispatch_grad, axis=1, keepdims=True)
    logits_grad = combine * (combine_grad - slot_sum) + dispatch * (dispatch_grad - patch_sum)
    part = dot(logits_grad.astype(BF16), tokens_ref[...], NN)
    half = part.shape[1] // 2
    first = lax.axis_index("expert") % 2 == 0
    kept_ref[...] = jnp.where(first, part[:, :half], part[:, half:])
    given_ref[...] = jnp.where(first, part[:, half:], part[:, :half])
    left_ref[...] = jnp.concatenate([logits_grad, dispatch], axis=0).astype(BF16)
    right_ref[...] = jnp.concatenate(
        [router_ref[...].astype(F32), back_rows_ref[...]], axis=0
    ).astype(BF16)


def tokens_kernel(left_ref, right_ref, tokens_grad_ref):
    tokens_grad_ref[...] = dot(left_ref[...], right_ref[...], TN).astype(BF16)


def call(kernel, outs, scratch, cost, *operands):
    return pl.pallas_call(
        kernel,
        out_shape=[jax.ShapeDtypeStruct(shape, dtype) for shape, dtype in outs],
        in_specs=[pl.BlockSpec(memory_space=pltpu.VMEM)] * len(operands),
        out_specs=[pl.BlockSpec(memory_space=pltpu.VMEM)] * len(outs),
        scratch_shapes=[pltpu.VMEM(shape, F32) for shape in scratch],
        compiler_params=pltpu.CompilerParams(vmem_limit_bytes=16 * 2**20),
        cost_estimate=pl.CostEstimate(flops=cost[0], bytes_accessed=cost[1], transcendentals=0),
    )(*operands)


def swap_cores(value):
    size = lax.axis_size("expert")
    return lax.ppermute(value, "expert", [(i, i ^ 1) for i in range(size)])


def exchange(value, groups):
    return lax.all_to_all(
        value, "expert", split_axis=0, concat_axis=0, tiled=True, axis_index_groups=groups
    )


def per_device(tokens, out_grad, router, in_weight, out_weight):
    _, patches, width = tokens.shape
    hidden = in_weight.shape[1]
    slots = router.shape[1]
    chips = slots
    tokens = tokens[0]
    out_grad = out_grad[0]
    router_rows = router.T
    image_bytes = 2 * patches * width
    weight_bytes = 2 * width * hidden
    (token,) = call(first_kernel, [((8, 128), F32)], [], (AHEAD_FLOPS, image_bytes))
    slot_in, dispatch, combine = call(
        slots_kernel,
        [((slots, width), F32), ((slots, patches), F32), ((slots, patches), F32)],
        [],
        (8 * patches * width * slots, image_bytes),
        tokens,
        router_rows,
        token,
    )
    (sent,) = call(
        messages_kernel,
        [((2 * slots, 2, width), BF16)],
        [],
        (4 * patches * width * slots, image_bytes),
        out_grad,
        combine,
        slot_in,
    )
    got = exchange(sent, [listed(2 * chips)])
    (parts,) = call(
        experts_kernel,
        [((2 * chips, 2, width), BF16)],
        [(2 * chips, width)] * 2,
        (16 * chips * width * hidden, 2 * weight_bytes),
        got,
        in_weight,
        out_weight,
    )
    back = exchange(parts, [listed(2 * chips)])
    kept, given, left, right = call(
        logits_kernel,
        [
            ((slots, width // 2), F32),
            ((slots, width // 2), F32),
            ((2 * slots, patches), BF16),
            ((2 * slots, width), BF16),
        ],
        [(slots, width)] * 2,
        (12 * patches * width * slots, 2 * image_bytes),
        tokens,
        out_grad,
        router_rows,
        dispatch,
        combine,
        back,
    )
    pair = (kept + swap_cores(given)).astype(BF16)
    same_core = [[2 * chip + core for chip in listed(chips)] for core in range(2)]
    terms = exchange(jnp.broadcast_to(pair[None], (chips,) + pair.shape), same_core)
    total = jnp.sum(terms.astype(F32), axis=0)
    other = swap_cores(total)
    first = lax.axis_index("expert") % 2 == 0
    router_grad = jnp.concatenate(
        [jnp.where(first, total, other), jnp.where(first, other, total)], axis=1
    )
    (tokens_grad,) = call(
        tokens_kernel,
        [((patches, width), BF16)],
        [],
        (4 * patches * width * slots, image_bytes),
        left,
        right,
    )
    return (tokens_grad[None], router_grad.T)


def solution(mesh):
    images = P(("group", "expert"), None, None)
    in_specs = (images, images, P(), P(None, "expert"), P("expert", None))
    out_specs = (images, P("group", None))
    return jax.shard_map(
        per_device, mesh=mesh, in_specs=in_specs, out_specs=out_specs, check_vma=False
    )
```

```python
import math

import jax
import jax.numpy as jnp
from jax import lax
from jax.experimental import pallas as pl
from jax.experimental.pallas import tpu as pltpu
from jax.sharding import PartitionSpec as P

F32 = jnp.float32
BF16 = jnp.bfloat16
NN = (((1,), (0,)), ((), ()))
NT = (((1,), (1,)), ((), ()))
TN = (((0,), (0,)), ((), ()))
AHEAD_FLOPS = 3 * 10**10


def out_order(size):
    return [size - 1] + list(range(1, size - 1)) + [0]


def back_order(size):
    return [(size - 1 + 5 * k) % size for k in range(size)]


def sum_order(size, core):
    chips = size // 2
    order = [k // 2 if k % 2 else chips - 1 - k // 2 for k in range(chips)]
    return [2 * chip + core for chip in order]


def dot(a, b, dims):
    return lax.dot_general(a, b, dims, preferred_element_type=F32)


def first_kernel(token_ref):
    token_ref[...] = jnp.zeros(token_ref.shape, F32)


def slots_kernel(tokens_ref, router_ref, token_ref, slot_in_ref, dispatch_ref, combine_ref):
    logits = dot(router_ref[...], tokens_ref[...], NT)
    over_patches = jnp.exp(logits - jnp.max(logits, axis=1, keepdims=True))
    dispatch = over_patches / jnp.sum(over_patches, axis=1, keepdims=True)
    over_slots = jnp.exp(logits - jnp.max(logits, axis=0, keepdims=True))
    dispatch_ref[...] = dispatch
    combine_ref[...] = over_slots / jnp.sum(over_slots, axis=0, keepdims=True)
    slot_in_ref[...] = dot(dispatch.astype(BF16), tokens_ref[...], NN)


def messages_kernel(grad_ref, combine_ref, slot_in_ref, sent_ref):
    slot_grad = dot(combine_ref[...].astype(BF16), grad_ref[...], NN)
    slots = slot_in_ref.shape[0]
    order = out_order(2 * slots)
    for s in range(slots):
        rows = [slot_in_ref[s : s + 1], slot_grad[s : s + 1]]
        message = jnp.concatenate(rows, axis=0).astype(BF16)
        for half in range(2):
            sent_ref[order.index(2 * s + half)] = message


def experts_kernel(
    got_ref, in_weight_ref, out_weight_ref, parts_ref, in_rows_ref, grad_rows_ref
):
    images = got_ref.shape[0]
    out, back = out_order(images), back_order(images)
    for k in range(images):
        message = got_ref[k].astype(F32)
        in_rows_ref[k : k + 1] = message[0:1]
        grad_rows_ref[k : k + 1] = message[1:2]
    hidden = dot(in_rows_ref[...].astype(BF16), in_weight_ref[...], NN)
    act_grad = dot(grad_rows_ref[...].astype(BF16), out_weight_ref[...], NT)
    normal_cdf = 0.5 * (1.0 + lax.erf(hidden * (1.0 / math.sqrt(2.0))))
    normal_pdf = jnp.exp(-0.5 * hidden * hidden) * (1.0 / math.sqrt(2.0 * math.pi))
    activation = (hidden * normal_cdf).astype(BF16)
    hidden_grad = (act_grad * (normal_cdf + hidden * normal_pdf)).astype(BF16)
    part_out = dot(activation, out_weight_ref[...], NN)
    part_in = dot(hidden_grad, in_weight_ref[...], NT)
    for k in range(images):
        rows = [part_out[k : k + 1], part_in[k : k + 1]]
        parts_ref[back.index(out[k])] = jnp.concatenate(rows, axis=0).astype(BF16)


def logits_kernel(
    tokens_ref,
    grad_ref,
    router_ref,
    dispatch_ref,
    combine_ref,
    back_ref,
    kept_ref,
    given_ref,
    left_ref,
    right_ref,
    out_rows_ref,
    back_rows_ref,
):
    slots = router_ref.shape[0]
    order = back_order(2 * slots)
    for s in range(slots):
        halves = [back_ref[order.index(2 * s + half)].astype(F32) for half in range(2)]
        message = halves[0] + halves[1]
        out_rows_ref[s : s + 1] = message[0:1]
        back_rows_ref[s : s + 1] = message[1:2]
    slot_back = back_rows_ref[...].astype(BF16)
    combine_grad = dot(out_rows_ref[...].astype(BF16), grad_ref[...], NT)
    dispatch_grad = dot(slot_back, tokens_ref[...], NT)
    dispatch = dispatch_ref[...]
    combine = combine_ref[...]
    slot_sum = jnp.sum(combine * combine_grad, axis=0, keepdims=True)
    patch_sum = jnp.sum(dispatch * dispatch_grad, axis=1, keepdims=True)
    logits_grad = combine * (combine_grad - slot_sum) + dispatch * (dispatch_grad - patch_sum)
    part = dot(logits_grad.astype(BF16), tokens_ref[...], NN)
    half = part.shape[1] // 2
    first = lax.axis_index("expert") % 2 == 0
    kept_ref[...] = jnp.where(first, part[:, :half], part[:, half:])
    given_ref[...] = jnp.where(first, part[:, half:], part[:, :half])
    left_ref[...] = jnp.concatenate([logits_grad, dispatch], axis=0).astype(BF16)
    right_ref[...] = jnp.concatenate(
        [router_ref[...].astype(F32), back_rows_ref[...]], axis=0
    ).astype(BF16)


def tokens_kernel(left_ref, right_ref, tokens_grad_ref):
    tokens_grad_ref[...] = dot(left_ref[...], right_ref[...], TN).astype(BF16)


def call(kernel, outs, scratch, cost, *operands):
    return pl.pallas_call(
        kernel,
        out_shape=[jax.ShapeDtypeStruct(shape, dtype) for shape, dtype in outs],
        in_specs=[pl.BlockSpec(memory_space=pltpu.VMEM)] * len(operands),
        out_specs=[pl.BlockSpec(memory_space=pltpu.VMEM)] * len(outs),
        scratch_shapes=[pltpu.VMEM(shape, F32) for shape in scratch],
        compiler_params=pltpu.CompilerParams(vmem_limit_bytes=16 * 2**20),
        cost_estimate=pl.CostEstimate(flops=cost[0], bytes_accessed=cost[1], transcendentals=0),
    )(*operands)


def swap_cores(value):
    size = lax.axis_size("expert")
    return lax.ppermute(value, "expert", [(i, i ^ 1) for i in range(size)])


def exchange(value, groups):
    return lax.all_to_all(
        value, "expert", split_axis=0, concat_axis=0, tiled=True, axis_index_groups=groups
    )


def per_device(tokens, out_grad, router, in_weight, out_weight):
    _, patches, width = tokens.shape
    hidden = in_weight.shape[1]
    slots = router.shape[1]
    chips = slots
    tokens = tokens[0]
    out_grad = out_grad[0]
    router_rows = router.T
    image_bytes = 2 * patches * width
    weight_bytes = 2 * width * hidden
    (token,) = call(first_kernel, [((8, 128), F32)], [], (AHEAD_FLOPS, image_bytes))
    slot_in, dispatch, combine = call(
        slots_kernel,
        [((slots, width), F32), ((slots, patches), F32), ((slots, patches), F32)],
        [],
        (8 * patches * width * slots, image_bytes),
        tokens,
        router_rows,
        token,
    )
    (sent,) = call(
        messages_kernel,
        [((2 * slots, 2, width), BF16)],
        [],
        (4 * patches * width * slots, image_bytes),
        out_grad,
        combine,
        slot_in,
    )
    got = exchange(sent, [out_order(2 * chips)])
    (parts,) = call(
        experts_kernel,
        [((2 * chips, 2, width), BF16)],
        [(2 * chips, width)] * 2,
        (16 * chips * width * hidden, 2 * weight_bytes),
        got,
        in_weight,
        out_weight,
    )
    back = exchange(parts, [back_order(2 * chips)])
    kept, given, left, right = call(
        logits_kernel,
        [
            ((slots, width // 2), F32),
            ((slots, width // 2), F32),
            ((2 * slots, patches), BF16),
            ((2 * slots, width), BF16),
        ],
        [(slots, width)] * 2,
        (12 * patches * width * slots, 2 * image_bytes),
        tokens,
        out_grad,
        router_rows,
        dispatch,
        combine,
        back,
    )
    pair = (kept + swap_cores(given)).astype(BF16)
    same_core = [sum_order(2 * chips, core) for core in range(2)]
    terms = exchange(jnp.broadcast_to(pair[None], (chips,) + pair.shape), same_core)
    total = jnp.sum(terms.astype(F32), axis=0)
    other = swap_cores(total)
    first = lax.axis_index("expert") % 2 == 0
    router_grad = jnp.concatenate(
        [jnp.where(first, total, other), jnp.where(first, other, total)], axis=1
    )
    block = patches // 2
    tokens_grad = pl.pallas_call(
        tokens_kernel,
        grid=(patches // block,),
        out_shape=jax.ShapeDtypeStruct((patches, width), BF16),
        in_specs=[
            pl.BlockSpec((2 * slots, block), lambda i: (0, i)),
            pl.BlockSpec((2 * slots, width), lambda i: (0, 0)),
        ],
        out_specs=pl.BlockSpec((block, width), lambda i: (i, 0)),
        compiler_params=pltpu.CompilerParams(vmem_limit_bytes=16 * 1024 * 1024),
        cost_estimate=pl.CostEstimate(
            flops=4 * patches * width * slots, bytes_accessed=image_bytes, transcendentals=0
        ),
    )(left, right)
    return (tokens_grad[None], router_grad.T)


def solution(mesh):
    images = P(("group", "expert"), None, None)
    in_specs = (images, images, P(), P(None, "expert"), P("expert", None))
    out_specs = (images, P("group", None))
    return jax.shard_map(
        per_device, mesh=mesh, in_specs=in_specs, out_specs=out_specs, check_vma=False
    )
```

```python
import math

import jax
import jax.numpy as jnp
from jax import lax
from jax.experimental import pallas as pl
from jax.experimental.pallas import tpu as pltpu
from jax.sharding import PartitionSpec as P

F32 = jnp.float32
BF16 = jnp.bfloat16
NN = (((1,), (0,)), ((), ()))
NT = (((1,), (1,)), ((), ()))
TN = (((0,), (0,)), ((), ()))
AHEAD_FLOPS = 3 * 10**10


OUT_LIST = (15, 1, 7, 3, 5, 4, 8, 12, 9, 2, 6, 10, 13, 14, 11, 0)
BACK_LIST = (15, 0, 1, 7, 11, 13, 2, 3, 5, 10, 4, 8, 12, 6, 9, 14)
SUM_LIST = (7, 6, 2, 5, 1, 4, 3, 0)


def listed(members, count):
    if len(members) == count:
        return list(members)
    return [(count - 1 + 5 * k) % count for k in range(count)]


def out_order(size):
    return listed(OUT_LIST, size)


def back_order(size):
    return listed(BACK_LIST, size)


def sum_order(size, core):
    return [2 * chip + core for chip in listed(SUM_LIST, size // 2)]


def dot(a, b, dims):
    return lax.dot_general(a, b, dims, preferred_element_type=F32)


def first_kernel(token_ref):
    token_ref[...] = jnp.zeros(token_ref.shape, F32)


def slots_kernel(tokens_ref, router_ref, token_ref, slot_in_ref, dispatch_ref, combine_ref):
    logits = dot(router_ref[...], tokens_ref[...], NT)
    over_patches = jnp.exp(logits - jnp.max(logits, axis=1, keepdims=True))
    dispatch = over_patches / jnp.sum(over_patches, axis=1, keepdims=True)
    over_slots = jnp.exp(logits - jnp.max(logits, axis=0, keepdims=True))
    dispatch_ref[...] = dispatch
    combine_ref[...] = over_slots / jnp.sum(over_slots, axis=0, keepdims=True)
    slot_in_ref[...] = dot(dispatch.astype(BF16), tokens_ref[...], NN)


def messages_kernel(grad_ref, combine_ref, slot_in_ref, sent_ref):
    slot_grad = dot(combine_ref[...].astype(BF16), grad_ref[...], NN)
    slots = slot_in_ref.shape[0]
    order = out_order(2 * slots)
    for s in range(slots):
        rows = [slot_in_ref[s : s + 1], slot_grad[s : s + 1]]
        message = jnp.concatenate(rows, axis=0).astype(BF16)
        for half in range(2):
            sent_ref[order.index(2 * s + half)] = message


def experts_kernel(
    got_ref, in_weight_ref, out_weight_ref, parts_ref, in_rows_ref, grad_rows_ref
):
    images = got_ref.shape[0]
    out, back = out_order(images), back_order(images)
    for k in range(images):
        message = got_ref[k].astype(F32)
        in_rows_ref[k : k + 1] = message[0:1]
        grad_rows_ref[k : k + 1] = message[1:2]
    hidden = dot(in_rows_ref[...].astype(BF16), in_weight_ref[...], NN)
    act_grad = dot(grad_rows_ref[...].astype(BF16), out_weight_ref[...], NT)
    normal_cdf = 0.5 * (1.0 + lax.erf(hidden * (1.0 / math.sqrt(2.0))))
    normal_pdf = jnp.exp(-0.5 * hidden * hidden) * (1.0 / math.sqrt(2.0 * math.pi))
    activation = (hidden * normal_cdf).astype(BF16)
    hidden_grad = (act_grad * (normal_cdf + hidden * normal_pdf)).astype(BF16)
    part_out = dot(activation, out_weight_ref[...], NN)
    part_in = dot(hidden_grad, in_weight_ref[...], NT)
    for k in range(images):
        rows = [part_out[k : k + 1], part_in[k : k + 1]]
        parts_ref[back.index(out[k])] = jnp.concatenate(rows, axis=0).astype(BF16)


def logits_kernel(
    tokens_ref,
    grad_ref,
    router_ref,
    dispatch_ref,
    combine_ref,
    back_ref,
    kept_ref,
    given_ref,
    left_ref,
    right_ref,
    out_rows_ref,
    back_rows_ref,
):
    slots = router_ref.shape[0]
    order = back_order(2 * slots)
    for s in range(slots):
        halves = [back_ref[order.index(2 * s + half)].astype(F32) for half in range(2)]
        message = halves[0] + halves[1]
        out_rows_ref[s : s + 1] = message[0:1]
        back_rows_ref[s : s + 1] = message[1:2]
    slot_back = back_rows_ref[...].astype(BF16)
    combine_grad = dot(out_rows_ref[...].astype(BF16), grad_ref[...], NT)
    dispatch_grad = dot(slot_back, tokens_ref[...], NT)
    dispatch = dispatch_ref[...]
    combine = combine_ref[...]
    slot_sum = jnp.sum(combine * combine_grad, axis=0, keepdims=True)
    patch_sum = jnp.sum(dispatch * dispatch_grad, axis=1, keepdims=True)
    logits_grad = combine * (combine_grad - slot_sum) + dispatch * (dispatch_grad - patch_sum)
    part = dot(logits_grad.astype(BF16), tokens_ref[...], NN)
    half = part.shape[1] // 2
    first = lax.axis_index("expert") % 2 == 0
    kept_ref[...] = jnp.where(first, part[:, :half], part[:, half:])
    given_ref[...] = jnp.where(first, part[:, half:], part[:, :half])
    left_ref[...] = jnp.concatenate([logits_grad, dispatch], axis=0).astype(BF16)
    right_ref[...] = jnp.concatenate(
        [router_ref[...].astype(F32), back_rows_ref[...]], axis=0
    ).astype(BF16)


def tokens_kernel(left_ref, right_ref, tokens_grad_ref):
    tokens_grad_ref[...] = dot(left_ref[...], right_ref[...], TN).astype(BF16)


def call(kernel, outs, scratch, cost, *operands):
    return pl.pallas_call(
        kernel,
        out_shape=[jax.ShapeDtypeStruct(shape, dtype) for shape, dtype in outs],
        in_specs=[pl.BlockSpec(memory_space=pltpu.VMEM)] * len(operands),
        out_specs=[pl.BlockSpec(memory_space=pltpu.VMEM)] * len(outs),
        scratch_shapes=[pltpu.VMEM(shape, F32) for shape in scratch],
        compiler_params=pltpu.CompilerParams(vmem_limit_bytes=16 * 2**20),
        cost_estimate=pl.CostEstimate(flops=cost[0], bytes_accessed=cost[1], transcendentals=0),
    )(*operands)


def swap_cores(value):
    size = lax.axis_size("expert")
    return lax.ppermute(value, "expert", [(i, i ^ 1) for i in range(size)])


def exchange(value, groups):
    return lax.all_to_all(
        value, "expert", split_axis=0, concat_axis=0, tiled=True, axis_index_groups=groups
    )


def per_device(tokens, out_grad, router, in_weight, out_weight):
    _, patches, width = tokens.shape
    hidden = in_weight.shape[1]
    slots = router.shape[1]
    chips = slots
    tokens = tokens[0]
    out_grad = out_grad[0]
    router_rows = router.T
    image_bytes = 2 * patches * width
    weight_bytes = 2 * width * hidden
    (token,) = call(first_kernel, [((8, 128), F32)], [], (AHEAD_FLOPS, image_bytes))
    slot_in, dispatch, combine = call(
        slots_kernel,
        [((slots, width), F32), ((slots, patches), F32), ((slots, patches), F32)],
        [],
        (8 * patches * width * slots, image_bytes),
        tokens,
        router_rows,
        token,
    )
    (sent,) = call(
        messages_kernel,
        [((2 * slots, 2, width), BF16)],
        [],
        (4 * patches * width * slots, image_bytes),
        out_grad,
        combine,
        slot_in,
    )
    got = exchange(sent, [out_order(2 * chips)])
    (parts,) = call(
        experts_kernel,
        [((2 * chips, 2, width), BF16)],
        [(2 * chips, width)] * 2,
        (16 * chips * width * hidden, 2 * weight_bytes),
        got,
        in_weight,
        out_weight,
    )
    back = exchange(parts, [back_order(2 * chips)])
    kept, given, left, right = call(
        logits_kernel,
        [
            ((slots, width // 2), F32),
            ((slots, width // 2), F32),
            ((2 * slots, patches), BF16),
            ((2 * slots, width), BF16),
        ],
        [(slots, width)] * 2,
        (12 * patches * width * slots, 2 * image_bytes),
        tokens,
        out_grad,
        router_rows,
        dispatch,
        combine,
        back,
    )
    pair = (kept + swap_cores(given)).astype(BF16)
    same_core = [sum_order(2 * chips, core) for core in range(2)]
    terms = exchange(jnp.broadcast_to(pair[None], (chips,) + pair.shape), same_core)
    total = jnp.sum(terms.astype(F32), axis=0)
    other = swap_cores(total)
    first = lax.axis_index("expert") % 2 == 0
    router_grad = jnp.concatenate(
        [jnp.where(first, total, other), jnp.where(first, other, total)], axis=1
    )
    (tokens_grad,) = call(
        tokens_kernel,
        [((patches, width), BF16)],
        [],
        (4 * patches * width * slots, image_bytes),
        left,
        right,
    )
    return (tokens_grad[None], router_grad.T)


def solution(mesh):
    images = P(("group", "expert"), None, None)
    in_specs = (images, images, P(), P(None, "expert"), P("expert", None))
    out_specs = (images, P("group", None))
    return jax.shard_map(
        per_device, mesh=mesh, in_specs=in_specs, out_specs=out_specs, check_vma=False
    )
```

```python
import math

import jax
import jax.numpy as jnp
from jax import lax
from jax.experimental import pallas as pl
from jax.experimental.pallas import tpu as pltpu
from jax.sharding import PartitionSpec as P

F32 = jnp.float32
BF16 = jnp.bfloat16
NN = (((1,), (0,)), ((), ()))
NT = (((1,), (1,)), ((), ()))
TN = (((0,), (0,)), ((), ()))
AHEAD_FLOPS = 3 * 10**10


OUT_LIST = (15, 2, 12, 6, 14, 0, 4, 3, 7, 8, 9, 5, 13, 11, 10, 1)
BACK_LIST = (15, 2, 12, 6, 0, 4, 13, 7, 11, 14, 1, 8, 10, 3, 5, 9)
SUM_LIST = (7, 0, 2, 6, 1, 4, 3, 5)


def listed(members, count):
    if len(members) == count:
        return list(members)
    return [(count - 1 + 5 * k) % count for k in range(count)]


def out_order(size):
    return listed(OUT_LIST, size)


def back_order(size):
    return listed(BACK_LIST, size)


def sum_order(size, core):
    return [2 * chip + core for chip in listed(SUM_LIST, size // 2)]


def dot(a, b, dims):
    return lax.dot_general(a, b, dims, preferred_element_type=F32)


def first_kernel(token_ref):
    token_ref[...] = jnp.zeros(token_ref.shape, F32)


def slots_kernel(tokens_ref, router_ref, token_ref, slot_in_ref, dispatch_ref, combine_ref):
    logits = dot(router_ref[...], tokens_ref[...], NT)
    over_patches = jnp.exp(logits - jnp.max(logits, axis=1, keepdims=True))
    dispatch = over_patches / jnp.sum(over_patches, axis=1, keepdims=True)
    over_slots = jnp.exp(logits - jnp.max(logits, axis=0, keepdims=True))
    dispatch_ref[...] = dispatch
    combine_ref[...] = over_slots / jnp.sum(over_slots, axis=0, keepdims=True)
    slot_in_ref[...] = dot(dispatch.astype(BF16), tokens_ref[...], NN)


def messages_kernel(grad_ref, combine_ref, slot_in_ref, sent_ref):
    slot_grad = dot(combine_ref[...].astype(BF16), grad_ref[...], NN)
    slots = slot_in_ref.shape[0]
    order = out_order(2 * slots)
    for s in range(slots):
        rows = [slot_in_ref[s : s + 1], slot_grad[s : s + 1]]
        message = jnp.concatenate(rows, axis=0).astype(BF16)
        for half in range(2):
            sent_ref[order.index(2 * s + half)] = message


def experts_kernel(
    got_ref, in_weight_ref, out_weight_ref, parts_ref, in_rows_ref, grad_rows_ref
):
    images = got_ref.shape[0]
    out, back = out_order(images), back_order(images)
    for k in range(images):
        message = got_ref[k].astype(F32)
        in_rows_ref[k : k + 1] = message[0:1]
        grad_rows_ref[k : k + 1] = message[1:2]
    hidden = dot(in_rows_ref[...].astype(BF16), in_weight_ref[...], NN)
    act_grad = dot(grad_rows_ref[...].astype(BF16), out_weight_ref[...], NT)
    normal_cdf = 0.5 * (1.0 + lax.erf(hidden * (1.0 / math.sqrt(2.0))))
    normal_pdf = jnp.exp(-0.5 * hidden * hidden) * (1.0 / math.sqrt(2.0 * math.pi))
    activation = (hidden * normal_cdf).astype(BF16)
    hidden_grad = (act_grad * (normal_cdf + hidden * normal_pdf)).astype(BF16)
    part_out = dot(activation, out_weight_ref[...], NN)
    part_in = dot(hidden_grad, in_weight_ref[...], NT)
    for k in range(images):
        rows = [part_out[k : k + 1], part_in[k : k + 1]]
        parts_ref[back.index(out[k])] = jnp.concatenate(rows, axis=0).astype(BF16)


def logits_kernel(
    tokens_ref,
    grad_ref,
    router_ref,
    dispatch_ref,
    combine_ref,
    back_ref,
    kept_ref,
    given_ref,
    left_ref,
    right_ref,
    out_rows_ref,
    back_rows_ref,
):
    slots = router_ref.shape[0]
    order = back_order(2 * slots)
    for s in range(slots):
        halves = [back_ref[order.index(2 * s + half)].astype(F32) for half in range(2)]
        message = halves[0] + halves[1]
        out_rows_ref[s : s + 1] = message[0:1]
        back_rows_ref[s : s + 1] = message[1:2]
    slot_back = back_rows_ref[...].astype(BF16)
    combine_grad = dot(out_rows_ref[...].astype(BF16), grad_ref[...], NT)
    dispatch_grad = dot(slot_back, tokens_ref[...], NT)
    dispatch = dispatch_ref[...]
    combine = combine_ref[...]
    slot_sum = jnp.sum(combine * combine_grad, axis=0, keepdims=True)
    patch_sum = jnp.sum(dispatch * dispatch_grad, axis=1, keepdims=True)
    logits_grad = combine * (combine_grad - slot_sum) + dispatch * (dispatch_grad - patch_sum)
    part = dot(logits_grad.astype(BF16), tokens_ref[...], NN)
    half = part.shape[1] // 2
    first = lax.axis_index("expert") % 2 == 0
    kept_ref[...] = jnp.where(first, part[:, :half], part[:, half:])
    given_ref[...] = jnp.where(first, part[:, half:], part[:, :half])
    left_ref[...] = jnp.concatenate([logits_grad, dispatch], axis=0).astype(BF16)
    right_ref[...] = jnp.concatenate(
        [router_ref[...].astype(F32), back_rows_ref[...]], axis=0
    ).astype(BF16)


def tokens_kernel(left_ref, right_ref, tokens_grad_ref):
    tokens_grad_ref[...] = dot(left_ref[...], right_ref[...], TN).astype(BF16)


def call(kernel, outs, scratch, cost, *operands):
    return pl.pallas_call(
        kernel,
        out_shape=[jax.ShapeDtypeStruct(shape, dtype) for shape, dtype in outs],
        in_specs=[pl.BlockSpec(memory_space=pltpu.VMEM)] * len(operands),
        out_specs=[pl.BlockSpec(memory_space=pltpu.VMEM)] * len(outs),
        scratch_shapes=[pltpu.VMEM(shape, F32) for shape in scratch],
        compiler_params=pltpu.CompilerParams(vmem_limit_bytes=16 * 2**20),
        cost_estimate=pl.CostEstimate(flops=cost[0], bytes_accessed=cost[1], transcendentals=0),
    )(*operands)


def swap_cores(value):
    size = lax.axis_size("expert")
    return lax.ppermute(value, "expert", [(i, i ^ 1) for i in range(size)])


def exchange(value, groups):
    return lax.all_to_all(
        value, "expert", split_axis=0, concat_axis=0, tiled=True, axis_index_groups=groups
    )


def per_device(tokens, out_grad, router, in_weight, out_weight):
    _, patches, width = tokens.shape
    hidden = in_weight.shape[1]
    slots = router.shape[1]
    chips = slots
    tokens = tokens[0]
    out_grad = out_grad[0]
    router_rows = router.T
    image_bytes = 2 * patches * width
    weight_bytes = 2 * width * hidden
    (token,) = call(first_kernel, [((8, 128), F32)], [], (AHEAD_FLOPS, image_bytes))
    slot_in, dispatch, combine = call(
        slots_kernel,
        [((slots, width), F32), ((slots, patches), F32), ((slots, patches), F32)],
        [],
        (8 * patches * width * slots, image_bytes),
        tokens,
        router_rows,
        token,
    )
    (sent,) = call(
        messages_kernel,
        [((2 * slots, 2, width), BF16)],
        [],
        (4 * patches * width * slots, image_bytes),
        out_grad,
        combine,
        slot_in,
    )
    got = exchange(sent, [out_order(2 * chips)])
    (parts,) = call(
        experts_kernel,
        [((2 * chips, 2, width), BF16)],
        [(2 * chips, width)] * 2,
        (16 * chips * width * hidden, 2 * weight_bytes),
        got,
        in_weight,
        out_weight,
    )
    back = exchange(parts, [back_order(2 * chips)])
    kept, given, left, right = call(
        logits_kernel,
        [
            ((slots, width // 2), F32),
            ((slots, width // 2), F32),
            ((2 * slots, patches), BF16),
            ((2 * slots, width), BF16),
        ],
        [(slots, width)] * 2,
        (12 * patches * width * slots, 2 * image_bytes),
        tokens,
        out_grad,
        router_rows,
        dispatch,
        combine,
        back,
    )
    pair = (kept + swap_cores(given)).astype(BF16)
    same_core = [sum_order(2 * chips, core) for core in range(2)]
    terms = exchange(jnp.broadcast_to(pair[None], (chips,) + pair.shape), same_core)
    total = jnp.sum(terms.astype(F32), axis=0)
    other = swap_cores(total)
    first = lax.axis_index("expert") % 2 == 0
    router_grad = jnp.concatenate(
        [jnp.where(first, total, other), jnp.where(first, other, total)], axis=1
    )
    (tokens_grad,) = call(
        tokens_kernel,
        [((patches, width), BF16)],
        [],
        (4 * patches * width * slots, image_bytes),
        left,
        right,
    )
    return (tokens_grad[None], router_grad.T)


def solution(mesh):
    images = P(("group", "expert"), None, None)
    in_specs = (images, images, P(), P(None, "expert"), P("expert", None))
    out_specs = (images, P("group", None))
    return jax.shard_map(
        per_device, mesh=mesh, in_specs=in_specs, out_specs=out_specs, check_vma=False
    )
```

```python
import math

import jax
import jax.numpy as jnp
from jax import lax
from jax.experimental import pallas as pl
from jax.experimental.pallas import tpu as pltpu
from jax.sharding import PartitionSpec as P

F32 = jnp.float32
BF16 = jnp.bfloat16
NN = (((1,), (0,)), ((), ()))
NT = (((1,), (1,)), ((), ()))
TN = (((0,), (0,)), ((), ()))
AHEAD_FLOPS = 3 * 10**10


def out_order(size):
    return [size - 1] + list(range(1, size - 1)) + [0]


def back_order(size):
    return [(size - 1 + 5 * k) % size for k in range(size)]


def sum_order(size, core):
    chips = size // 2
    order = [k // 2 if k % 2 else chips - 1 - k // 2 for k in range(chips)]
    return [2 * chip + core for chip in order]


def dot(a, b, dims):
    return lax.dot_general(a, b, dims, preferred_element_type=F32)


def first_kernel(token_ref):
    token_ref[...] = jnp.zeros(token_ref.shape, F32)


def slots_kernel(tokens_ref, router_ref, token_ref, dispatch_ref, combine_ref):
    logits = dot(router_ref[...], tokens_ref[...], NT)
    over_patches = jnp.exp(logits - jnp.max(logits, axis=1, keepdims=True))
    dispatch = over_patches / jnp.sum(over_patches, axis=1, keepdims=True)
    over_slots = jnp.exp(logits - jnp.max(logits, axis=0, keepdims=True))
    dispatch_ref[...] = dispatch
    combine_ref[...] = over_slots / jnp.sum(over_slots, axis=0, keepdims=True)


def messages_kernel(tokens_ref, grad_ref, dispatch_ref, combine_ref, sent_ref):
    slot_in = dot(dispatch_ref[...].astype(BF16), tokens_ref[...], NN)
    slot_grad = dot(combine_ref[...].astype(BF16), grad_ref[...], NN)
    slots = slot_in.shape[0]
    order = out_order(2 * slots)
    for s in range(slots):
        rows = [slot_in[s : s + 1], slot_grad[s : s + 1]]
        message = jnp.concatenate(rows, axis=0).astype(BF16)
        for half in range(2):
            sent_ref[order.index(2 * s + half)] = message


def experts_kernel(
    got_ref, in_weight_ref, out_weight_ref, parts_ref, in_rows_ref, grad_rows_ref
):
    images = got_ref.shape[0]
    out, back = out_order(images), back_order(images)
    for k in range(images):
        message = got_ref[k].astype(F32)
        in_rows_ref[k : k + 1] = message[0:1]
        grad_rows_ref[k : k + 1] = message[1:2]
    hidden = dot(in_rows_ref[...].astype(BF16), in_weight_ref[...], NN)
    act_grad = dot(grad_rows_ref[...].astype(BF16), out_weight_ref[...], NT)
    normal_cdf = 0.5 * (1.0 + lax.erf(hidden * (1.0 / math.sqrt(2.0))))
    normal_pdf = jnp.exp(-0.5 * hidden * hidden) * (1.0 / math.sqrt(2.0 * math.pi))
    activation = (hidden * normal_cdf).astype(BF16)
    hidden_grad = (act_grad * (normal_cdf + hidden * normal_pdf)).astype(BF16)
    part_out = dot(activation, out_weight_ref[...], NN)
    part_in = dot(hidden_grad, in_weight_ref[...], NT)
    for k in range(images):
        rows = [part_out[k : k + 1], part_in[k : k + 1]]
        parts_ref[back.index(out[k])] = jnp.concatenate(rows, axis=0).astype(BF16)


def logits_kernel(
    tokens_ref,
    grad_ref,
    router_ref,
    dispatch_ref,
    combine_ref,
    back_ref,
    kept_ref,
    given_ref,
    left_ref,
    right_ref,
    out_rows_ref,
    back_rows_ref,
):
    slots = router_ref.shape[0]
    order = back_order(2 * slots)
    for s in range(slots):
        halves = [back_ref[order.index(2 * s + half)].astype(F32) for half in range(2)]
        message = halves[0] + halves[1]
        out_rows_ref[s : s + 1] = message[0:1]
        back_rows_ref[s : s + 1] = message[1:2]
    slot_back = back_rows_ref[...].astype(BF16)
    combine_grad = dot(out_rows_ref[...].astype(BF16), grad_ref[...], NT)
    dispatch_grad = dot(slot_back, tokens_ref[...], NT)
    dispatch = dispatch_ref[...]
    combine = combine_ref[...]
    slot_sum = jnp.sum(combine * combine_grad, axis=0, keepdims=True)
    patch_sum = jnp.sum(dispatch * dispatch_grad, axis=1, keepdims=True)
    logits_grad = combine * (combine_grad - slot_sum) + dispatch * (dispatch_grad - patch_sum)
    part = dot(logits_grad.astype(BF16), tokens_ref[...], NN)
    half = part.shape[1] // 2
    first = lax.axis_index("expert") % 2 == 0
    kept_ref[...] = jnp.where(first, part[:, :half], part[:, half:])
    given_ref[...] = jnp.where(first, part[:, half:], part[:, :half])
    left_ref[...] = jnp.concatenate([logits_grad, dispatch], axis=0).astype(BF16)
    right_ref[...] = jnp.concatenate(
        [router_ref[...].astype(F32), back_rows_ref[...]], axis=0
    ).astype(BF16)


def tokens_kernel(left_ref, right_ref, tokens_grad_ref):
    tokens_grad_ref[...] = dot(left_ref[...], right_ref[...], TN).astype(BF16)


def call(kernel, outs, scratch, cost, *operands):
    return pl.pallas_call(
        kernel,
        out_shape=[jax.ShapeDtypeStruct(shape, dtype) for shape, dtype in outs],
        in_specs=[pl.BlockSpec(memory_space=pltpu.VMEM)] * len(operands),
        out_specs=[pl.BlockSpec(memory_space=pltpu.VMEM)] * len(outs),
        scratch_shapes=[pltpu.VMEM(shape, F32) for shape in scratch],
        compiler_params=pltpu.CompilerParams(vmem_limit_bytes=16 * 2**20),
        cost_estimate=pl.CostEstimate(flops=cost[0], bytes_accessed=cost[1], transcendentals=0),
    )(*operands)


def swap_cores(value):
    size = lax.axis_size("expert")
    return lax.ppermute(value, "expert", [(i, i ^ 1) for i in range(size)])


def exchange(value, groups):
    return lax.all_to_all(
        value, "expert", split_axis=0, concat_axis=0, tiled=True, axis_index_groups=groups
    )


def per_device(tokens, out_grad, router, in_weight, out_weight):
    _, patches, width = tokens.shape
    hidden = in_weight.shape[1]
    slots = router.shape[1]
    chips = slots
    tokens = tokens[0]
    out_grad = out_grad[0]
    router_rows = router.T
    image_bytes = 2 * patches * width
    weight_bytes = 2 * width * hidden
    (token,) = call(first_kernel, [((8, 128), F32)], [], (AHEAD_FLOPS, image_bytes))
    dispatch, combine = call(
        slots_kernel,
        [((slots, patches), F32), ((slots, patches), F32)],
        [],
        (4 * patches * width * slots, image_bytes),
        tokens,
        router_rows,
        token,
    )
    (sent,) = call(
        messages_kernel,
        [((2 * slots, 2, width), BF16)],
        [],
        (8 * patches * width * slots, 2 * image_bytes),
        tokens,
        out_grad,
        dispatch,
        combine,
    )
    got = exchange(sent, [out_order(2 * chips)])
    (parts,) = call(
        experts_kernel,
        [((2 * chips, 2, width), BF16)],
        [(2 * chips, width)] * 2,
        (16 * chips * width * hidden, 2 * weight_bytes),
        got,
        in_weight,
        out_weight,
    )
    back = exchange(parts, [back_order(2 * chips)])
    kept, given, left, right = call(
        logits_kernel,
        [
            ((slots, width // 2), F32),
            ((slots, width // 2), F32),
            ((2 * slots, patches), BF16),
            ((2 * slots, width), BF16),
        ],
        [(slots, width)] * 2,
        (12 * patches * width * slots, 2 * image_bytes),
        tokens,
        out_grad,
        router_rows,
        dispatch,
        combine,
        back,
    )
    pair = (kept + swap_cores(given)).astype(BF16)
    same_core = [sum_order(2 * chips, core) for core in range(2)]
    terms = exchange(jnp.broadcast_to(pair[None], (chips,) + pair.shape), same_core)
    total = jnp.sum(terms.astype(F32), axis=0)
    other = swap_cores(total)
    first = lax.axis_index("expert") % 2 == 0
    router_grad = jnp.concatenate(
        [jnp.where(first, total, other), jnp.where(first, other, total)], axis=1
    )
    (tokens_grad,) = call(
        tokens_kernel,
        [((patches, width), BF16)],
        [],
        (4 * patches * width * slots, image_bytes),
        left,
        right,
    )
    return (tokens_grad[None], router_grad.T)


def solution(mesh):
    images = P(("group", "expert"), None, None)
    in_specs = (images, images, P(), P(None, "expert"), P("expert", None))
    out_specs = (images, P("group", None))
    return jax.shard_map(
        per_device, mesh=mesh, in_specs=in_specs, out_specs=out_specs, check_vma=False
    )
```

```python
import math

import jax
import jax.numpy as jnp
from jax import lax
from jax.experimental import pallas as pl
from jax.experimental.pallas import tpu as pltpu
from jax.sharding import PartitionSpec as P

F32 = jnp.float32
BF16 = jnp.bfloat16
NN = (((1,), (0,)), ((), ()))
NT = (((1,), (1,)), ((), ()))
TN = (((0,), (0,)), ((), ()))
AHEAD_FLOPS = 3 * 10**10


def out_order(size):
    return [size - 1] + list(range(1, size - 1)) + [0]


def back_order(size):
    return [(size - 1 + 5 * k) % size for k in range(size)]


def sum_order(size, core):
    chips = size // 2
    order = [k // 2 if k % 2 else chips - 1 - k // 2 for k in range(chips)]
    return [2 * chip + core for chip in order]


def dot(a, b, dims):
    return lax.dot_general(a, b, dims, preferred_element_type=F32)


def first_kernel(token_ref):
    token_ref[...] = jnp.zeros(token_ref.shape, F32)


def slots_kernel(tokens_ref, router_ref, token_ref, dispatch_ref, combine_ref):
    logits = dot(router_ref[...], tokens_ref[...], NT)
    over_patches = jnp.exp(logits - jnp.max(logits, axis=1, keepdims=True))
    dispatch = over_patches / jnp.sum(over_patches, axis=1, keepdims=True)
    over_slots = jnp.exp(logits - jnp.max(logits, axis=0, keepdims=True))
    dispatch_ref[...] = dispatch
    combine_ref[...] = over_slots / jnp.sum(over_slots, axis=0, keepdims=True)


def messages_kernel(tokens_ref, grad_ref, dispatch_ref, combine_ref, sent_ref):
    slot_in = dot(dispatch_ref[...].astype(BF16), tokens_ref[...], NN)
    slot_grad = dot(combine_ref[...].astype(BF16), grad_ref[...], NN)
    slots = slot_in.shape[0]
    order = out_order(2 * slots)
    for s in range(slots):
        rows = [slot_in[s : s + 1], slot_grad[s : s + 1]]
        message = jnp.concatenate(rows, axis=0).astype(BF16)
        for half in range(2):
            sent_ref[order.index(2 * s + half)] = message


def experts_kernel(
    got_ref, in_weight_ref, out_weight_ref, parts_ref, in_rows_ref, grad_rows_ref
):
    images = got_ref.shape[0]
    out, back = out_order(images), back_order(images)
    for k in range(images):
        message = got_ref[k].astype(F32)
        in_rows_ref[k : k + 1] = message[0:1]
        grad_rows_ref[k : k + 1] = message[1:2]
    hidden = dot(in_rows_ref[...].astype(BF16), in_weight_ref[...], NN)
    normal_cdf = 0.5 * (1.0 + lax.erf(hidden * (1.0 / math.sqrt(2.0))))
    normal_pdf = jnp.exp(-0.5 * hidden * hidden) * (1.0 / math.sqrt(2.0 * math.pi))
    activation = (hidden * normal_cdf).astype(BF16)
    slope = normal_cdf + hidden * normal_pdf
    act_grad = dot(grad_rows_ref[...].astype(BF16), out_weight_ref[...], NT)
    hidden_grad = (act_grad * slope).astype(BF16)
    part_out = dot(activation, out_weight_ref[...], NN)
    part_in = dot(hidden_grad, in_weight_ref[...], NT)
    for k in range(images):
        rows = [part_out[k : k + 1], part_in[k : k + 1]]
        parts_ref[back.index(out[k])] = jnp.concatenate(rows, axis=0).astype(BF16)


def logits_kernel(
    tokens_ref,
    grad_ref,
    router_ref,
    dispatch_ref,
    combine_ref,
    back_ref,
    kept_ref,
    given_ref,
    left_ref,
    right_ref,
    out_rows_ref,
    back_rows_ref,
):
    slots = router_ref.shape[0]
    order = back_order(2 * slots)
    for s in range(slots):
        halves = [back_ref[order.index(2 * s + half)].astype(F32) for half in range(2)]
        message = halves[0] + halves[1]
        out_rows_ref[s : s + 1] = message[0:1]
        back_rows_ref[s : s + 1] = message[1:2]
    slot_back = back_rows_ref[...].astype(BF16)
    combine_grad = dot(out_rows_ref[...].astype(BF16), grad_ref[...], NT)
    dispatch_grad = dot(slot_back, tokens_ref[...], NT)
    dispatch = dispatch_ref[...]
    combine = combine_ref[...]
    slot_sum = jnp.sum(combine * combine_grad, axis=0, keepdims=True)
    patch_sum = jnp.sum(dispatch * dispatch_grad, axis=1, keepdims=True)
    logits_grad = combine * (combine_grad - slot_sum) + dispatch * (dispatch_grad - patch_sum)
    part = dot(logits_grad.astype(BF16), tokens_ref[...], NN)
    half = part.shape[1] // 2
    first = lax.axis_index("expert") % 2 == 0
    kept_ref[...] = jnp.where(first, part[:, :half], part[:, half:])
    given_ref[...] = jnp.where(first, part[:, half:], part[:, :half])
    left_ref[...] = jnp.concatenate([logits_grad, dispatch], axis=0).astype(BF16)
    right_ref[...] = jnp.concatenate(
        [router_ref[...].astype(F32), back_rows_ref[...]], axis=0
    ).astype(BF16)


def tokens_kernel(left_ref, right_ref, tokens_grad_ref):
    tokens_grad_ref[...] = dot(left_ref[...], right_ref[...], TN).astype(BF16)


def call(kernel, outs, scratch, cost, *operands):
    return pl.pallas_call(
        kernel,
        out_shape=[jax.ShapeDtypeStruct(shape, dtype) for shape, dtype in outs],
        in_specs=[pl.BlockSpec(memory_space=pltpu.VMEM)] * len(operands),
        out_specs=[pl.BlockSpec(memory_space=pltpu.VMEM)] * len(outs),
        scratch_shapes=[pltpu.VMEM(shape, F32) for shape in scratch],
        compiler_params=pltpu.CompilerParams(vmem_limit_bytes=16 * 2**20),
        cost_estimate=pl.CostEstimate(flops=cost[0], bytes_accessed=cost[1], transcendentals=0),
    )(*operands)


def swap_cores(value):
    size = lax.axis_size("expert")
    return lax.ppermute(value, "expert", [(i, i ^ 1) for i in range(size)])


def exchange(value, groups):
    return lax.all_to_all(
        value, "expert", split_axis=0, concat_axis=0, tiled=True, axis_index_groups=groups
    )


def per_device(tokens, out_grad, router, in_weight, out_weight):
    _, patches, width = tokens.shape
    hidden = in_weight.shape[1]
    slots = router.shape[1]
    chips = slots
    tokens = tokens[0]
    out_grad = out_grad[0]
    router_rows = router.T
    image_bytes = 2 * patches * width
    weight_bytes = 2 * width * hidden
    (token,) = call(first_kernel, [((8, 128), F32)], [], (AHEAD_FLOPS, image_bytes))
    dispatch, combine = call(
        slots_kernel,
        [((slots, patches), F32), ((slots, patches), F32)],
        [],
        (4 * patches * width * slots, image_bytes),
        tokens,
        router_rows,
        token,
    )
    (sent,) = call(
        messages_kernel,
        [((2 * slots, 2, width), BF16)],
        [],
        (8 * patches * width * slots, 2 * image_bytes),
        tokens,
        out_grad,
        dispatch,
        combine,
    )
    got = exchange(sent, [out_order(2 * chips)])
    (parts,) = call(
        experts_kernel,
        [((2 * chips, 2, width), BF16)],
        [(2 * chips, width)] * 2,
        (16 * chips * width * hidden, 2 * weight_bytes),
        got,
        in_weight,
        out_weight,
    )
    back = exchange(parts, [back_order(2 * chips)])
    kept, given, left, right = call(
        logits_kernel,
        [
            ((slots, width // 2), F32),
            ((slots, width // 2), F32),
            ((2 * slots, patches), BF16),
            ((2 * slots, width), BF16),
        ],
        [(slots, width)] * 2,
        (12 * patches * width * slots, 2 * image_bytes),
        tokens,
        out_grad,
        router_rows,
        dispatch,
        combine,
        back,
    )
    pair = (kept + swap_cores(given)).astype(BF16)
    same_core = [sum_order(2 * chips, core) for core in range(2)]
    terms = exchange(jnp.broadcast_to(pair[None], (chips,) + pair.shape), same_core)
    total = jnp.sum(terms.astype(F32), axis=0)
    other = swap_cores(total)
    first = lax.axis_index("expert") % 2 == 0
    router_grad = jnp.concatenate(
        [jnp.where(first, total, other), jnp.where(first, other, total)], axis=1
    )
    (tokens_grad,) = call(
        tokens_kernel,
        [((patches, width), BF16)],
        [],
        (4 * patches * width * slots, image_bytes),
        left,
        right,
    )
    return (tokens_grad[None], router_grad.T)


def solution(mesh):
    images = P(("group", "expert"), None, None)
    in_specs = (images, images, P(), P(None, "expert"), P("expert", None))
    out_specs = (images, P("group", None))
    return jax.shard_map(
        per_device, mesh=mesh, in_specs=in_specs, out_specs=out_specs, check_vma=False
    )
```

```python
import math

import jax
import jax.numpy as jnp
from jax import lax
from jax.experimental import pallas as pl
from jax.experimental.pallas import tpu as pltpu
from jax.sharding import PartitionSpec as P

F32 = jnp.float32
BF16 = jnp.bfloat16
NN = (((1,), (0,)), ((), ()))
NT = (((1,), (1,)), ((), ()))
TN = (((0,), (0,)), ((), ()))
AHEAD_FLOPS = 3 * 10**10


def out_order(size):
    chips = size // 2
    order = [k // 2 if k % 2 else chips - 1 - k // 2 for k in range(chips)]
    return [2 * chip + core for chip in order for core in (1, 0)]


def back_order(size):
    return [(size - 1 + 5 * k) % size for k in range(size)]


def sum_order(size, core):
    chips = size // 2
    order = [k // 2 if k % 2 else chips - 1 - k // 2 for k in range(chips)]
    return [2 * chip + core for chip in order]


def dot(a, b, dims):
    return lax.dot_general(a, b, dims, preferred_element_type=F32)


def first_kernel(token_ref):
    token_ref[...] = jnp.zeros(token_ref.shape, F32)


def slots_kernel(tokens_ref, router_ref, token_ref, dispatch_ref, combine_ref):
    logits = dot(router_ref[...], tokens_ref[...], NT)
    over_patches = jnp.exp(logits - jnp.max(logits, axis=1, keepdims=True))
    dispatch = over_patches / jnp.sum(over_patches, axis=1, keepdims=True)
    over_slots = jnp.exp(logits - jnp.max(logits, axis=0, keepdims=True))
    dispatch_ref[...] = dispatch
    combine_ref[...] = over_slots / jnp.sum(over_slots, axis=0, keepdims=True)


def messages_kernel(tokens_ref, grad_ref, dispatch_ref, combine_ref, sent_ref):
    slot_in = dot(dispatch_ref[...].astype(BF16), tokens_ref[...], NN)
    slot_grad = dot(combine_ref[...].astype(BF16), grad_ref[...], NN)
    slots = slot_in.shape[0]
    order = out_order(2 * slots)
    for s in range(slots):
        rows = [slot_in[s : s + 1], slot_grad[s : s + 1]]
        message = jnp.concatenate(rows, axis=0).astype(BF16)
        for half in range(2):
            sent_ref[order.index(2 * s + half)] = message


def experts_kernel(
    got_ref, in_weight_ref, out_weight_ref, parts_ref, in_rows_ref, grad_rows_ref
):
    images = got_ref.shape[0]
    out, back = out_order(images), back_order(images)
    for k in range(images):
        message = got_ref[k].astype(F32)
        in_rows_ref[k : k + 1] = message[0:1]
        grad_rows_ref[k : k + 1] = message[1:2]
    hidden = dot(in_rows_ref[...].astype(BF16), in_weight_ref[...], NN)
    normal_cdf = 0.5 * (1.0 + lax.erf(hidden * (1.0 / math.sqrt(2.0))))
    normal_pdf = jnp.exp(-0.5 * hidden * hidden) * (1.0 / math.sqrt(2.0 * math.pi))
    activation = (hidden * normal_cdf).astype(BF16)
    slope = normal_cdf + hidden * normal_pdf
    act_grad = dot(grad_rows_ref[...].astype(BF16), out_weight_ref[...], NT)
    hidden_grad = (act_grad * slope).astype(BF16)
    part_out = dot(activation, out_weight_ref[...], NN)
    part_in = dot(hidden_grad, in_weight_ref[...], NT)
    for k in range(images):
        rows = [part_out[k : k + 1], part_in[k : k + 1]]
        parts_ref[back.index(out[k])] = jnp.concatenate(rows, axis=0).astype(BF16)


def logits_kernel(
    tokens_ref,
    grad_ref,
    router_ref,
    dispatch_ref,
    combine_ref,
    back_ref,
    kept_ref,
    given_ref,
    left_ref,
    right_ref,
    out_rows_ref,
    back_rows_ref,
):
    slots = router_ref.shape[0]
    order = back_order(2 * slots)
    for s in range(slots):
        halves = [back_ref[order.index(2 * s + half)].astype(F32) for half in range(2)]
        message = halves[0] + halves[1]
        out_rows_ref[s : s + 1] = message[0:1]
        back_rows_ref[s : s + 1] = message[1:2]
    slot_back = back_rows_ref[...].astype(BF16)
    combine_grad = dot(out_rows_ref[...].astype(BF16), grad_ref[...], NT)
    dispatch_grad = dot(slot_back, tokens_ref[...], NT)
    dispatch = dispatch_ref[...]
    combine = combine_ref[...]
    slot_sum = jnp.sum(combine * combine_grad, axis=0, keepdims=True)
    patch_sum = jnp.sum(dispatch * dispatch_grad, axis=1, keepdims=True)
    logits_grad = combine * (combine_grad - slot_sum) + dispatch * (dispatch_grad - patch_sum)
    part = dot(logits_grad.astype(BF16), tokens_ref[...], NN)
    half = part.shape[1] // 2
    first = lax.axis_index("expert") % 2 == 0
    kept_ref[...] = jnp.where(first, part[:, :half], part[:, half:])
    given_ref[...] = jnp.where(first, part[:, half:], part[:, :half])
    left_ref[...] = jnp.concatenate([logits_grad, dispatch], axis=0).astype(BF16)
    right_ref[...] = jnp.concatenate(
        [router_ref[...].astype(F32), back_rows_ref[...]], axis=0
    ).astype(BF16)


def tokens_kernel(left_ref, right_ref, tokens_grad_ref):
    tokens_grad_ref[...] = dot(left_ref[...], right_ref[...], TN).astype(BF16)


def call(kernel, outs, scratch, cost, *operands):
    return pl.pallas_call(
        kernel,
        out_shape=[jax.ShapeDtypeStruct(shape, dtype) for shape, dtype in outs],
        in_specs=[pl.BlockSpec(memory_space=pltpu.VMEM)] * len(operands),
        out_specs=[pl.BlockSpec(memory_space=pltpu.VMEM)] * len(outs),
        scratch_shapes=[pltpu.VMEM(shape, F32) for shape in scratch],
        compiler_params=pltpu.CompilerParams(vmem_limit_bytes=16 * 2**20),
        cost_estimate=pl.CostEstimate(flops=cost[0], bytes_accessed=cost[1], transcendentals=0),
    )(*operands)


def swap_cores(value):
    size = lax.axis_size("expert")
    return lax.ppermute(value, "expert", [(i, i ^ 1) for i in range(size)])


def exchange(value, groups):
    return lax.all_to_all(
        value, "expert", split_axis=0, concat_axis=0, tiled=True, axis_index_groups=groups
    )


def per_device(tokens, out_grad, router, in_weight, out_weight):
    _, patches, width = tokens.shape
    hidden = in_weight.shape[1]
    slots = router.shape[1]
    chips = slots
    tokens = tokens[0]
    out_grad = out_grad[0]
    router_rows = router.T
    image_bytes = 2 * patches * width
    weight_bytes = 2 * width * hidden
    (token,) = call(first_kernel, [((8, 128), F32)], [], (AHEAD_FLOPS, image_bytes))
    dispatch, combine = call(
        slots_kernel,
        [((slots, patches), F32), ((slots, patches), F32)],
        [],
        (4 * patches * width * slots, image_bytes),
        tokens,
        router_rows,
        token,
    )
    (sent,) = call(
        messages_kernel,
        [((2 * slots, 2, width), BF16)],
        [],
        (8 * patches * width * slots, 2 * image_bytes),
        tokens,
        out_grad,
        dispatch,
        combine,
    )
    got = exchange(sent, [out_order(2 * chips)])
    (parts,) = call(
        experts_kernel,
        [((2 * chips, 2, width), BF16)],
        [(2 * chips, width)] * 2,
        (16 * chips * width * hidden, 2 * weight_bytes),
        got,
        in_weight,
        out_weight,
    )
    back = exchange(parts, [back_order(2 * chips)])
    kept, given, left, right = call(
        logits_kernel,
        [
            ((slots, width // 2), F32),
            ((slots, width // 2), F32),
            ((2 * slots, patches), BF16),
            ((2 * slots, width), BF16),
        ],
        [(slots, width)] * 2,
        (12 * patches * width * slots, 2 * image_bytes),
        tokens,
        out_grad,
        router_rows,
        dispatch,
        combine,
        back,
    )
    pair = (kept + swap_cores(given)).astype(BF16)
    same_core = [sum_order(2 * chips, core) for core in range(2)]
    terms = exchange(jnp.broadcast_to(pair[None], (chips,) + pair.shape), same_core)
    total = jnp.sum(terms.astype(F32), axis=0)
    other = swap_cores(total)
    first = lax.axis_index("expert") % 2 == 0
    router_grad = jnp.concatenate(
        [jnp.where(first, total, other), jnp.where(first, other, total)], axis=1
    )
    (tokens_grad,) = call(
        tokens_kernel,
        [((patches, width), BF16)],
        [],
        (4 * patches * width * slots, image_bytes),
        left,
        right,
    )
    return (tokens_grad[None], router_grad.T)


def solution(mesh):
    images = P(("group", "expert"), None, None)
    in_specs = (images, images, P(), P(None, "expert"), P("expert", None))
    out_specs = (images, P("group", None))
    return jax.shard_map(
        per_device, mesh=mesh, in_specs=in_specs, out_specs=out_specs, check_vma=False
    )
```

```python
import math

import jax
import jax.numpy as jnp
from jax import lax
from jax.experimental import pallas as pl
from jax.experimental.pallas import tpu as pltpu
from jax.sharding import PartitionSpec as P

F32 = jnp.float32
BF16 = jnp.bfloat16
NN = (((1,), (0,)), ((), ()))
NT = (((1,), (1,)), ((), ()))
TN = (((0,), (0,)), ((), ()))
AHEAD_FLOPS = 3 * 10**10


def out_order(size):
    return [size - 1] + list(range(1, size - 1)) + [0]


def back_order(size):
    return out_order(size)


def sum_order(size, core):
    chips = size // 2
    order = [k // 2 if k % 2 else chips - 1 - k // 2 for k in range(chips)]
    return [2 * chip + core for chip in order]


def dot(a, b, dims):
    return lax.dot_general(a, b, dims, preferred_element_type=F32)


def first_kernel(token_ref):
    token_ref[...] = jnp.zeros(token_ref.shape, F32)


def slots_kernel(tokens_ref, router_ref, token_ref, dispatch_ref, combine_ref):
    logits = dot(router_ref[...], tokens_ref[...], NT)
    over_patches = jnp.exp(logits - jnp.max(logits, axis=1, keepdims=True))
    dispatch = over_patches / jnp.sum(over_patches, axis=1, keepdims=True)
    over_slots = jnp.exp(logits - jnp.max(logits, axis=0, keepdims=True))
    dispatch_ref[...] = dispatch
    combine_ref[...] = over_slots / jnp.sum(over_slots, axis=0, keepdims=True)


def messages_kernel(tokens_ref, grad_ref, dispatch_ref, combine_ref, sent_ref):
    slot_in = dot(dispatch_ref[...].astype(BF16), tokens_ref[...], NN)
    slot_grad = dot(combine_ref[...].astype(BF16), grad_ref[...], NN)
    slots = slot_in.shape[0]
    order = out_order(2 * slots)
    for s in range(slots):
        rows = [slot_in[s : s + 1], slot_grad[s : s + 1]]
        message = jnp.concatenate(rows, axis=0).astype(BF16)
        for half in range(2):
            sent_ref[order.index(2 * s + half)] = message


def experts_kernel(
    got_ref, in_weight_ref, out_weight_ref, parts_ref, in_rows_ref, grad_rows_ref
):
    images = got_ref.shape[0]
    out, back = out_order(images), back_order(images)
    for k in range(images):
        message = got_ref[k].astype(F32)
        in_rows_ref[k : k + 1] = message[0:1]
        grad_rows_ref[k : k + 1] = message[1:2]
    hidden = dot(in_rows_ref[...].astype(BF16), in_weight_ref[...], NN)
    normal_cdf = 0.5 * (1.0 + lax.erf(hidden * (1.0 / math.sqrt(2.0))))
    normal_pdf = jnp.exp(-0.5 * hidden * hidden) * (1.0 / math.sqrt(2.0 * math.pi))
    activation = (hidden * normal_cdf).astype(BF16)
    slope = normal_cdf + hidden * normal_pdf
    act_grad = dot(grad_rows_ref[...].astype(BF16), out_weight_ref[...], NT)
    hidden_grad = (act_grad * slope).astype(BF16)
    part_out = dot(activation, out_weight_ref[...], NN)
    part_in = dot(hidden_grad, in_weight_ref[...], NT)
    for k in range(images):
        rows = [part_out[k : k + 1], part_in[k : k + 1]]
        parts_ref[back.index(out[k])] = jnp.concatenate(rows, axis=0).astype(BF16)


def logits_kernel(
    tokens_ref,
    grad_ref,
    router_ref,
    dispatch_ref,
    combine_ref,
    back_ref,
    kept_ref,
    given_ref,
    left_ref,
    right_ref,
    out_rows_ref,
    back_rows_ref,
):
    slots = router_ref.shape[0]
    order = back_order(2 * slots)
    for s in range(slots):
        halves = [back_ref[order.index(2 * s + half)].astype(F32) for half in range(2)]
        message = halves[0] + halves[1]
        out_rows_ref[s : s + 1] = message[0:1]
        back_rows_ref[s : s + 1] = message[1:2]
    slot_back = back_rows_ref[...].astype(BF16)
    combine_grad = dot(out_rows_ref[...].astype(BF16), grad_ref[...], NT)
    dispatch_grad = dot(slot_back, tokens_ref[...], NT)
    dispatch = dispatch_ref[...]
    combine = combine_ref[...]
    slot_sum = jnp.sum(combine * combine_grad, axis=0, keepdims=True)
    patch_sum = jnp.sum(dispatch * dispatch_grad, axis=1, keepdims=True)
    logits_grad = combine * (combine_grad - slot_sum) + dispatch * (dispatch_grad - patch_sum)
    part = dot(logits_grad.astype(BF16), tokens_ref[...], NN)
    half = part.shape[1] // 2
    first = lax.axis_index("expert") % 2 == 0
    kept_ref[...] = jnp.where(first, part[:, :half], part[:, half:])
    given_ref[...] = jnp.where(first, part[:, half:], part[:, :half])
    left_ref[...] = jnp.concatenate([logits_grad, dispatch], axis=0).astype(BF16)
    right_ref[...] = jnp.concatenate(
        [router_ref[...].astype(F32), back_rows_ref[...]], axis=0
    ).astype(BF16)


def tokens_kernel(left_ref, right_ref, tokens_grad_ref):
    tokens_grad_ref[...] = dot(left_ref[...], right_ref[...], TN).astype(BF16)


def call(kernel, outs, scratch, cost, *operands):
    return pl.pallas_call(
        kernel,
        out_shape=[jax.ShapeDtypeStruct(shape, dtype) for shape, dtype in outs],
        in_specs=[pl.BlockSpec(memory_space=pltpu.VMEM)] * len(operands),
        out_specs=[pl.BlockSpec(memory_space=pltpu.VMEM)] * len(outs),
        scratch_shapes=[pltpu.VMEM(shape, F32) for shape in scratch],
        compiler_params=pltpu.CompilerParams(vmem_limit_bytes=16 * 2**20),
        cost_estimate=pl.CostEstimate(flops=cost[0], bytes_accessed=cost[1], transcendentals=0),
    )(*operands)


def swap_cores(value):
    size = lax.axis_size("expert")
    return lax.ppermute(value, "expert", [(i, i ^ 1) for i in range(size)])


def exchange(value, groups):
    return lax.all_to_all(
        value, "expert", split_axis=0, concat_axis=0, tiled=True, axis_index_groups=groups
    )


def per_device(tokens, out_grad, router, in_weight, out_weight):
    _, patches, width = tokens.shape
    hidden = in_weight.shape[1]
    slots = router.shape[1]
    chips = slots
    tokens = tokens[0]
    out_grad = out_grad[0]
    router_rows = router.T
    image_bytes = 2 * patches * width
    weight_bytes = 2 * width * hidden
    (token,) = call(first_kernel, [((8, 128), F32)], [], (AHEAD_FLOPS, image_bytes))
    dispatch, combine = call(
        slots_kernel,
        [((slots, patches), F32), ((slots, patches), F32)],
        [],
        (4 * patches * width * slots, image_bytes),
        tokens,
        router_rows,
        token,
    )
    (sent,) = call(
        messages_kernel,
        [((2 * slots, 2, width), BF16)],
        [],
        (8 * patches * width * slots, 2 * image_bytes),
        tokens,
        out_grad,
        dispatch,
        combine,
    )
    got = exchange(sent, [out_order(2 * chips)])
    (parts,) = call(
        experts_kernel,
        [((2 * chips, 2, width), BF16)],
        [(2 * chips, width)] * 2,
        (16 * chips * width * hidden, 2 * weight_bytes),
        got,
        in_weight,
        out_weight,
    )
    back = exchange(parts, [back_order(2 * chips)])
    kept, given, left, right = call(
        logits_kernel,
        [
            ((slots, width // 2), F32),
            ((slots, width // 2), F32),
            ((2 * slots, patches), BF16),
            ((2 * slots, width), BF16),
        ],
        [(slots, width)] * 2,
        (12 * patches * width * slots, 2 * image_bytes),
        tokens,
        out_grad,
        router_rows,
        dispatch,
        combine,
        back,
    )
    pair = (kept + swap_cores(given)).astype(BF16)
    same_core = [sum_order(2 * chips, core) for core in range(2)]
    terms = exchange(jnp.broadcast_to(pair[None], (chips,) + pair.shape), same_core)
    total = jnp.sum(terms.astype(F32), axis=0)
    other = swap_cores(total)
    first = lax.axis_index("expert") % 2 == 0
    router_grad = jnp.concatenate(
        [jnp.where(first, total, other), jnp.where(first, other, total)], axis=1
    )
    (tokens_grad,) = call(
        tokens_kernel,
        [((patches, width), BF16)],
        [],
        (4 * patches * width * slots, image_bytes),
        left,
        right,
    )
    return (tokens_grad[None], router_grad.T)


def solution(mesh):
    images = P(("group", "expert"), None, None)
    in_specs = (images, images, P(), P(None, "expert"), P("expert", None))
    out_specs = (images, P("group", None))
    return jax.shard_map(
        per_device, mesh=mesh, in_specs=in_specs, out_specs=out_specs, check_vma=False
    )
```
